32 devices in a mesh: seq: 8 (over y, x, core), fsdp: 4 (over z).
Axes of the slice: x: 2, y: 2, z: 4, core: 2. Of those that a mesh axis runs over, the one named last changes fastest.
Arguments:
- tokens: bfloat16 [4, 2048, 1600], P('fsdp', 'seq'), may hold values from -6 to 6
- doc_ids: int32 [4, 2048], P('fsdp', 'seq'), may hold values from 0 to 1, never falling along the last dimension, each value on 1 to 1792 neighbouring positions
- in_weight: bfloat16 [1600, 8640], P('fsdp', 'seq'), may hold values from -0.15625 to 0.15625
- out_weight: bfloat16 [4800, 1600], P('fsdp', 'seq'), may hold values from -0.1875 to 0.1875
- gate_up: bfloat16 [1600, 11008], P('fsdp', 'seq'), may hold values from -0.15625 to 0.15625
- down_weight: bfloat16 [5504, 1600], P('fsdp', 'seq'), may hold values from -0.109375 to 0.109375
- select_weight: bfloat16 [132, 3200], P('fsdp', 'seq'), may hold values from -0.109375 to 0.109375
- step_weight: bfloat16 [100, 3200], P('fsdp', 'seq'), may hold values from -0.625 to 0.625
- first_gain: float32 [1600], replicated, may hold values from 0.25 to 1.75
- second_gain: float32 [1600], replicated, may hold values from 0.25 to 1.75
- attn_gain: float32 [1600], replicated, may hold values from 0.25 to 1.75
- mamba_gain: float32 [3200], replicated, may hold values from 0.25 to 1.75
- conv_weight: float32 [4, 3200], replicated, may hold values from -3 to 3
- conv_bias: float32 [3200], replicated, may hold values from -3 to 3
- step_bias: float32 [3200], replicated, may hold values from -7 to -2.5
- decay_log: float32 [16, 3200], replicated, may hold values from -3 to 2.5
- skip_gain: float32 [3200], replicated, may hold values from 0.5 to 1.5
- cotangent: bfloat16 [4, 2048, 1600], P('fsdp', 'seq'), may hold values from -6 to 6
Outputs:
- out_tokens: bfloat16 [4, 2048, 1600], P('fsdp', 'seq')
- tokens_grad: bfloat16 [4, 2048, 1600], P('fsdp', 'seq')
- in_grad: float32 [1600, 8640], P('fsdp', 'seq')
- out_grad: float32 [4800, 1600], P('fsdp', 'seq')
- gate_up_grad: float32 [1600, 11008], P('fsdp', 'seq')
- down_grad: float32 [5504, 1600], P('fsdp', 'seq')
- select_grad: float32 [132, 3200], P('fsdp', 'seq')
- step_weight_grad: float32 [100, 3200], P('fsdp', 'seq')
- first_gain_grad: float32 [1600], replicated
- second_gain_grad: float32 [1600], replicated
- attn_gain_grad: float32 [1600], replicated
- mamba_gain_grad: float32 [3200], replicated
- conv_weight_grad: float32 [4, 3200], replicated
- conv_bias_grad: float32 [3200], replicated
- step_bias_grad: float32 [3200], replicated
- decay_log_grad: float32 [16, 3200], replicated
- skip_gain_grad: float32 [3200], replicated
The draws below stay inside these ranges and needn't reach their ends.
Inputs may be any that keep to these rules, and one draw needn't show every extreme that they name: Along each group doc_ids never falls and starts at 0; each value labels one run of 1 to 2048 - 256 * (1) tokens.
All inputs are finite; a program needn't handle non-finite values.
Results may differ from the reference program's by a relative error of at most 0.02.
Values may be sent and summed in bfloat16 or wider, within the bound.
A program may use at most 448 MiB of HBM per device.

```python
import math
import jax
import jax.numpy as jnp
import numpy as np
from jax import lax

D = 1600
QUERY_HEADS = 25
KEY_VALUE_HEADS = 5
HEAD_SIZE = 64
DI = 3200
NS = 16
DTR = 100
KC = 4
F = 5504
WINDOW_TOKENS = 1024
DOCS = 2
TOK_DEV = 256
GROUP = 2048
SEQS = 4
P_SIZE = 8640
CAT = 4800
R = 132


def block_levels(key, shape, split, low, largest):
    loudness, own = 1.0, jax.random.fold_in(key, 6)
    for dim, blocks in split:
        steps = jnp.exp(jax.random.uniform(jax.random.fold_in(own, dim), (blocks,), jnp.float32, low / len(split), largest / len(split)))
        loudness = loudness * jnp.repeat(steps, shape[dim] // blocks).reshape([-1 if axis == dim else 1 for axis in range(len(shape))])
    return loudness


def length_profile(number_of, total, most, skew):
    portions = [(1 << 20) // math.isqrt(standing ** skew) + 1 for standing in range(2, number_of + 1)]
    spare, holding = total - most - (number_of - 1), [1] * (number_of - 1)
    while spare > 0:
        movable = [i for i in range(number_of - 1) if holding[i] < most]
        whole, budget = sum([portions[i] for i in movable]), spare
        for i in movable:
            extra = min(most - holding[i], max(1, budget * portions[i] // whole), spare)
            holding[i] = holding[i] + extra
            spare = spare - extra
    return np.array([most] + holding)


def ragged(stream_key, count, total, limit, skew):
    if count == 2:
        one = jax.random.randint(stream_key, (), max(1, total - limit), min(limit, total - 1) + 1)
        return jnp.stack([one, total - one])
    tallies = jnp.asarray(length_profile(count, total, limit, skew), jnp.int32)
    couples = (count - 1) // 2
    source_of, sink = tallies[1:1 + 2 * couples:2], tallies[2:2 + 2 * couples:2]
    slack = jnp.minimum(source_of - 1, limit - sink)
    moved = jax.random.randint(jax.random.fold_in(stream_key, 1), (couples,), 0, 1 << 20) % (slack + 1)
    tallies = tallies.at[1:1 + 2 * couples:2].set(source_of - moved).at[2:2 + 2 * couples:2].set(sink + moved)
    return tallies[jax.random.permutation(jax.random.fold_in(stream_key, 2), count)]


def bell_draw(own_key, dims, deviation, limit, split=(), kind=jnp.bfloat16):
    entries = jax.random.normal(own_key, dims, jnp.float32) * deviation
    if len(split) > 0:
        entries = block_levels(own_key, dims, split, -0.22, 0.18) * entries
    return jnp.clip(entries, min=-limit, max=limit).astype(kind)


def setup_inputs(seed: int = 0) -> dict:
    streams_of = jax.random.split(jax.random.key(seed), 19)
    return {
        "tokens": bell_draw(streams_of[0], (SEQS, GROUP, D), 1.0, 6.0, ((0, 4), (1, 8))),
        "doc_ids": jax.vmap(lambda own: jnp.searchsorted(jnp.cumsum(ragged(own, DOCS, GROUP, GROUP - TOK_DEV * (DOCS - 1), 0)), jnp.arange(GROUP), side="right"))(jax.random.split(streams_of[1], SEQS)).reshape((SEQS, GROUP)).astype(jnp.int32),
        "in_weight": bell_draw(streams_of[2], (D, P_SIZE), D ** -0.5, 0.15625, ((0, 4), (1, 8))),
        "out_weight": bell_draw(streams_of[3], (CAT, D), (CAT // 4) ** -0.5, 0.1875, ((0, 4), (1, 8))),
        "gate_up": bell_draw(streams_of[4], (D, 2 * F), D ** -0.5, 0.15625, ((0, 4), (1, 8))),
        "down_weight": bell_draw(streams_of[5], (F, D), (F // 2) ** -0.5, 0.109375, ((0, 4), (1, 8))),
        "select_weight": bell_draw(streams_of[6], (R, DI), DI ** -0.5, 0.109375, ((0, 4), (1, 8))),
        "step_weight": bell_draw(streams_of[7], (DTR, DI), DTR ** -0.5, 0.625, ((0, 4), (1, 8))),
        "first_gain": jnp.clip(1.0 + 0.15 * jax.random.normal(streams_of[8], (D,), jnp.float32), 0.25, 1.75),
        "second_gain": jnp.clip(1.0 + 0.15 * jax.random.normal(streams_of[9], (D,), jnp.float32), 0.25, 1.75),
        "attn_gain": jnp.clip(1.0 + 0.15 * jax.random.normal(streams_of[10], (QUERY_HEADS * HEAD_SIZE,), jnp.float32), 0.25, 1.75),
        "mamba_gain": jnp.clip(1.0 + 0.15 * jax.random.normal(streams_of[11], (DI,), jnp.float32), 0.25, 1.75),
        "conv_weight": bell_draw(streams_of[12], (KC, DI), 0.5, 3.0, (), jnp.float32),
        "conv_bias": bell_draw(streams_of[13], (DI,), 0.5, 3.0, (), jnp.float32),
        "step_bias": jnp.clip(jax.random.uniform(streams_of[14], (DI,), jnp.float32, -7.0, -2.5), -7.0, -2.5),
        "decay_log": jnp.clip(jax.random.uniform(streams_of[15], (NS, DI), jnp.float32, -3.0, 2.5), -3.0, 2.5),
        "skip_gain": jnp.clip(jax.random.uniform(streams_of[16], (DI,), jnp.float32, 0.5, 1.5), 0.5, 1.5),
        "cotangent": bell_draw(streams_of[17], (SEQS, GROUP, D), 1.0, 6.0, ((0, 4), (1, 8))),
    }


@jax.custom_vjp
def low(v):
    return lax.optimization_barrier(v.astype(jnp.bfloat16)).astype(jnp.float32)

@jax.custom_vjp
def low_back(v):
    return v

def low_keep(v):
    return (low(v), None)

def low_pass(kept, grad):
    return (grad,)

def back_keep(v):
    return (v, None)

def back_low(kept, grad):
    return (low(grad),)
low.defvjp(low_keep, low_pass)
low_back.defvjp(back_keep, back_low)
norm_eps = 1e-05
masked_score = -1e+30
highest = lax.Precision.HIGHEST

def product(left, right):
    return jnp.dot(left, right, precision=highest)

def rms_norm(value, gain):
    return value * lax.rsqrt(lax.optimization_barrier(jnp.mean(value * value, axis=-1, keepdims=True)) + norm_eps) * gain

def attend_group(query_rows, key_rows, value_rows, seq_ids):
    token_length = query_rows.shape[0]
    block_len = math.gcd(token_length, 512)
    query_groups = QUERY_HEADS // KEY_VALUE_HEADS
    heads_of_queries = query_rows.reshape(token_length, KEY_VALUE_HEADS, query_groups, HEAD_SIZE)
    padded_keys = jnp.concatenate([jnp.zeros((WINDOW_TOKENS, KEY_VALUE_HEADS, HEAD_SIZE), jnp.float32), key_rows.reshape(token_length, KEY_VALUE_HEADS, HEAD_SIZE)], 0)
    padded_values = jnp.concatenate([jnp.zeros((WINDOW_TOKENS, KEY_VALUE_HEADS, HEAD_SIZE), jnp.float32), value_rows.reshape(token_length, KEY_VALUE_HEADS, HEAD_SIZE)], 0)
    pad_ids = jnp.concatenate([jnp.full((WINDOW_TOKENS,), -1, jnp.int32), seq_ids], 0)

    def one_block(first_row):
        query_block = lax.dynamic_slice_in_dim(heads_of_queries, first_row, block_len, 0)
        key_block = lax.dynamic_slice_in_dim(padded_keys, first_row, block_len + WINDOW_TOKENS, 0)
        value_block = lax.dynamic_slice_in_dim(padded_values, first_row, block_len + WINDOW_TOKENS, 0)
        query_ids = lax.dynamic_slice_in_dim(seq_ids, first_row, block_len, 0)
        key_ids = lax.dynamic_slice_in_dim(pad_ids, first_row, block_len + WINDOW_TOKENS, 0)
        query_pos = first_row + jnp.arange(block_len, dtype=jnp.int32)
        key_pos = first_row - WINDOW_TOKENS + jnp.arange(block_len + WINDOW_TOKENS, dtype=jnp.int32)
        offset = query_pos[:, None] - key_pos[None, :]
        allowed = (offset >= 0) & (offset < WINDOW_TOKENS) & (query_ids[:, None] == key_ids[None, :])
        scores = low_back(jnp.einsum('qhgd,khd->hgqk', query_block, key_block, precision=highest) * HEAD_SIZE ** (-0.5))
        scores = jnp.where(allowed[None, None], scores, masked_score)
        weights = low(jax.nn.softmax(scores, axis=-1))
        attended = jnp.einsum('hgqk,khd->qhgd', weights, value_block, precision=highest)
        return attended.reshape(block_len, QUERY_HEADS * HEAD_SIZE)
    starts = jnp.arange(token_length // block_len, dtype=jnp.int32) * block_len
    return lax.map(jax.checkpoint(one_block), starts).reshape(token_length, QUERY_HEADS * HEAD_SIZE)

def mamba_group(inputs, gate_z, seq_ids, select_weight, step_weight, conv_weight, conv_bias, step_bias, decay_log, skip_gain):
    token_length = inputs.shape[0]
    pad_inputs = jnp.concatenate([jnp.zeros((KC - 1, DI), jnp.float32), inputs], 0)
    pad_ids = jnp.concatenate([jnp.full((KC - 1,), -1, jnp.int32), seq_ids], 0)
    conv_sum = jnp.zeros((token_length, DI), jnp.float32) + conv_bias
    for tap_index in range(KC):
        begin_row = KC - 1 - tap_index
        same_doc = (pad_ids[begin_row:begin_row + token_length] == seq_ids).astype(jnp.float32)
        conv_sum = conv_sum + conv_weight[tap_index] * pad_inputs[begin_row:begin_row + token_length] * same_doc[:, None]
    activated = low(jax.nn.silu(conv_sum))
    selected = low_back(product(activated, select_weight.T))
    step_raw = low(selected[:, :DTR])
    b_in = selected[:, DTR:DTR + NS]
    c_out = selected[:, DTR + NS:]
    step_size = jax.nn.softplus(low_back(product(step_raw, step_weight)) + step_bias)
    decay_rate = -jnp.exp(decay_log)
    previous = jnp.concatenate([seq_ids[:1], seq_ids[:-1]], 0)
    keep_state = (seq_ids == previous).astype(jnp.float32)
    block_len = math.gcd(token_length, 64)
    block_count = token_length // block_len

    def scan_block(carry_state, pieces):

        def one_token(carried, token_item):
            step_now, input_now, b_now, c_now, keep_now = token_item
            carried = jnp.exp(step_now[None, :] * decay_rate) * keep_now * carried + (step_now * input_now)[None, :] * b_now[:, None]
            return (carried, lax.optimization_barrier(jnp.sum(c_now[:, None] * carried, 0)))
        return lax.scan(one_token, carry_state, pieces)
    pieces = (step_size.reshape(block_count, block_len, DI), activated.reshape(block_count, block_len, DI), b_in.reshape(block_count, block_len, NS), c_out.reshape(block_count, block_len, NS), keep_state.reshape(block_count, block_len))
    _, emitted = lax.scan(jax.checkpoint(scan_block), jnp.zeros((NS, DI), jnp.float32), pieces)
    output = emitted.reshape(token_length, DI) + skip_gain * activated
    return output * jax.nn.silu(gate_z)

def layer_group(params, seq_x, seq_ids):
    in_weight, out_weight, gate_up, down_weight, select_weight, step_weight, first_gain, second_gain, attn_gain, mamba_gain, conv_weight, conv_bias, step_bias, decay_log, skip_gain = params
    query_w = QUERY_HEADS * HEAD_SIZE
    key_weight = KEY_VALUE_HEADS * HEAD_SIZE
    normed = low(rms_norm(seq_x, first_gain))
    projected = low_back(low(product(normed, in_weight)))
    query_rows = projected[:, :query_w]
    key_rows = projected[:, query_w:query_w + key_weight]
    value_rows = projected[:, query_w + key_weight:query_w + 2 * key_weight]
    inputs = projected[:, query_w + 2 * key_weight:query_w + 2 * key_weight + DI]
    gate_z = projected[:, query_w + 2 * key_weight + DI:]
    attended = low_back(attend_group(query_rows, key_rows, value_rows, seq_ids))
    mamba_out = mamba_group(inputs, gate_z, seq_ids, select_weight, step_weight, conv_weight, conv_bias, step_bias, decay_log, skip_gain)
    joined = low(jnp.concatenate([rms_norm(attended, attn_gain), rms_norm(mamba_out, mamba_gain)], 1))
    mixed = low_back(0.5 * product(joined, out_weight))
    hidden = seq_x + mixed
    second_normed = low(rms_norm(hidden, second_gain))
    gate_up_out = low_back(low(product(second_normed, gate_up)))
    inner = low(jax.nn.silu(gate_up_out[:, :F]) * gate_up_out[:, F:])
    return hidden + low_back(product(inner, down_weight))

def reference(tokens, doc_ids, in_weight, out_weight, gate_up, down_weight, select_weight, step_weight, first_gain, second_gain, attn_gain, mamba_gain, conv_weight, conv_bias, step_bias, decay_log, skip_gain, cotangent):
    params = (in_weight.astype(jnp.float32), out_weight.astype(jnp.float32), gate_up.astype(jnp.float32), down_weight.astype(jnp.float32), select_weight.astype(jnp.float32), step_weight.astype(jnp.float32), first_gain.astype(jnp.float32), second_gain.astype(jnp.float32), attn_gain.astype(jnp.float32), mamba_gain.astype(jnp.float32), conv_weight.astype(jnp.float32), conv_bias.astype(jnp.float32), step_bias.astype(jnp.float32), decay_log.astype(jnp.float32), skip_gain.astype(jnp.float32))

    def whole(weights, inputs):

        def one_group(group_item):
            return layer_group(weights, group_item[0], group_item[1])
        return lax.map(one_group, (inputs, doc_ids))
    result, pullback = jax.vjp(whole, params, tokens.astype(jnp.float32))
    weight_grads, token_grads = pullback(cotangent.astype(jnp.float32))
    return (result.astype(jnp.bfloat16), token_grads.astype(jnp.bfloat16), weight_grads[0], weight_grads[1], weight_grads[2], weight_grads[3], weight_grads[4], weight_grads[5], weight_grads[6], weight_grads[7], weight_grads[8], weight_grads[9], weight_grads[10], weight_grads[11], weight_grads[12], weight_grads[13], weight_grads[14])
```

```python
import functools

import jax
import jax.numpy as jnp
from jax import lax
from jax.experimental import pallas as pl
from jax.experimental.pallas import tpu as pltpu
from jax.sharding import PartitionSpec as P

QUERY_HEADS = 25
KEY_VALUE_HEADS = 5
HEAD_SIZE = 64
DI = 3200
NS = 16
DTR = 100
KC = 4
F = 5504
WINDOW_TOKENS = 1024

norm_eps = 1e-05
masked_score = -1e30
log2e = 1.4426950408889634
bf16 = jnp.bfloat16
f32 = jnp.float32


def matmul(left, right):
    return jnp.dot(left, right, preferred_element_type=f32)


def dot_tn(left, right):
    return lax.dot_general(left, right, (((0,), (0,)), ((), ())), preferred_element_type=f32)


def dot_nt(left, right):
    return lax.dot_general(left, right, (((1,), (1,)), ((), ())), preferred_element_type=f32)


def rms_norm(value, gain):
    scale = lax.rsqrt(jnp.mean(value * value, axis=-1, keepdims=True) + norm_eps)
    return (value * scale * gain, scale)


def norm_back(value, scale, gain, upstream):
    weighted = upstream * gain
    gain_grad = jnp.sum(upstream * value * scale, 0)
    inner_mean = jnp.mean(weighted * value, axis=-1, keepdims=True)
    return (scale * weighted - value * (scale * scale * scale) * inner_mean, gain_grad)


def park(part, j, value):
    for k, lane in enumerate(range(0, value.shape[1], 128)):
        end = min(lane + 128, value.shape[1])
        part[64 * k + 8 * j : 64 * k + 8 * j + 8, : end - lane] = value[:, lane:end]


def fold(part, out, t0):
    for k, lane in enumerate(range(0, out.shape[1], 128)):
        end = min(lane + 128, out.shape[1])
        total = part[pl.ds(64 * k, 8, stride=8), :]
        for s in range(1, 8):
            total = total + part[pl.ds(64 * k + s, 8, stride=8), :]
        out[pl.ds(t0, 8), lane:end] = total[:, : end - lane]


def scan_fwd_body(step_ref, push_ref, b_ref, c_ref, rate_ref, y_ref, st_ref, h_scr, part_scr):
    block = step_ref.shape[0]

    @pl.when(pl.program_id(0) == 0)
    def _():
        h_scr[...] = jnp.zeros_like(h_scr)

    rate = rate_ref[...]

    def group(index, state):
        t0 = pl.multiple_of(index * 8, 8)
        step8 = step_ref[pl.ds(t0, 8), :]
        push8 = push_ref[pl.ds(t0, 8), :]
        b_roll = pltpu.roll(b_ref[...], block - t0, 1)
        c_roll = pltpu.roll(c_ref[...], block - t0, 1)
        for j in range(8):
            decay = jnp.exp2(step8[j : j + 1, :] * rate)
            state = decay * state + push8[j : j + 1, :] * b_roll[:, j : j + 1]
            st_ref[t0 + j] = state
            out = c_roll[:, j : j + 1] * state
            park(part_scr, j, out[:8] + out[8:])
        fold(part_scr, y_ref, t0)
        return state

    h_scr[...] = lax.fori_loop(0, block // 8, group, h_scr[...])


def scan_bwd_body(
    step_ref, push_ref, dpre_ref, b_ref, c_ref, st_ref, prev_ref, rate_ref,
    pr_ref, pushed_ref, db_ref, dc_ref, log_ref, g_scr, log_scr, part1, part2,
):
    block = step_ref.shape[0]
    count = pl.num_programs(0)
    which = pl.program_id(0)

    @pl.when(which == 0)
    def _():
        g_scr[...] = jnp.zeros_like(g_scr)
        log_scr[...] = jnp.zeros_like(log_scr)

    lane_ids = lax.broadcasted_iota(jnp.int32, (NS, block), 1)
    before = prev_ref[0] * jnp.where(which == count - 1, 0.0, 1.0)

    def group(turn, carried):
        grad_in, state, db_acc, dc_acc = carried
        t0 = pl.multiple_of((block // 8 - 1 - turn) * 8, 8)
        step8 = step_ref[pl.ds(t0, 8), :]
        push8 = push_ref[pl.ds(t0, 8), :]
        dpre8 = dpre_ref[pl.ds(t0, 8), :]
        b_roll = pltpu.roll(b_ref[...], block - t0, 1)
        c_roll = pltpu.roll(c_ref[...], block - t0, 1)
        rate = rate_ref[...]
        log_acc = log_scr[...]
        for j in range(7, -1, -1):
            if j > 0:
                prior = st_ref[t0 + (j - 1)]
            else:
                prior = jnp.where(t0 > 0, st_ref[jnp.maximum(t0 - 1, 0)], before)
            step_row = step8[j : j + 1, :]
            dpre_row = dpre8[j : j + 1, :]
            grad = c_roll[:, j : j + 1] * dpre_row + grad_in
            grad_in = grad * jnp.exp2(step_row * (rate * log2e))
            flow = grad_in * prior
            by_rate = flow * rate
            park(part1, j, by_rate[:8] + by_rate[8:])
            by_b = grad * b_roll[:, j : j + 1]
            park(part2, j, by_b[:8] + by_b[8:])
            log_acc = log_acc + flow * step_row
            db = jnp.sum(grad * push8[j : j + 1, :], axis=1, keepdims=True)
            dc = jnp.sum(state * dpre_row, axis=1, keepdims=True)
            here = lane_ids == t0 + j
            db_acc = jnp.where(here, db, db_acc)
            dc_acc = jnp.where(here, dc, dc_acc)
            state = prior
        log_scr[...] = log_acc
        fold(part1, pr_ref, t0)
        fold(part2, pushed_ref, t0)
        return (grad_in, state, db_acc, dc_acc)

    zero = jnp.zeros((NS, block), f32)
    grad_in, _, db_acc, dc_acc = lax.fori_loop(
        0, block // 8, group, (g_scr[...], st_ref[block - 1], zero, zero)
    )
    g_scr[...] = grad_in
    db_ref[...] = db_acc
    dc_ref[...] = dc_acc

    @pl.when(which == count - 1)
    def _():
        log_ref[...] = log_scr[...] * rate_ref[...]


SCAN_BLOCK = 128


def scan_forward(step_keep, push, b_t, c_t, rate):
    tokens, width = step_keep.shape
    block = SCAN_BLOCK
    padded = (width + 127) // 128 * 128
    rows = pl.BlockSpec((block, width), lambda i: (i, 0))
    cols = pl.BlockSpec((NS, block), lambda i: (0, i))
    fixed = pl.BlockSpec((NS, width), lambda i: (0, 0))
    return pl.pallas_call(
        scan_fwd_body,
        grid=(tokens // block,),
        in_specs=[rows, rows, cols, cols, fixed],
        out_specs=[rows, pl.BlockSpec((block, NS, width), lambda i: (i, 0, 0))],
        out_shape=[
            jax.ShapeDtypeStruct((tokens, width), f32),
            jax.ShapeDtypeStruct((tokens, NS, width), f32),
        ],
        scratch_shapes=[pltpu.VMEM((NS, width), f32), pltpu.VMEM((padded // 2, 128), f32)],
        compiler_params=pltpu.CompilerParams(vmem_limit_bytes=40 << 20),
        cost_estimate=pl.CostEstimate(
            flops=tokens * width * NS * 8, bytes_accessed=tokens * width * NS * 4, transcendentals=tokens * width * NS
        ),
        name="scan_forward",
    )(step_keep, push, b_t, c_t, rate * log2e)


def scan_backward(step_keep, push, d_pre, b_t, c_t, states, rate):
    tokens, width = step_keep.shape
    block = SCAN_BLOCK
    padded = (width + 127) // 128 * 128
    last = tokens // block - 1
    rows = pl.BlockSpec((block, width), lambda i: (last - i, 0))
    cols = pl.BlockSpec((NS, block), lambda i: (0, last - i))
    fixed = pl.BlockSpec((NS, width), lambda i: (0, 0))
    return pl.pallas_call(
        scan_bwd_body,
        grid=(tokens // block,),
        in_specs=[
            rows, rows, rows, cols, cols,
            pl.BlockSpec((block, NS, width), lambda i: (last - i, 0, 0)),
            pl.BlockSpec((1, NS, width), lambda i: (jnp.maximum((last - i) * block - 1, 0), 0, 0)),
            fixed,
        ],
        out_specs=[rows, rows, cols, cols, fixed],
        out_shape=[
            jax.ShapeDtypeStruct((tokens, width), f32),
            jax.ShapeDtypeStruct((tokens, width), f32),
            jax.ShapeDtypeStruct((NS, tokens), f32),
            jax.ShapeDtypeStruct((NS, tokens), f32),
            jax.ShapeDtypeStruct((NS, width), f32),
        ],
        scratch_shapes=[
            pltpu.VMEM((NS, width), f32),
            pltpu.VMEM((NS, width), f32),
            pltpu.VMEM((padded // 2, 128), f32),
            pltpu.VMEM((padded // 2, 128), f32),
        ],
        compiler_params=pltpu.CompilerParams(vmem_limit_bytes=40 << 20),
        cost_estimate=pl.CostEstimate(
            flops=tokens * width * NS * 18, bytes_accessed=tokens * width * NS * 4, transcendentals=tokens * width * NS
        ),
        name="scan_backward",
    )(step_keep, push, d_pre, b_t, c_t, states, states, rate)


def attn_fwd_body(qt_ref, k_ref, vt_ref, bias_ref, out_ref, lse_ref):
    queries = bias_ref.shape[1]
    for head in range(qt_ref.shape[2] // queries):
        cols = slice(head * queries, (head + 1) * queries)
        scores = matmul(k_ref[0], qt_ref[0][:, cols]) + bias_ref[...]
        row_max = jnp.max(scores, 0, keepdims=True)
        exp_scores = jnp.exp(scores - row_max)
        row_total = jnp.sum(exp_scores, 0, keepdims=True)
        probs = (exp_scores * (1.0 / row_total)).astype(bf16)
        out_ref[0, :, cols] = matmul(vt_ref[0], probs)
        lse_ref[0, :, cols] = row_max + jnp.log(row_total)


def attn_bwd_body(
    q_ref, qt_ref, k_ref, kt_ref, v_ref, do_ref, dot_ref, lse_ref, bias_ref, dqt_ref, dk_ref, dv_ref
):
    queries = bias_ref.shape[1]
    dk = jnp.zeros(dk_ref.shape[1:], f32)
    dv = jnp.zeros(dv_ref.shape[1:], f32)
    for head in range(qt_ref.shape[2] // queries):
        cols = slice(head * queries, (head + 1) * queries)
        scores = matmul(k_ref[0], qt_ref[0][:, cols]) + bias_ref[...]
        probs = jnp.exp(scores - lse_ref[0][:, cols])
        d_probs = matmul(v_ref[0], dot_ref[0][:, cols])
        inner = jnp.sum(probs * d_probs, 0, keepdims=True)
        d_scores = (probs * (d_probs - inner)).astype(bf16)
        dqt_ref[0, :, cols] = matmul(kt_ref[0], d_scores) * (HEAD_SIZE**-0.5)
        dk = dk + matmul(d_scores, q_ref[0][cols])
        dv = dv + matmul(probs.astype(bf16), do_ref[0][cols])
    dk_ref[0] = dk
    dv_ref[0] = dv


def per_head(*dims):
    return pl.BlockSpec((1,) + dims, lambda h: (h, 0, 0))


def attention_forward(q_t, k, v_t, bias):
    heads, size, span = q_t.shape
    keys = k.shape[1]
    return pl.pallas_call(
        attn_fwd_body,
        grid=(heads,),
        in_specs=[per_head(size, span), per_head(keys, size), per_head(size, keys),
                  pl.BlockSpec(bias.shape, lambda h: (0, 0))],
        out_specs=[per_head(size, span), per_head(1, span)],
        out_shape=[
            jax.ShapeDtypeStruct((heads, size, span), f32),
            jax.ShapeDtypeStruct((heads, 1, span), f32),
        ],
        compiler_params=pltpu.CompilerParams(vmem_limit_bytes=40 << 20),
        cost_estimate=pl.CostEstimate(
            flops=heads * keys * span * 4 * 128, bytes_accessed=8 << 20, transcendentals=heads * keys * span
        ),
        name="attention_forward",
    )(q_t, k, v_t, bias)


def attention_backward(q, q_t, k, k_t, v, d_out, d_out_t, lse, bias):
    heads, size, span = q_t.shape
    keys = k.shape[1]
    return pl.pallas_call(
        attn_bwd_body,
        grid=(heads,),
        in_specs=[per_head(span, size), per_head(size, span), per_head(keys, size), per_head(size, keys),
                  per_head(keys, size), per_head(span, size), per_head(size, span), per_head(1, span),
                  pl.BlockSpec(bias.shape, lambda h: (0, 0))],
        out_specs=[per_head(size, span), per_head(keys, size), per_head(keys, size)],
        out_shape=[
            jax.ShapeDtypeStruct((heads, size, span), f32),
            jax.ShapeDtypeStruct((heads, keys, size), f32),
            jax.ShapeDtypeStruct((heads, keys, size), f32),
        ],
        compiler_params=pltpu.CompilerParams(vmem_limit_bytes=40 << 20),
        cost_estimate=pl.CostEstimate(
            flops=heads * keys * span * 10 * 128, bytes_accessed=16 << 20, transcendentals=heads * keys * span
        ),
        name="attention_backward",
    )(q, q_t, k, k_t, v, d_out, d_out_t, lse, bias)


def layer(
    n,
    m,
    tokens,
    doc_ids,
    in_weight,
    out_weight,
    gate_up,
    down_weight,
    select_weight,
    step_weight,
    first_gain,
    second_gain,
    attn_gain,
    mamba_gain,
    conv_weight,
    conv_bias,
    step_bias,
    decay_log,
    skip_gain,
    cotangent,
):
    me = lax.axis_index("seq")
    query_w = QUERY_HEADS * HEAD_SIZE
    key_w = KEY_VALUE_HEADS * HEAD_SIZE
    groups = QUERY_HEADS // KEY_VALUE_HEADS
    q_own, k_own, c_own, f_own = query_w // n, key_w // n, DI // n, F // n
    local = tokens.shape[1]
    length = local * n
    starts = (0, query_w, query_w + key_w, query_w + 2 * key_w, query_w + 2 * key_w + DI)
    widths = (q_own, k_own, k_own, c_own, c_own)

    def own_cols(value):
        return lax.dynamic_slice_in_dim(value, me * c_own, c_own, value.ndim - 1)

    in_cols = lax.all_gather(in_weight, "seq", axis=1, tiled=True)
    in_cols = jnp.concatenate(
        [lax.dynamic_slice_in_dim(in_cols, s + me * w, w, 1) for s, w in zip(starts, widths)], 1
    )
    in_full = lax.all_gather(in_cols, "fsdp", axis=0, tiled=True)
    select_own = lax.all_gather(select_weight, "fsdp", axis=0, tiled=True)
    step_own = lax.all_gather(step_weight, "fsdp", axis=0, tiled=True)

    half = n // 2
    route_a = [(d, 2 * d if d < half else 2 * (d - half) + 1) for d in range(n)]
    route_b = [(d, 2 * d + 1 if d < half else 2 * (d - half)) for d in range(n)]
    low_half = me < half
    even = me % 2 == 0
    piece0, piece1 = gate_up[:, :f_own], gate_up[:, f_own:]
    got_a = lax.ppermute(jnp.where(low_half, piece0, piece1), "seq", route_a)
    got_b = lax.ppermute(jnp.where(low_half, piece1, piece0), "seq", route_b)
    gu_cols = jnp.concatenate([jnp.where(even, got_a, got_b), jnp.where(even, got_b, got_a)], 1)
    gu_full = lax.all_gather(gu_cols, "fsdp", axis=0, tiled=True)

    out_rows = lax.all_gather(out_weight, "fsdp", axis=0, tiled=True)
    out_rows = jnp.concatenate(
        [out_rows[:query_w].reshape(n, q_own, -1), out_rows[query_w:].reshape(n, c_own, -1)], 1
    )
    out_full = lax.all_to_all(out_rows, "seq", 0, 0, tiled=False)
    out_full = out_full.transpose(1, 0, 2).reshape(q_own + c_own, -1)
    down_rows = lax.all_gather(down_weight, "fsdp", axis=0, tiled=True).reshape(n, f_own, -1)
    down_full = lax.all_to_all(down_rows, "seq", 0, 0, tiled=False)
    down_full = down_full.transpose(1, 0, 2).reshape(f_own, -1)

    seq_x = tokens[0].astype(f32)
    ids = lax.all_gather(doc_ids[0], "seq", axis=0, tiled=True)
    normed_one, scale_one = rms_norm(seq_x, first_gain)
    normed_one = lax.all_gather(normed_one.astype(bf16), "seq", axis=0, tiled=True)
    projected = matmul(normed_one, in_full).astype(bf16)
    edges = [0]
    for w in widths:
        edges.append(edges[-1] + w)
    queries_c = projected[:, : edges[1]]
    kv_c = projected[:, edges[1] : edges[3]]
    inputs = projected[:, edges[3] : edges[4]].astype(f32)
    gate_z = projected[:, edges[4] :].astype(f32)

    queries = lax.all_to_all(queries_c, "seq", 0, 1, tiled=True) * bf16(HEAD_SIZE**-0.5)
    kv_all = lax.all_gather(kv_c, "seq", axis=0, tiled=False)
    reach = (WINDOW_TOKENS + local - 2) // local
    span = min((reach + 1) * local, length)
    first_key = jnp.clip((me - reach) * local, 0, length - span)
    kv_win = lax.dynamic_slice_in_dim(kv_all, first_key, span, 1)
    keys = kv_win[:, :, :k_own].transpose(1, 0, 2).reshape(span, KEY_VALUE_HEADS, HEAD_SIZE)
    values = kv_win[:, :, k_own:].transpose(1, 0, 2).reshape(span, KEY_VALUE_HEADS, HEAD_SIZE)
    query_pos = me * local + jnp.arange(local, dtype=jnp.int32)
    key_pos = first_key + jnp.arange(span, dtype=jnp.int32)
    offset = query_pos[None, :] - key_pos[:, None]
    key_ids = lax.dynamic_slice_in_dim(ids, first_key, span, 0)
    allowed = (offset >= 0) & (offset < WINDOW_TOKENS) & (doc_ids[0][None, :] == key_ids[:, None])
    bias = jnp.where(allowed, 0.0, masked_score).astype(f32)
    q_heads = queries.reshape(local, KEY_VALUE_HEADS, groups, HEAD_SIZE)
    q_t = q_heads.transpose(1, 3, 2, 0).reshape(KEY_VALUE_HEADS, HEAD_SIZE, groups * local)
    q_rows = q_heads.transpose(1, 2, 0, 3).reshape(KEY_VALUE_HEADS, groups * local, HEAD_SIZE)
    k_rows, k_t = keys.transpose(1, 0, 2), keys.transpose(1, 2, 0)
    v_rows, v_t = values.transpose(1, 0, 2), values.transpose(1, 2, 0)
    attended_t, lse = attention_forward(q_t, k_rows, v_t, bias)

    def heads_to_rows(value):
        value = value.reshape(KEY_VALUE_HEADS, HEAD_SIZE, groups, local)
        return value.transpose(3, 0, 2, 1).reshape(local, query_w)

    attended = heads_to_rows(attended_t)
    attn_normed, attn_scale = rms_norm(attended, attn_gain)
    attn_c = lax.all_to_all(attn_normed.astype(bf16), "seq", 1, 0, tiled=True)

    conv_w, conv_b, step_b, decay_l, skip_g, mamba_g = (
        own_cols(v) for v in (conv_weight, conv_bias, step_bias, decay_log, skip_gain, mamba_gain)
    )
    padded_inputs = jnp.pad(inputs, ((KC - 1, 0), (0, 0)))
    padded_ids = jnp.pad(ids, (KC - 1, 0), constant_values=-1)
    conv_sum = conv_b + jnp.zeros_like(inputs)
    same_masks = []
    for tap in range(KC):
        begin = KC - 1 - tap
        same = (padded_ids[begin : begin + length] == ids).astype(f32)[:, None]
        same_masks.append(same)
        conv_sum = conv_sum + conv_w[tap] * padded_inputs[begin : begin + length] * same
    activated_b = jax.nn.silu(conv_sum).astype(bf16)
    activated = activated_b.astype(f32)
    selected = lax.psum(dot_nt(activated_b, select_own), "seq")
    step_raw = selected[:, :DTR].astype(bf16)
    b_t = selected[:, DTR : DTR + NS].T
    c_t = selected[:, DTR + NS :].T
    step_pre = matmul(step_raw, step_own) + step_b
    step_size = jax.nn.softplus(step_pre)
    rate = -jnp.exp(decay_l)
    changed = jnp.concatenate([jnp.zeros((1,), f32), (ids[1:] != ids[:-1]).astype(f32)])
    step_keep = step_size + 1e30 * changed[:, None]
    push = step_size * activated
    scan_out, states = scan_forward(step_keep, push, b_t, c_t, rate)
    mamba_pre = scan_out + skip_g * activated
    gate_sig = jax.nn.sigmoid(gate_z)
    mamba_out = mamba_pre * gate_z * gate_sig
    square_sum = lax.psum(jnp.sum(mamba_out * mamba_out, -1), "seq")
    mamba_scale = lax.rsqrt(square_sum / DI + norm_eps)[:, None]
    mamba_normed = mamba_out * mamba_scale * mamba_g
    joined = jnp.concatenate([attn_c, mamba_normed.astype(bf16)], 1)
    mixed = lax.psum_scatter(matmul(joined, out_full).astype(bf16), "seq", scatter_dimension=0, tiled=True)
    hidden = seq_x + 0.5 * mixed.astype(f32)
    normed_two, scale_two = rms_norm(hidden, second_gain)
    normed_two = lax.all_gather(normed_two.astype(bf16), "seq", axis=0, tiled=True)
    gate_up_out = matmul(normed_two, gu_full).astype(bf16)
    gate_part = gate_up_out[:, :f_own].astype(f32)
    up_part = gate_up_out[:, f_own:].astype(f32)
    gate_act = jax.nn.sigmoid(gate_part)
    inner = (gate_part * gate_act * up_part).astype(bf16)
    ffn = lax.psum_scatter(matmul(inner, down_full).astype(bf16), "seq", scatter_dimension=0, tiled=True)
    out_tokens = (hidden + ffn.astype(f32)).astype(bf16)

    d_ffn = lax.all_gather(cotangent[0], "seq", axis=0, tiled=True)
    down_term = dot_tn(inner, d_ffn).astype(bf16)
    d_inner = dot_nt(d_ffn, down_full)
    d_gate_up = jnp.concatenate(
        [
            d_inner * up_part * gate_act * (1.0 + gate_part * (1.0 - gate_act)),
            d_inner * gate_part * gate_act,
        ],
        1,
    ).astype(bf16)
    gate_up_term = dot_tn(normed_two, d_gate_up).astype(bf16)
    d_normed_two = lax.psum_scatter(
        dot_nt(d_gate_up, gu_full).astype(bf16), "seq", scatter_dimension=0, tiled=True
    ).astype(f32)
    d_hidden_part, second_grad = norm_back(hidden, scale_two, second_gain, d_normed_two)
    d_hidden = cotangent[0].astype(f32) + d_hidden_part
    d_mixed = lax.all_gather(d_hidden.astype(bf16), "seq", axis=0, tiled=True)
    out_term = (0.5 * dot_tn(joined, d_mixed)).astype(bf16)
    d_joined = 0.5 * dot_nt(d_mixed, out_full)

    d_attn = lax.all_to_all(d_joined[:, :q_own].astype(bf16), "seq", 0, 1, tiled=True).astype(f32)
    d_attended, attn_grad = norm_back(attended, attn_scale, attn_gain, d_attn)
    do_heads = d_attended.astype(bf16).reshape(local, KEY_VALUE_HEADS, groups, HEAD_SIZE)
    do_t = do_heads.transpose(1, 3, 2, 0).reshape(KEY_VALUE_HEADS, HEAD_SIZE, groups * local)
    do_rows = do_heads.transpose(1, 2, 0, 3).reshape(KEY_VALUE_HEADS, groups * local, HEAD_SIZE)
    dq_t, dk, dv = attention_backward(q_rows, q_t, k_rows, k_t, v_rows, do_rows, do_t, lse, bias)
    d_queries = lax.all_to_all(heads_to_rows(dq_t).astype(bf16), "seq", 1, 0, tiled=True)
    dk = dk.transpose(1, 0, 2).reshape(span, n, k_own)
    dv = dv.transpose(1, 0, 2).reshape(span, n, k_own)
    dkv = jnp.concatenate([dk, dv], 2).transpose(1, 0, 2).astype(bf16)
    dkv = lax.dynamic_update_slice_in_dim(jnp.zeros((n, length, 2 * k_own), bf16), dkv, first_key, 1)
    dkv = lax.psum_scatter(dkv, "seq", scatter_dimension=0, tiled=True)[0]

    u = d_joined[:, q_own:]
    weighted = u * mamba_g
    inner_mean = lax.psum(jnp.sum(weighted * mamba_out, -1), "seq")[:, None] / DI
    mamba_grad = jnp.sum(u * mamba_out * mamba_scale, 0)
    d_mamba = mamba_scale * weighted - mamba_out * (mamba_scale * mamba_scale * mamba_scale) * inner_mean
    d_pre = d_mamba * gate_z * gate_sig
    d_gate = d_mamba * mamba_pre * gate_sig * (1.0 + gate_z * (1.0 - gate_sig))
    skip_grad = jnp.sum(d_pre * activated, 0)
    by_rate, pushed, db_t, dc_t, decay_log_grad = scan_backward(
        step_keep, push, d_pre, b_t, c_t, states, rate
    )
    step_grads = by_rate + pushed * activated
    d_step_pre = step_grads * jax.nn.sigmoid(step_pre)
    step_bias_grad = jnp.sum(d_step_pre, 0)
    d_step_low = d_step_pre.astype(bf16)
    step_term = dot_tn(step_raw, d_step_low)
    d_selected = jnp.concatenate([dot_nt(d_step_low, step_own), db_t.T, dc_t.T], 1)
    d_selected = lax.psum(d_selected, "seq").astype(bf16)
    select_term = dot_tn(d_selected, activated_b)
    d_activated = d_pre * skip_g + pushed * step_size + matmul(d_selected, select_own)
    conv_sig = jax.nn.sigmoid(conv_sum)
    d_conv = d_activated * conv_sig * (1.0 + conv_sum * (1.0 - conv_sig))
    conv_bias_grad = jnp.sum(d_conv, 0)
    ext_grad = jnp.zeros((length + KC - 1, c_own), f32)
    conv_rows = []
    for tap in range(KC):
        begin = KC - 1 - tap
        masked_grad = d_conv * same_masks[tap]
        conv_rows.append(jnp.sum(masked_grad * padded_inputs[begin : begin + length], 0))
        ext_grad = ext_grad + jnp.pad(conv_w[tap] * masked_grad, ((begin, tap), (0, 0)))
    d_inputs = ext_grad[KC - 1 :]
    d_projected = jnp.concatenate([d_queries, dkv, d_inputs.astype(bf16), d_gate.astype(bf16)], 1)
    in_term = dot_tn(normed_one, d_projected).astype(bf16)
    d_normed_one = lax.psum_scatter(
        dot_nt(d_projected, in_full).astype(bf16), "seq", scatter_dimension=0, tiled=True
    ).astype(f32)
    d_x_part, first_grad = norm_back(seq_x, scale_one, first_gain, d_normed_one)
    tokens_grad = (d_hidden + d_x_part).astype(bf16)

    down_sum = lax.all_to_all(
        down_term.reshape(f_own, n, -1).transpose(1, 0, 2), "seq", 0, 0, tiled=False
    ).reshape(F, -1)
    down_sum = lax.psum_scatter(down_sum, "fsdp", scatter_dimension=0, tiled=True).astype(f32)
    out_sum = lax.all_to_all(
        out_term.reshape(q_own + c_own, n, -1).transpose(1, 0, 2), "seq", 0, 0, tiled=False
    )
    out_sum = jnp.concatenate(
        [out_sum[:, :q_own].reshape(query_w, -1), out_sum[:, q_own:].reshape(DI, -1)], 0
    )
    out_sum = lax.psum_scatter(out_sum, "fsdp", scatter_dimension=0, tiled=True).astype(f32)
    gu_sum = lax.psum_scatter(gate_up_term, "fsdp", scatter_dimension=0, tiled=True)
    gate_g, up_g = gu_sum[:, :f_own], gu_sum[:, f_own:]
    back_a = lax.ppermute(jnp.where(even, gate_g, up_g), "seq", [(t, s) for s, t in route_a])
    back_b = lax.ppermute(jnp.where(even, up_g, gate_g), "seq", [(t, s) for s, t in route_b])
    gu_sum = jnp.concatenate(
        [jnp.where(low_half, back_a, back_b), jnp.where(low_half, back_b, back_a)], 1
    ).astype(f32)
    in_part = lax.psum_scatter(in_term, "fsdp", scatter_dimension=0, tiled=True)
    in_sum = jnp.zeros((in_part.shape[0], sum(widths) * n), bf16)
    for s, w, e in zip(starts, widths, edges):
        in_sum = lax.dynamic_update_slice_in_dim(in_sum, in_part[:, e : e + w], s + me * w, 1)
    in_sum = lax.psum_scatter(in_sum, "seq", scatter_dimension=1, tiled=True).astype(f32)
    select_sum = lax.psum_scatter(select_term.astype(bf16), "fsdp", scatter_dimension=0, tiled=True).astype(f32)
    step_sum = lax.psum_scatter(step_term.astype(bf16), "fsdp", scatter_dimension=0, tiled=True).astype(f32)

    wide = jnp.stack([first_grad, second_grad, attn_grad])
    channel = jnp.concatenate(
        [
            mamba_grad[None], jnp.stack(conv_rows), conv_bias_grad[None], step_bias_grad[None],
            decay_log_grad, skip_grad[None],
        ],
        0,
    )
    wide = lax.psum(wide, ("seq", "fsdp"))
    channel = lax.all_gather(lax.psum(channel, "fsdp"), "seq", axis=1, tiled=True)
    return (
        out_tokens[None],
        tokens_grad[None],
        in_sum,
        out_sum,
        gu_sum,
        down_sum,
        select_sum,
        step_sum,
        wide[0],
        wide[1],
        wide[2],
        channel[0],
        channel[1 : 1 + KC],
        channel[1 + KC],
        channel[2 + KC],
        channel[3 + KC : 3 + KC + NS],
        channel[3 + KC + NS],
    )


def solution(mesh):
    split = P("fsdp", "seq")
    seq3 = P("fsdp", "seq", None)
    return jax.shard_map(
        functools.partial(layer, mesh.shape["seq"], mesh.shape["fsdp"]),
        mesh=mesh,
        in_specs=(seq3,) + (split,) * 7 + (P(),) * 9 + (seq3,),
        out_specs=(seq3, seq3) + (split,) * 6 + (P(),) * 9,
        check_vma=False,
    )
```

```python
import functools

import jax
import jax.numpy as jnp
from jax import lax
from jax.experimental import pallas as pl
from jax.experimental.pallas import tpu as pltpu
from jax.sharding import PartitionSpec as P

QUERY_HEADS = 25
KEY_VALUE_HEADS = 5
HEAD_SIZE = 64
DI = 3200
NS = 16
DTR = 100
KC = 4
F = 5504
WINDOW_TOKENS = 1024

norm_eps = 1e-05
masked_score = -1e30
log2e = 1.4426950408889634
bf16 = jnp.bfloat16
f32 = jnp.float32
MESH = pl.DeviceIdType.MESH


def matmul(left, right):
    return jnp.dot(left, right, preferred_element_type=f32)


def dot_tn(left, right):
    return lax.dot_general(left, right, (((0,), (0,)), ((), ())), preferred_element_type=f32)


def dot_nt(left, right):
    return lax.dot_general(left, right, (((1,), (1,)), ((), ())), preferred_element_type=f32)


def rms_norm(value, gain):
    scale = lax.rsqrt(jnp.mean(value * value, axis=-1, keepdims=True) + norm_eps)
    return (value * scale * gain, scale)


def norm_back(value, scale, gain, upstream):
    weighted = upstream * gain
    gain_grad = jnp.sum(upstream * value * scale, 0)
    inner_mean = jnp.mean(weighted * value, axis=-1, keepdims=True)
    return (scale * weighted - value * (scale * scale * scale) * inner_mean, gain_grad)


def park(part, j, value):
    for k, lane in enumerate(range(0, value.shape[1], 128)):
        end = min(lane + 128, value.shape[1])
        part[64 * k + 8 * j : 64 * k + 8 * j + 8, : end - lane] = value[:, lane:end]


def fold(part, out, t0):
    for k, lane in enumerate(range(0, out.shape[1], 128)):
        end = min(lane + 128, out.shape[1])
        total = part[pl.ds(64 * k, 8, stride=8), :]
        for s in range(1, 8):
            total = total + part[pl.ds(64 * k + s, 8, stride=8), :]
        out[pl.ds(t0, 8), lane:end] = total[:, : end - lane]


def scan_fwd_body(step_ref, push_ref, b_ref, c_ref, rate_ref, y_ref, st_ref, h_scr, part_scr):
    block = step_ref.shape[0]

    @pl.when(pl.program_id(0) == 0)
    def _():
        h_scr[...] = jnp.zeros_like(h_scr)

    rate = rate_ref[...]

    def group(index, state):
        t0 = pl.multiple_of(index * 8, 8)
        step8 = step_ref[pl.ds(t0, 8), :]
        push8 = push_ref[pl.ds(t0, 8), :]
        b_roll = pltpu.roll(b_ref[...], block - t0, 1)
        c_roll = pltpu.roll(c_ref[...], block - t0, 1)
        for j in range(8):
            decay = jnp.exp2(step8[j : j + 1, :] * rate)
            state = decay * state + push8[j : j + 1, :] * b_roll[:, j : j + 1]
            st_ref[t0 + j] = state
            out = c_roll[:, j : j + 1] * state
            park(part_scr, j, out[:8] + out[8:])
        fold(part_scr, y_ref, t0)
        return state

    h_scr[...] = lax.fori_loop(0, block // 8, group, h_scr[...])


def scan_bwd_body(
    step_ref, push_ref, dpre_ref, b_ref, c_ref, st_ref, prev_ref, rate_ref,
    pr_ref, pushed_ref, db_ref, dc_ref, log_ref, g_scr, log_scr, part1, part2,
):
    block = step_ref.shape[0]
    count = pl.num_programs(0)
    which = pl.program_id(0)

    @pl.when(which == 0)
    def _():
        g_scr[...] = jnp.zeros_like(g_scr)
        log_scr[...] = jnp.zeros_like(log_scr)

    lane_ids = lax.broadcasted_iota(jnp.int32, (NS, block), 1)
    before = prev_ref[0] * jnp.where(which == count - 1, 0.0, 1.0)

    def group(turn, carried):
        grad_in, state, db_acc, dc_acc = carried
        t0 = pl.multiple_of((block // 8 - 1 - turn) * 8, 8)
        step8 = step_ref[pl.ds(t0, 8), :]
        push8 = push_ref[pl.ds(t0, 8), :]
        dpre8 = dpre_ref[pl.ds(t0, 8), :]
        b_roll = pltpu.roll(b_ref[...], block - t0, 1)
        c_roll = pltpu.roll(c_ref[...], block - t0, 1)
        rate = rate_ref[...]
        log_acc = log_scr[...]
        for j in range(7, -1, -1):
            if j > 0:
                prior = st_ref[t0 + (j - 1)]
            else:
                prior = jnp.where(t0 > 0, st_ref[jnp.maximum(t0 - 1, 0)], before)
            step_row = step8[j : j + 1, :]
            dpre_row = dpre8[j : j + 1, :]
            grad = c_roll[:, j : j + 1] * dpre_row + grad_in
            grad_in = grad * jnp.exp2(step_row * (rate * log2e))
            flow = grad_in * prior
            by_rate = flow * rate
            park(part1, j, by_rate[:8] + by_rate[8:])
            by_b = grad * b_roll[:, j : j + 1]
            park(part2, j, by_b[:8] + by_b[8:])
            log_acc = log_acc + flow * step_row
            db = jnp.sum(grad * push8[j : j + 1, :], axis=1, keepdims=True)
            dc = jnp.sum(state * dpre_row, axis=1, keepdims=True)
            here = lane_ids == t0 + j
            db_acc = jnp.where(here, db, db_acc)
            dc_acc = jnp.where(here, dc, dc_acc)
            state = prior
        log_scr[...] = log_acc
        fold(part1, pr_ref, t0)
        fold(part2, pushed_ref, t0)
        return (grad_in, state, db_acc, dc_acc)

    zero = jnp.zeros((NS, block), f32)
    grad_in, _, db_acc, dc_acc = lax.fori_loop(
        0, block // 8, group, (g_scr[...], st_ref[block - 1], zero, zero)
    )
    g_scr[...] = grad_in
    db_ref[...] = db_acc
    dc_ref[...] = dc_acc

    @pl.when(which == count - 1)
    def _():
        log_ref[...] = log_scr[...] * rate_ref[...]


SCAN_BLOCK = 128


def scan_forward(step_keep, push, b_t, c_t, rate):
    tokens, width = step_keep.shape
    block = SCAN_BLOCK
    padded = (width + 127) // 128 * 128
    rows = pl.BlockSpec((block, width), lambda i: (i, 0))
    cols = pl.BlockSpec((NS, block), lambda i: (0, i))
    fixed = pl.BlockSpec((NS, width), lambda i: (0, 0))
    return pl.pallas_call(
        scan_fwd_body,
        grid=(tokens // block,),
        in_specs=[rows, rows, cols, cols, fixed],
        out_specs=[rows, pl.BlockSpec((block, NS, width), lambda i: (i, 0, 0))],
        out_shape=[
            jax.ShapeDtypeStruct((tokens, width), f32),
            jax.ShapeDtypeStruct((tokens, NS, width), f32),
        ],
        scratch_shapes=[pltpu.VMEM((NS, width), f32), pltpu.VMEM((padded // 2, 128), f32)],
        compiler_params=pltpu.CompilerParams(vmem_limit_bytes=40 << 20),
        cost_estimate=pl.CostEstimate(
            flops=tokens * width * NS * 8, bytes_accessed=tokens * width * NS * 4, transcendentals=tokens * width * NS
        ),
        name="scan_forward",
    )(step_keep, push, b_t, c_t, rate * log2e)


def scan_backward(step_keep, push, d_pre, b_t, c_t, states, rate):
    tokens, width = step_keep.shape
    block = SCAN_BLOCK
    padded = (width + 127) // 128 * 128
    last = tokens // block - 1
    rows = pl.BlockSpec((block, width), lambda i: (last - i, 0))
    cols = pl.BlockSpec((NS, block), lambda i: (0, last - i))
    fixed = pl.BlockSpec((NS, width), lambda i: (0, 0))
    return pl.pallas_call(
        scan_bwd_body,
        grid=(tokens // block,),
        in_specs=[
            rows, rows, rows, cols, cols,
            pl.BlockSpec((block, NS, width), lambda i: (last - i, 0, 0)),
            pl.BlockSpec((1, NS, width), lambda i: (jnp.maximum((last - i) * block - 1, 0), 0, 0)),
            fixed,
        ],
        out_specs=[rows, rows, cols, cols, fixed],
        out_shape=[
            jax.ShapeDtypeStruct((tokens, width), f32),
            jax.ShapeDtypeStruct((tokens, width), f32),
            jax.ShapeDtypeStruct((NS, tokens), f32),
            jax.ShapeDtypeStruct((NS, tokens), f32),
            jax.ShapeDtypeStruct((NS, width), f32),
        ],
        scratch_shapes=[
            pltpu.VMEM((NS, width), f32),
            pltpu.VMEM((NS, width), f32),
            pltpu.VMEM((padded // 2, 128), f32),
            pltpu.VMEM((padded // 2, 128), f32),
        ],
        compiler_params=pltpu.CompilerParams(vmem_limit_bytes=40 << 20),
        cost_estimate=pl.CostEstimate(
            flops=tokens * width * NS * 18, bytes_accessed=tokens * width * NS * 4, transcendentals=tokens * width * NS
        ),
        name="scan_backward",
    )(step_keep, push, d_pre, b_t, c_t, states, states, rate)


def places():
    me = lax.axis_index("seq")
    core, x, y = me % 2, (me // 2) % 2, me // 4
    sibling = me + 1 - 2 * core
    return me, core, sibling, 2 - 4 * x, 4 - 8 * y


def remote(src, dst, sems, k, to, axis="seq"):
    return pltpu.make_async_remote_copy(
        src_ref=src,
        dst_ref=dst,
        send_sem=sems.at[0, k],
        recv_sem=sems.at[1, k],
        device_id={axis: to},
        device_id_type=MESH,
    )


def greet(devices, axis="seq"):
    barrier = pltpu.get_barrier_semaphore()
    for d in devices:
        pl.semaphore_signal(barrier, inc=1, device_id={axis: d}, device_id_type=MESH)
    pl.semaphore_wait(barrier, len(devices))


def block_at(ref, d):
    if len(ref.shape) == 3:
        return ref.at[d]
    width = ref.shape[1] // 8
    return ref.at[:, pl.ds(pl.multiple_of(d * width, width), width)]


def halves(ref, tile):
    rows = ref.shape[0]
    top = (rows // 2 + tile - 1) // tile * tile
    return ref.at[pl.ds(0, top)], ref.at[pl.ds(top, rows - top)]


def gather_steps(out, sems, base, tile):
    me, core, sib, step_x, step_y = places()
    at_x, at_y = me + step_x, me + step_y
    diag = me + step_x + step_y

    def send(block, k, to):
        copy = remote(block, block, sems, base + k, to)
        copy.start()
        return copy

    mine, from_x, from_y, far = (block_at(out, d) for d in (me, at_x, at_y, diag))
    own_x, own_y, own_s = send(mine, 0, at_x), send(mine, 1, at_y), send(mine, 2, sib)
    own_x.wait_recv()
    on_y = send(halves(from_x, tile)[0], 3, at_y)
    pass_x = send(from_x, 5, sib)
    own_y.wait_recv()
    on_x = send(halves(from_y, tile)[1], 4, at_x)
    pass_y = send(from_y, 6, sib)
    on_y.wait_recv()
    pass_top = send(halves(far, tile)[0], 7, sib)
    on_x.wait_recv()
    pass_low = send(halves(far, tile)[1], 8, sib)
    for copy in (own_s, pass_x, pass_y, pass_top, pass_low):
        copy.wait()
    for copy in (own_x, own_y, on_x, on_y):
        copy.wait_send()


def gather_body(x_ref, out_ref, sems, local_sem):
    me, core, sib, step_x, step_y = places()
    mine = pltpu.make_async_copy(x_ref, out_ref.at[me], local_sem)
    mine.start()
    greet([sib, me + step_x, me + step_y])
    mine.wait()
    gather_steps(out_ref, sems, 0, 16)


def add_rows(out, parts, rows):
    def step(i, _):
        at = pl.ds(pl.multiple_of(i * rows, rows), rows)
        total = parts[0][at, :].astype(f32)
        for p in parts[1:]:
            total = total + p[at, :].astype(f32)
        out[at, :] = total.astype(out.dtype)
        return 0

    lax.fori_loop(0, out.shape[0] // rows, step, 0)


def scatter_steps(p_ref, out, from_sib, acc, got_x, got_y, last_x, last_y, sems, tile):
    me, core, sib, step_x, step_y = places()
    dests = (me + step_x + step_y, me + step_x, me + step_y, me)

    def send(src, dst, k, to):
        copy = remote(src, dst, sems, k, to)
        copy.start()
        return copy

    pairs = [send(block_at(p_ref, d + 1 - 2 * core), from_sib.at[k], k, sib) for k, d in enumerate(dests)]
    out_x, out_y = [], []
    for k, d in enumerate(dests):
        pairs[k].wait_recv()
        add_rows(acc.at[k], [block_at(p_ref, d), from_sib.at[k]], tile)
        top, low = halves(acc.at[k], tile)
        if k == 0:
            out_x.append(send(top, got_x.at[0], 4, me + step_x))
            out_y.append(send(low, got_y.at[0], 5, me + step_y))
        if k == 1:
            out_x.append(send(top, got_x.at[1], 6, me + step_x))
        if k == 2:
            out_y.append(send(low, got_y.at[1], 7, me + step_y))
    out_x[0].wait_recv()
    add_rows(got_x.at[0], [got_x.at[0], halves(acc.at[2], tile)[0]], tile)
    last_a = send(got_x.at[0], last_y, 8, me + step_y)
    out_y[0].wait_recv()
    add_rows(got_y.at[0], [got_y.at[0], halves(acc.at[1], tile)[1]], tile)
    last_b = send(got_y.at[0], last_x, 9, me + step_x)
    out_x[1].wait_recv()
    out_y[1].wait_recv()
    top, low = halves(acc.at[3], tile)
    out_top, out_low = halves(out, tile)
    last_a.wait_recv()
    add_rows(out_top, [got_x.at[1], top, last_y], tile)
    last_b.wait_recv()
    add_rows(out_low, [got_y.at[1], low, last_x], tile)
    for copy in pairs + out_x + out_y + [last_a, last_b]:
        copy.wait_send()


def scatter_body(p_ref, out_ref, from_sib, acc, got_x, got_y, last_x, last_y, sems):
    me, core, sib, step_x, step_y = places()
    greet([sib, me + step_x, me + step_y])
    scatter_steps(p_ref, out_ref, from_sib, acc, got_x, got_y, last_x, last_y, sems, 16)


def sum_body(p_ref, out_ref, from_sib, acc, got_x, got_y, last_x, last_y, sems):
    me, core, sib, step_x, step_y = places()
    greet([sib, me + step_x, me + step_y])
    scatter_steps(p_ref, block_at(out_ref, me), from_sib, acc, got_x, got_y, last_x, last_y, sems, 8)
    gather_steps(out_ref, sems, 10, 8)


def scatter_scratch(rows, width, dtype, tile):
    top = (rows // 2 + tile - 1) // tile * tile
    low = rows - top
    return [
        pltpu.VMEM((4, rows, width), dtype),
        pltpu.VMEM((4, rows, width), dtype),
        pltpu.VMEM((2, top, width), dtype),
        pltpu.VMEM((2, low, width), dtype),
        pltpu.VMEM((low, width), dtype),
        pltpu.VMEM((top, width), dtype),
    ]


def direct_body(axis, size, modes, *refs):
    count = len(modes)
    ins, outs, (sems, local_sems) = refs[:count], refs[count : 2 * count], refs[2 * count :]
    me = lax.axis_index(axis)
    own = []
    for a, (x, out, mode) in enumerate(zip(ins, outs, modes)):
        copy = pltpu.make_async_copy(x.at[me] if mode == "exchange" else x, out.at[me], local_sems.at[a])
        copy.start()
        own.append(copy)
    others = [(me + k) % size for k in range(1, size)]
    greet(others, axis)
    copies = []
    for a, (x, out, mode) in enumerate(zip(ins, outs, modes)):
        for k, to in enumerate(others):
            src = x.at[to] if mode == "exchange" else x
            copy = remote(src, out.at[me], sems, a * (size - 1) + k, to, axis)
            copy.start()
            copies.append(copy)
    for copy in own + copies:
        copy.wait()


any_space = pl.BlockSpec(memory_space=pl.ANY)
vmem_space = pl.BlockSpec(memory_space=pltpu.VMEM)


def comm_params(collective_id):
    return pltpu.CompilerParams(
        collective_id=collective_id, has_side_effects=True, vmem_limit_bytes=40 << 20
    )


def direct(axis, size, arrays, modes, collective_id):
    shapes = [x.shape if mode == "exchange" else (size,) + x.shape for x, mode in zip(arrays, modes)]
    return pl.pallas_call(
        functools.partial(direct_body, axis, size, modes),
        out_shape=[jax.ShapeDtypeStruct(s, x.dtype) for s, x in zip(shapes, arrays)],
        in_specs=[any_space] * len(arrays),
        out_specs=[any_space] * len(arrays),
        scratch_shapes=[
            pltpu.SemaphoreType.DMA((2, len(arrays) * (size - 1))),
            pltpu.SemaphoreType.DMA((len(arrays),)),
        ],
        compiler_params=comm_params(collective_id),
        name="direct_" + axis,
    )(*arrays)


def seq_gather(n, block, collective_id):
    if n != 8:
        return lax.all_gather(block, "seq", axis=0, tiled=False)
    return pl.pallas_call(
        gather_body,
        out_shape=jax.ShapeDtypeStruct((8,) + block.shape, block.dtype),
        in_specs=[any_space],
        out_specs=any_space,
        scratch_shapes=[pltpu.SemaphoreType.DMA((2, 9)), pltpu.SemaphoreType.DMA],
        compiler_params=comm_params(collective_id),
        name="seq_gather",
    )(block)


def seq_scatter(n, parts, collective_id):
    if n != 8:
        return lax.psum_scatter(parts, "seq", scatter_dimension=0, tiled=False).astype(f32)
    _, rows, width = parts.shape
    return pl.pallas_call(
        scatter_body,
        out_shape=jax.ShapeDtypeStruct((rows, width), f32),
        in_specs=[vmem_space],
        out_specs=vmem_space,
        scratch_shapes=scatter_scratch(rows, width, parts.dtype, 16) + [pltpu.SemaphoreType.DMA((2, 10))],
        compiler_params=comm_params(collective_id),
        name="seq_scatter",
    )(parts)


def seq_sum(n, parts, collective_id):
    if n != 8:
        return lax.psum(parts, "seq")
    rows, length = parts.shape
    return pl.pallas_call(
        sum_body,
        out_shape=jax.ShapeDtypeStruct(parts.shape, f32),
        in_specs=[vmem_space],
        out_specs=vmem_space,
        scratch_shapes=scatter_scratch(rows, length // 8, f32, 8) + [pltpu.SemaphoreType.DMA((2, 19))],
        compiler_params=comm_params(collective_id),
        name="seq_sum",
    )(parts)


def seq_token_sum(n, value, collective_id):
    if n != 8:
        return lax.psum(value, "seq")
    (got,) = direct("seq", n, [value.reshape(-1, 128)], ("gather",), collective_id)
    return jnp.sum(got, 0).reshape(-1)


def exchange(n, blocks, collective_id):
    if n != 8:
        return lax.all_to_all(blocks, "seq", 0, 0, tiled=False)
    return direct("seq", n, [blocks], ("exchange",), collective_id)[0]


def deal(total, parts, n):
    unit = 5 * n
    nat = jnp.arange(total, dtype=jnp.int32)
    start = jnp.zeros_like(nat)
    at = 0
    for w in parts[:-1]:
        at += w
        start = jnp.where(nat >= at, at, start)
    inside = nat - start
    owner = (inside % unit) // 5
    col = owner * (total // n) + start // n + (inside // unit) * 5 + inside % 5
    return (col[:, None] == nat[None, :]).astype(bf16)


def exact(left, right, contract, precision=None):
    return lax.dot_general(left, right, (contract, ((), ())), precision=precision, preferred_element_type=f32)


def attn_fwd_body(qt_ref, kt_ref, vt_ref, bias_ref, out_ref, lse_ref):
    keys = kt_ref[...].T
    for head in range(qt_ref.shape[0] // HEAD_SIZE):
        rows = slice(head * HEAD_SIZE, (head + 1) * HEAD_SIZE)
        scores = matmul(keys, qt_ref[rows, :]) + bias_ref[...]
        row_max = jnp.max(scores, 0, keepdims=True)
        exp_scores = jnp.exp(scores - row_max)
        row_total = jnp.sum(exp_scores, 0, keepdims=True)
        probs = (exp_scores * (1.0 / row_total)).astype(bf16)
        out_ref[rows, :] = matmul(vt_ref[...], probs)
        lse_ref[0, head : head + 1, :] = row_max + jnp.log(row_total)


def attn_bwd_body(qt_ref, kt_ref, vt_ref, dot_ref, lse_ref, bias_ref, dqt_ref, dkt_ref, dvt_ref):
    keys, values = kt_ref[...].T, vt_ref[...].T
    dk = jnp.zeros(keys.shape, f32)
    dv = jnp.zeros(values.shape, f32)
    for head in range(qt_ref.shape[0] // HEAD_SIZE):
        rows = slice(head * HEAD_SIZE, (head + 1) * HEAD_SIZE)
        q_t, do_t = qt_ref[rows, :], dot_ref[rows, :]
        scores = matmul(keys, q_t) + bias_ref[...]
        probs = jnp.exp(scores - lse_ref[0, head : head + 1, :])
        d_probs = matmul(values, do_t)
        inner = jnp.sum(probs * d_probs, 0, keepdims=True)
        d_scores = (probs * (d_probs - inner)).astype(bf16)
        dqt_ref[rows, :] = (matmul(kt_ref[...], d_scores) * (HEAD_SIZE**-0.5)).astype(bf16)
        dk = dk + matmul(d_scores, q_t.T)
        dv = dv + matmul(probs.astype(bf16), do_t.T)
    dkt_ref[...] = dk.T.astype(bf16)
    dvt_ref[...] = dv.T.astype(bf16)


def attn_specs(tokens, span, groups):
    heads = pl.BlockSpec((groups * HEAD_SIZE, tokens), lambda h: (h, 0))
    key = pl.BlockSpec((HEAD_SIZE, span), lambda h: (h, 0))
    value = pl.BlockSpec((HEAD_SIZE, span), lambda h: (KEY_VALUE_HEADS + h, 0))
    lse = pl.BlockSpec((1, 8, tokens), lambda h: (h, 0, 0))
    bias = pl.BlockSpec((span, tokens), lambda h: (0, 0))
    return heads, key, value, lse, bias


def attention_forward(q_t, kv_t, bias):
    span, tokens = bias.shape
    heads, key, value, lse, bias_spec = attn_specs(tokens, span, QUERY_HEADS // KEY_VALUE_HEADS)
    return pl.pallas_call(
        attn_fwd_body,
        grid=(KEY_VALUE_HEADS,),
        in_specs=[heads, key, value, bias_spec],
        out_specs=[heads, lse],
        out_shape=[
            jax.ShapeDtypeStruct(q_t.shape, f32),
            jax.ShapeDtypeStruct((KEY_VALUE_HEADS, 8, tokens), f32),
        ],
        compiler_params=pltpu.CompilerParams(vmem_limit_bytes=40 << 20),
        cost_estimate=pl.CostEstimate(
            flops=QUERY_HEADS * span * tokens * 512, bytes_accessed=8 << 20, transcendentals=QUERY_HEADS * span * tokens
        ),
        name="attention_forward",
    )(q_t, kv_t, kv_t, bias)


def attention_backward(q_t, kv_t, do_t, lse, bias):
    span, tokens = bias.shape
    heads, key, value, lse_spec, bias_spec = attn_specs(tokens, span, QUERY_HEADS // KEY_VALUE_HEADS)
    return pl.pallas_call(
        attn_bwd_body,
        grid=(KEY_VALUE_HEADS,),
        in_specs=[heads, key, value, heads, lse_spec, bias_spec],
        out_specs=[heads, key, key],
        out_shape=[
            jax.ShapeDtypeStruct(q_t.shape, bf16),
            jax.ShapeDtypeStruct((KEY_VALUE_HEADS * HEAD_SIZE, span), bf16),
            jax.ShapeDtypeStruct((KEY_VALUE_HEADS * HEAD_SIZE, span), bf16),
        ],
        compiler_params=pltpu.CompilerParams(vmem_limit_bytes=40 << 20),
        cost_estimate=pl.CostEstimate(
            flops=QUERY_HEADS * span * tokens * 1280, bytes_accessed=16 << 20, transcendentals=QUERY_HEADS * span * tokens
        ),
        name="attention_backward",
    )(q_t, kv_t, kv_t, do_t, lse, bias)


def layer(
    n,
    m,
    tokens,
    doc_ids,
    in_weight,
    out_weight,
    gate_up,
    down_weight,
    select_weight,
    step_weight,
    first_gain,
    second_gain,
    attn_gain,
    mamba_gain,
    conv_weight,
    conv_bias,
    step_bias,
    decay_log,
    skip_gain,
    cotangent,
):
    fast = n == 8
    me = lax.axis_index("seq")
    query_w = QUERY_HEADS * HEAD_SIZE
    key_w = KEY_VALUE_HEADS * HEAD_SIZE
    q_own, k_own, c_own, f_own = query_w // n, key_w // n, DI // n, F // n
    p_own = q_own + 2 * k_own + 2 * c_own
    kinds = (query_w, key_w, key_w, DI, DI)
    local, width = tokens.shape[1:]
    length = local * n
    z_rows = in_weight.shape[0]
    sel_rows = select_weight.shape[0]
    wide = p_own * n
    starts = (0, query_w, query_w + key_w, query_w + 2 * key_w, query_w + 2 * key_w + DI)
    widths = (q_own, k_own, k_own, c_own, c_own)
    highest = lax.Precision.HIGHEST

    small_w = jnp.concatenate([select_weight, step_weight], 0)
    if fast:
        deal_in, deal_small, deal_out = deal(p_own, (p_own,), n), deal(c_own, (c_own,), n), deal(out_weight.shape[0], (out_weight.shape[0],), n)
        in_blocks = exact(deal_in, in_weight, ((0,), (1,))).astype(bf16).reshape(n, p_own // n, z_rows)
        small_blocks = exact(deal_small, small_w, ((0,), (1,))).astype(bf16).reshape(n, c_own // n, -1)
        in_blocks, small_blocks, ids = direct(
            "seq", n, [in_blocks, small_blocks, doc_ids.reshape(-1, 128)], ("exchange", "exchange", "gather"), 0
        )
        ids = ids.reshape(-1)
        in_cols = in_blocks.reshape(p_own, z_rows).T
        small_cols = small_blocks.reshape(c_own, -1).T
        gu_blocks = gate_up.T.reshape(n, -1, z_rows)
        out_blocks = exact(deal_out, out_weight, ((0,), (0,))).astype(bf16).reshape(n, -1, out_weight.shape[1])
        down_blocks = down_weight.reshape(n, -1, down_weight.shape[1])
        gu_blocks, out_blocks, down_blocks = direct(
            "seq", n, [gu_blocks, out_blocks, down_blocks], ("exchange",) * 3, 1
        )
        gu_cols = gu_blocks.reshape(-1, z_rows).T
        out_rows = out_blocks.transpose(1, 0, 2).reshape(-1, width)
        down_rows = down_blocks.transpose(1, 0, 2).reshape(-1, width)
        (small_full,) = direct("fsdp", m, [small_cols], ("gather",), 2)
        out_full = lax.all_gather(out_rows, "fsdp", axis=0, tiled=True)
        down_full = lax.all_gather(down_rows, "fsdp", axis=0, tiled=True)
    else:
        ids = lax.all_gather(doc_ids[0], "seq", axis=0, tiled=True)
        in_cols = lax.all_gather(in_weight, "seq", axis=1, tiled=True)
        in_cols = jnp.concatenate(
            [lax.dynamic_slice_in_dim(in_cols, s + me * w, w, 1) for s, w in zip(starts, widths)], 1
        )
        small_full = lax.all_gather(small_w, "fsdp", axis=0, tiled=False)
        half = n // 2
        route_a = [(d, 2 * d if d < half else 2 * (d - half) + 1) for d in range(n)]
        route_b = [(d, 2 * d + 1 if d < half else 2 * (d - half)) for d in range(n)]
        low_half = me < half
        even = me % 2 == 0
        piece0, piece1 = gate_up[:, :f_own], gate_up[:, f_own:]
        got_a = lax.ppermute(jnp.where(low_half, piece0, piece1), "seq", route_a)
        got_b = lax.ppermute(jnp.where(low_half, piece1, piece0), "seq", route_b)
        gu_cols = jnp.concatenate([jnp.where(even, got_a, got_b), jnp.where(even, got_b, got_a)], 1)
        out_rows = lax.all_gather(out_weight, "fsdp", axis=0, tiled=True)
        out_rows = jnp.concatenate(
            [out_rows[:query_w].reshape(n, q_own, -1), out_rows[query_w:].reshape(n, c_own, -1)], 1
        )
        out_full = exchange(n, out_rows, None).transpose(1, 0, 2).reshape(q_own + c_own, -1)
        down_rows = lax.all_gather(down_weight, "fsdp", axis=0, tiled=True).reshape(n, f_own, -1)
        down_full = exchange(n, down_rows, None).transpose(1, 0, 2).reshape(f_own, -1)
    in_full = lax.all_gather(in_cols, "fsdp", axis=0, tiled=True)
    gu_full = lax.all_gather(gu_cols, "fsdp", axis=0, tiled=True)
    select_own = small_full[:, :sel_rows].reshape(-1, c_own)
    step_own = small_full[:, sel_rows:].reshape(-1, c_own)

    params = jnp.concatenate(
        [mamba_gain[None], conv_weight, conv_bias[None], step_bias[None], decay_log, skip_gain[None]], 0
    )
    if fast:
        params = params.reshape(-1, c_own)
        params = exact(params, deal(c_own, (c_own,), n), ((1,), (0,)), highest).reshape(-1, n, n, c_own // n)
        params = lax.dynamic_index_in_dim(params, me, 2, False).reshape(-1, c_own)
    else:
        params = lax.dynamic_slice_in_dim(params, me * c_own, c_own, 1)
    mamba_g, conv_w, conv_b, step_b = params[0], params[1 : 1 + KC], params[1 + KC], params[2 + KC]
    decay_l, skip_g = params[3 + KC : 3 + KC + NS], params[3 + KC + NS]

    def heads_in(blocks):
        blocks = blocks.reshape(query_w, local)
        return exact(deal(query_w, (query_w,), n), blocks, ((1,), (0,))).astype(bf16) if fast else blocks

    def heads_out(value):
        if fast:
            value = exact(deal(query_w, (query_w,), n), value, ((0,), (0,))).astype(bf16)
        return value.reshape(n, q_own, local)

    seq_x = tokens[0].astype(f32)
    normed_one, scale_one = rms_norm(seq_x, first_gain)
    normed_one = seq_gather(n, normed_one.astype(bf16), 3).reshape(length, width)
    qkv_w = q_own + 2 * k_own
    qkv_t = exact(in_full[:, :qkv_w], normed_one, ((0,), (1,))).astype(bf16)
    branch = matmul(normed_one, in_full[:, qkv_w:]).astype(bf16)
    inputs = branch[:, :c_own].astype(f32)
    gate_z = branch[:, c_own:].astype(f32)

    q_blocks = qkv_t[:q_own].reshape(q_own, n, local).transpose(1, 0, 2)
    q_t = heads_in(exchange(n, q_blocks, 4)) * bf16(HEAD_SIZE**-0.5)
    kv_all = seq_gather(n, qkv_t[q_own:], 5)
    reach = (WINDOW_TOKENS + local - 2) // local
    span = min((reach + 1) * local, length)
    first_key = jnp.clip((me - reach) * local, 0, length - span)
    kv_win = lax.dynamic_slice_in_dim(kv_all, first_key, span, 2)
    if fast:
        deal_kv = deal(2 * key_w, (key_w, key_w), n)
        kv_t = exact(deal_kv, kv_win.reshape(2 * key_w, span), ((1,), (0,))).astype(bf16)
    else:
        kv_t = jnp.concatenate(
            [kv_win[:, :k_own].reshape(key_w, span), kv_win[:, k_own:].reshape(key_w, span)], 0
        )
    query_pos = me * local + jnp.arange(local, dtype=jnp.int32)
    key_pos = first_key + jnp.arange(span, dtype=jnp.int32)
    offset = query_pos[None, :] - key_pos[:, None]
    key_ids = lax.dynamic_slice_in_dim(ids, first_key, span, 0)
    allowed = (offset >= 0) & (offset < WINDOW_TOKENS) & (doc_ids[0][None, :] == key_ids[:, None])
    bias = jnp.where(allowed, 0.0, masked_score).astype(f32)
    attended, lse = attention_forward(q_t, kv_t, bias)
    attn_scale = lax.rsqrt(jnp.mean(attended * attended, axis=0, keepdims=True) + norm_eps)
    attn_normed = (attended * attn_scale * attn_gain[:, None]).astype(bf16)
    attn_c = exchange(n, heads_out(attn_normed), 6).transpose(0, 2, 1).reshape(length, q_own)

    padded_inputs = jnp.pad(inputs, ((KC - 1, 0), (0, 0)))
    padded_ids = jnp.pad(ids, (KC - 1, 0), constant_values=-1)
    conv_sum = conv_b + jnp.zeros_like(inputs)
    same_masks = []
    for tap in range(KC):
        begin = KC - 1 - tap
        same = (padded_ids[begin : begin + length] == ids).astype(f32)[:, None]
        same_masks.append(same)
        conv_sum = conv_sum + conv_w[tap] * padded_inputs[begin : begin + length] * same
    activated_b = jax.nn.silu(conv_sum).astype(bf16)
    activated = activated_b.astype(f32)
    sel_pad = jnp.pad(select_own, ((0, (-select_own.shape[0]) % 8), (0, 0)))
    selected = seq_sum(n, dot_nt(sel_pad, activated_b), 7)
    step_raw = selected[:DTR].astype(bf16)
    b_t = selected[DTR : DTR + NS]
    c_t = selected[DTR + NS : DTR + 2 * NS]
    step_pre = dot_tn(step_raw, step_own) + step_b
    step_size = jax.nn.softplus(step_pre)
    rate = -jnp.exp(decay_l)
    changed = jnp.concatenate([jnp.zeros((1,), f32), (ids[1:] != ids[:-1]).astype(f32)])
    step_keep = step_size + 1e30 * changed[:, None]
    push = step_size * activated
    scan_out, states = scan_forward(step_keep, push, b_t, c_t, rate)
    mamba_pre = scan_out + skip_g * activated
    gate_sig = jax.nn.sigmoid(gate_z)
    mamba_out = mamba_pre * gate_z * gate_sig
    square_sum = seq_token_sum(n, jnp.sum(mamba_out * mamba_out, -1), 8)
    mamba_scale = lax.rsqrt(square_sum / DI + norm_eps)[:, None]
    mamba_normed = mamba_out * mamba_scale * mamba_g
    joined = jnp.concatenate([attn_c, mamba_normed.astype(bf16)], 1)
    mixed = seq_scatter(n, matmul(joined, out_full).astype(bf16).reshape(n, local, width), 9)
    hidden = seq_x + 0.5 * mixed
    normed_two, scale_two = rms_norm(hidden, second_gain)
    normed_two = seq_gather(n, normed_two.astype(bf16), 10).reshape(length, width)
    gate_up_out = matmul(normed_two, gu_full).astype(bf16)
    gate_part = gate_up_out[:, :f_own].astype(f32)
    up_part = gate_up_out[:, f_own:].astype(f32)
    gate_act = jax.nn.sigmoid(gate_part)
    inner = (gate_part * gate_act * up_part).astype(bf16)
    ffn = seq_scatter(n, matmul(inner, down_full).astype(bf16).reshape(n, local, width), 11)
    out_tokens = (hidden + ffn).astype(bf16)

    d_ffn = seq_gather(n, cotangent[0], 12).reshape(length, width)
    down_term = dot_tn(inner, d_ffn).astype(bf16)
    d_inner = dot_nt(d_ffn, down_full)
    d_gate_up = jnp.concatenate(
        [
            d_inner * up_part * gate_act * (1.0 + gate_part * (1.0 - gate_act)),
            d_inner * gate_part * gate_act,
        ],
        1,
    ).astype(bf16)
    gate_up_term = dot_tn(normed_two, d_gate_up).astype(bf16)
    d_normed_two = seq_scatter(n, dot_nt(d_gate_up, gu_full).astype(bf16).reshape(n, local, width), 13)
    d_hidden_part, second_grad = norm_back(hidden, scale_two, second_gain, d_normed_two)
    d_hidden = cotangent[0].astype(f32) + d_hidden_part
    d_mixed = seq_gather(n, d_hidden.astype(bf16), 14).reshape(length, width)
    out_term = (0.5 * dot_tn(joined, d_mixed)).astype(bf16)
    d_joined = 0.5 * dot_nt(d_mixed, out_full)

    d_attn = d_joined[:, :q_own].astype(bf16).reshape(n, local, q_own).transpose(0, 2, 1)
    d_attn = heads_in(exchange(n, d_attn, 15)).astype(f32)
    weighted_a = d_attn * attn_gain[:, None]
    attn_grad = jnp.sum(d_attn * attended * attn_scale, 1)
    mean_a = jnp.mean(weighted_a * attended, axis=0, keepdims=True)
    d_attended = attn_scale * weighted_a - attended * (attn_scale * attn_scale * attn_scale) * mean_a
    dq_t, dk_t, dv_t = attention_backward(q_t, kv_t, d_attended.astype(bf16), lse, bias)
    d_queries = exchange(n, heads_out(dq_t), 16).transpose(0, 2, 1).reshape(length, q_own)
    if fast:
        dkv = exact(deal_kv, jnp.concatenate([dk_t, dv_t], 0), ((0,), (0,))).astype(bf16).reshape(n, 2 * k_own, span)
    else:
        dkv = jnp.concatenate([dk_t.reshape(n, k_own, span), dv_t.reshape(n, k_own, span)], 1)
    dkv = lax.dynamic_update_slice_in_dim(jnp.zeros((n, 2 * k_own, length), bf16), dkv, first_key, 2)
    dkv = seq_scatter(n, dkv, 17).astype(bf16).T

    u = d_joined[:, q_own:]
    weighted = u * mamba_g
    inner_mean = seq_token_sum(n, jnp.sum(weighted * mamba_out, -1), 18)[:, None] / DI
    mamba_grad = jnp.sum(u * mamba_out * mamba_scale, 0)
    d_mamba = mamba_scale * weighted - mamba_out * (mamba_scale * mamba_scale * mamba_scale) * inner_mean
    d_pre = d_mamba * gate_z * gate_sig
    d_gate = d_mamba * mamba_pre * gate_sig * (1.0 + gate_z * (1.0 - gate_sig))
    skip_grad = jnp.sum(d_pre * activated, 0)
    by_rate, pushed, db_t, dc_t, decay_log_grad = scan_backward(
        step_keep, push, d_pre, b_t, c_t, states, rate
    )
    step_grads = by_rate + pushed * activated
    d_step_pre = step_grads * jax.nn.sigmoid(step_pre)
    step_bias_grad = jnp.sum(d_step_pre, 0)
    d_step_low = d_step_pre.astype(bf16)
    step_term = matmul(step_raw, d_step_low)
    d_selected = jnp.concatenate(
        [dot_nt(step_own, d_step_low), db_t, dc_t, jnp.zeros(((-DTR - 2 * NS) % 8, length), f32)], 0
    )
    d_selected = seq_sum(n, d_selected, 19)[: DTR + 2 * NS].astype(bf16)
    select_term = matmul(d_selected, activated_b)
    d_activated = d_pre * skip_g + pushed * step_size + dot_tn(d_selected, select_own)
    conv_sig = jax.nn.sigmoid(conv_sum)
    d_conv = d_activated * conv_sig * (1.0 + conv_sum * (1.0 - conv_sig))
    conv_bias_grad = jnp.sum(d_conv, 0)
    ext_grad = jnp.zeros((length + KC - 1, c_own), f32)
    conv_rows = []
    for tap in range(KC):
        begin = KC - 1 - tap
        masked_grad = d_conv * same_masks[tap]
        conv_rows.append(jnp.sum(masked_grad * padded_inputs[begin : begin + length], 0))
        ext_grad = ext_grad + jnp.pad(conv_w[tap] * masked_grad, ((begin, tap), (0, 0)))
    d_inputs = ext_grad[KC - 1 :]
    d_projected = jnp.concatenate([d_queries, dkv, d_inputs.astype(bf16), d_gate.astype(bf16)], 1)
    in_term = dot_tn(normed_one, d_projected).astype(bf16)
    d_normed_one = seq_scatter(n, dot_nt(d_projected, in_full).astype(bf16).reshape(n, local, width), 20)
    d_x_part, first_grad = norm_back(seq_x, scale_one, first_gain, d_normed_one)
    tokens_grad = (d_hidden + d_x_part).astype(bf16)

    gu_part = lax.psum_scatter(gate_up_term, "fsdp", scatter_dimension=0, tiled=True)
    in_part = lax.psum_scatter(in_term, "fsdp", scatter_dimension=0, tiled=True)
    small_term = jnp.concatenate(
        [select_term.reshape(m, sel_rows, c_own), step_term.reshape(m, -1, c_own)], 1
    ).astype(bf16)
    channel = jnp.concatenate(
        [
            mamba_grad[None], jnp.stack(conv_rows), conv_bias_grad[None], step_bias_grad[None],
            decay_log_grad, skip_grad[None],
        ],
        0,
    )
    wide_grads = jnp.stack([first_grad, second_grad, attn_grad])
    small_z, channel_z, wide_z = direct(
        "fsdp", m, [small_term, channel, wide_grads], ("exchange", "gather", "gather"), 21
    )
    small_part = jnp.sum(small_z.astype(f32), 0)
    channel, wide_grads = jnp.sum(channel_z, 0), jnp.sum(wide_z, 0)
    if fast:
        out_part = lax.psum_scatter(out_term.reshape(m, -1, width), "fsdp", scatter_dimension=0, tiled=False)
        down_part = lax.psum_scatter(down_term.reshape(m, -1, width), "fsdp", scatter_dimension=0, tiled=False)
        out_blocks = out_part.reshape(-1, n, width // n).transpose(1, 0, 2)
        down_blocks = down_part.reshape(-1, n, width // n).transpose(1, 0, 2)
        gu_blocks = gu_part.T.reshape(n, -1, z_rows)
        gu_blocks, out_blocks, down_blocks = direct(
            "seq", n, [gu_blocks, out_blocks, down_blocks], ("exchange",) * 3, 22
        )
        gu_sum = gu_blocks.reshape(-1, z_rows).T.astype(f32)
        out_sum = exact(deal_out, out_blocks.reshape(-1, width // n), ((1,), (0,)))
        down_sum = down_blocks.reshape(-1, width // n).astype(f32)
        small_blocks = small_part.astype(bf16).T.reshape(n, c_own // n, -1)
        small_blocks, channel_all, wide_all = direct(
            "seq", n, [small_blocks, channel, wide_grads], ("exchange", "gather", "gather"), 23
        )
        small_sum = exact(small_blocks.reshape(c_own, -1), deal_small, ((0,), (1,)))
        channel_rows = channel.shape[0]
        channel = channel_all.reshape(n, channel_rows, n, c_own // n).transpose(1, 2, 0, 3).reshape(-1, c_own)
        channel = exact(channel, deal_small, ((1,), (1,)), highest).reshape(channel_rows, DI)
        wide_grads = jnp.sum(wide_all, 0)
        (in_blocks,) = direct("seq", n, [in_part.T.reshape(n, -1, z_rows)], ("exchange",), 24)
        in_sum = exact(in_blocks.reshape(p_own, z_rows), deal_in, ((0,), (1,)))
    else:
        out_blocks = exchange(n, out_term.reshape(q_own + c_own, n, -1).transpose(1, 0, 2), None)
        out_sum = jnp.concatenate(
            [out_blocks[:, :q_own].reshape(query_w, -1), out_blocks[:, q_own:].reshape(DI, -1)], 0
        )
        out_sum = lax.psum_scatter(out_sum, "fsdp", scatter_dimension=0, tiled=True).astype(f32)
        down_sum = exchange(n, down_term.reshape(f_own, n, -1).transpose(1, 0, 2), None).reshape(F, -1)
        down_sum = lax.psum_scatter(down_sum, "fsdp", scatter_dimension=0, tiled=True).astype(f32)
        gate_g, up_g = gu_part[:, :f_own], gu_part[:, f_own:]
        back_a = lax.ppermute(jnp.where(even, gate_g, up_g), "seq", [(t, s) for s, t in route_a])
        back_b = lax.ppermute(jnp.where(even, up_g, gate_g), "seq", [(t, s) for s, t in route_b])
        gu_sum = jnp.concatenate(
            [jnp.where(low_half, back_a, back_b), jnp.where(low_half, back_b, back_a)], 1
        ).astype(f32)
        in_sum = jnp.zeros((z_rows, wide), bf16)
        at = 0
        for s, w in zip(starts, widths):
            in_sum = lax.dynamic_update_slice_in_dim(in_sum, in_part[:, at : at + w], s + me * w, 1)
            at += w
        in_sum = lax.psum_scatter(in_sum, "seq", scatter_dimension=1, tiled=True).astype(f32)
        small_sum = small_part
        channel = lax.all_gather(channel, "seq", axis=1, tiled=True)
        wide_grads = lax.psum(wide_grads, "seq")
    return (
        out_tokens[None],
        tokens_grad[None],
        in_sum,
        out_sum,
        gu_sum,
        down_sum,
        small_sum[:sel_rows],
        small_sum[sel_rows:],
        wide_grads[0],
        wide_grads[1],
        wide_grads[2],
        channel[0],
        channel[1 : 1 + KC],
        channel[1 + KC],
        channel[2 + KC],
        channel[3 + KC : 3 + KC + NS],
        channel[3 + KC + NS],
    )


def solution(mesh):
    split = P("fsdp", "seq")
    seq3 = P("fsdp", "seq", None)
    return jax.shard_map(
        functools.partial(layer, mesh.shape["seq"], mesh.shape["fsdp"]),
        mesh=mesh,
        in_specs=(seq3,) + (split,) * 7 + (P(),) * 9 + (seq3,),
        out_specs=(seq3, seq3) + (split,) * 6 + (P(),) * 9,
        check_vma=False,
    )
```

```python
import functools
import math

import jax
import jax.numpy as jnp
from jax import lax
from jax.experimental import pallas as pl
from jax.experimental.pallas import tpu as pltpu
from jax.sharding import PartitionSpec as P

QUERY_HEADS = 25
KEY_VALUE_HEADS = 5
HEAD_SIZE = 64
DI = 3200
NS = 16
DTR = 100
KC = 4
F = 5504
WINDOW_TOKENS = 1024

norm_eps = 1e-05
masked_score = -1e30
log2e = 1.4426950408889634
bf16 = jnp.bfloat16
f32 = jnp.float32
MESH = pl.DeviceIdType.MESH


def matmul(left, right):
    return jnp.dot(left, right, preferred_element_type=f32)


def dot_tn(left, right):
    return lax.dot_general(left, right, (((0,), (0,)), ((), ())), preferred_element_type=f32)


def dot_nt(left, right):
    return lax.dot_general(left, right, (((1,), (1,)), ((), ())), preferred_element_type=f32)


def rms_norm(value, gain):
    scale = lax.rsqrt(jnp.mean(value * value, axis=-1, keepdims=True) + norm_eps)
    return (value * scale * gain, scale)


def norm_back(value, scale, gain, upstream):
    weighted = upstream * gain
    gain_grad = jnp.sum(upstream * value * scale, 0)
    inner_mean = jnp.mean(weighted * value, axis=-1, keepdims=True)
    return (scale * weighted - value * (scale * scale * scale) * inner_mean, gain_grad)


def park(part, j, value):
    for k, lane in enumerate(range(0, value.shape[1], 128)):
        end = min(lane + 128, value.shape[1])
        part[64 * k + 8 * j : 64 * k + 8 * j + 8, : end - lane] = value[:, lane:end]


def fold(part, out, t0):
    for k, lane in enumerate(range(0, out.shape[1], 128)):
        end = min(lane + 128, out.shape[1])
        total = part[pl.ds(64 * k, 8, stride=8), :]
        for s in range(1, 8):
            total = total + part[pl.ds(64 * k + s, 8, stride=8), :]
        out[pl.ds(t0, 8), lane:end] = total[:, : end - lane]


def spread(split_ref, eye_ref, out_scr):
    eye = eye_ref[...]
    ones = jnp.ones((2 * NS, 128), bf16)
    for first in range(0, split_ref.shape[0], 16):
        split = split_ref[first : first + 16, :]
        spaced = jnp.concatenate([split[j : j + 1, :] * eye for j in range(16)], 0).astype(bf16)
        out_scr[first * NS : (first + 16) * NS, :] = matmul(spaced, ones)


def widen(value, width):
    return jnp.concatenate([value] * (width // 128) + ([value[:, : width % 128]] if width % 128 else []), 1)


def scan_fwd_body(
    step_ref, push_ref, b_ref, c_ref, rate_ref, eye_ref, y_ref, st_ref, h_scr, part_scr, b_scr, c_scr
):
    block = step_ref.shape[0]

    @pl.when(pl.program_id(0) == 0)
    def _():
        h_scr[...] = jnp.zeros_like(h_scr)

    spread(b_ref, eye_ref, b_scr)
    spread(c_ref, eye_ref, c_scr)
    rate = rate_ref[...]
    width = rate.shape[1]

    def group(index, state):
        t0 = pl.multiple_of(index * 8, 8)
        step8 = step_ref[pl.ds(t0, 8), :]
        push8 = push_ref[pl.ds(t0, 8), :]
        for j in range(8):
            at = pl.ds(pl.multiple_of((t0 + j) * NS, NS), NS)
            decay = jnp.exp(step8[j : j + 1, :] * rate)
            state = decay * state + push8[j : j + 1, :] * widen(b_scr[at, :], width)
            st_ref[t0 + j] = state.astype(bf16)
            out = widen(c_scr[at, :], width) * state
            park(part_scr, j, out[:8] + out[8:])
        fold(part_scr, y_ref, t0)
        return state

    h_scr[...] = lax.fori_loop(0, block // 8, group, h_scr[...])


def scan_bwd_body(
    step_ref, push_ref, dpre_ref, b_ref, c_ref, st_ref, prev_ref, rate_ref, eye_ref, *refs
):
    pr_ref, pushed_ref, db_ref, dc_ref, log_ref = refs[-12:-7]
    g_scr, log_scr, part1, part2, b_scr, c_scr, grad_scr = refs[-7:]
    block = step_ref.shape[0]
    count = pl.num_programs(0)
    which = pl.program_id(0)

    @pl.when(which == 0)
    def _():
        g_scr[...] = jnp.zeros_like(g_scr)
        log_scr[...] = jnp.zeros_like(log_scr)

    spread(b_ref, eye_ref, b_scr)
    spread(c_ref, eye_ref, c_scr)
    width = rate_ref.shape[1]
    before = prev_ref[0].astype(f32) * jnp.where(which == count - 1, 0.0, 1.0)

    def group(turn, grad_in):
        t0 = pl.multiple_of((block // 8 - 1 - turn) * 8, 8)
        step8 = step_ref[pl.ds(t0, 8), :]
        dpre8 = dpre_ref[pl.ds(t0, 8), :]
        rate = rate_ref[...]
        log_acc = log_scr[...]
        for j in range(7, -1, -1):
            at = pl.ds(pl.multiple_of((t0 + j) * NS, NS), NS)
            if j > 0:
                prior = st_ref[t0 + (j - 1)].astype(f32)
            else:
                prior = jnp.where(t0 > 0, st_ref[jnp.maximum(t0 - 1, 0)].astype(f32), before)
            step_row = step8[j : j + 1, :]
            grad = widen(c_scr[at, :], width) * dpre8[j : j + 1, :] + grad_in
            grad_scr[at, :] = grad.astype(bf16)
            grad_in = grad * jnp.exp(step_row * rate)
            flow = grad_in * prior
            by_rate = flow * rate
            park(part1, j, by_rate[:8] + by_rate[8:])
            by_b = grad * widen(b_scr[at, :], width)
            park(part2, j, by_b[:8] + by_b[8:])
            log_acc = log_acc + flow * step_row
        log_scr[...] = log_acc
        fold(part1, pr_ref, t0)
        fold(part2, pushed_ref, t0)
        return grad_in

    g_scr[...] = lax.fori_loop(0, block // 8, group, g_scr[...])

    lanes = lax.broadcasted_iota(jnp.int32, (NS, block), 1)

    def own_token(left, right_ref, out_ref):
        right = right_ref[...].astype(bf16)

        totals = []
        for i in range(block // 16):
            pairs = dot_nt(left(i), right)
            total = pairs[:NS]
            for j in range(1, 16):
                total = jnp.where(lanes == i * 16 + j, pairs[j * NS : (j + 1) * NS], total)
            totals.append(total)
        total = totals[0]
        for i in range(1, block // 16):
            total = jnp.where(lanes >= i * 16, totals[i], total)
        out_ref[...] = total

    own_token(lambda i: grad_scr[i * 16 * NS : (i + 1) * 16 * NS, :], push_ref, db_ref)
    own_token(lambda i: st_ref[i * 16 : (i + 1) * 16].reshape(16 * NS, width), dpre_ref, dc_ref)

    @pl.when(which == count - 1)
    def _():
        log_ref[...] = log_scr[...] * rate_ref[...]


SCAN_BLOCK = 128


def split_halves(value):
    high = lax.reduce_precision(value, 8, 7)
    low = lax.reduce_precision(value - high, 8, 7)
    return jnp.concatenate([high, low], 0).T


def scan_forward(step_keep, push, b_t, c_t, rate):
    tokens, width = step_keep.shape
    block = SCAN_BLOCK
    padded = (width + 127) // 128 * 128
    rows = pl.BlockSpec((block, width), lambda i: (i, 0))
    halves_spec = pl.BlockSpec((block, 2 * NS), lambda i: (i, 0))
    fixed = pl.BlockSpec((NS, width), lambda i: (0, 0))
    eye = jnp.concatenate([jnp.eye(NS, dtype=f32)] * 2, 1)
    return pl.pallas_call(
        scan_fwd_body,
        grid=(tokens // block,),
        in_specs=[rows, rows, halves_spec, halves_spec, fixed, pl.BlockSpec(eye.shape, lambda i: (0, 0))],
        out_specs=[rows, pl.BlockSpec((block, NS, width), lambda i: (i, 0, 0))],
        out_shape=[
            jax.ShapeDtypeStruct((tokens, width), f32),
            jax.ShapeDtypeStruct((tokens, NS, width), bf16),
        ],
        scratch_shapes=[
            pltpu.VMEM((NS, width), f32),
            pltpu.VMEM((padded // 2, 128), f32),
            pltpu.VMEM((block * NS, 128), f32),
            pltpu.VMEM((block * NS, 128), f32),
        ],
        compiler_params=pltpu.CompilerParams(vmem_limit_bytes=40 << 20),
        cost_estimate=pl.CostEstimate(
            flops=tokens * width * NS * 8, bytes_accessed=tokens * width * NS * 4, transcendentals=tokens * width * NS
        ),
        name="scan_forward",
    )(step_keep, push, split_halves(b_t), split_halves(c_t), rate, eye)


def scan_backward(step_keep, push, d_pre, b_t, c_t, states, rate, after=()):
    tokens, width = step_keep.shape
    block = SCAN_BLOCK
    padded = (width + 127) // 128 * 128
    last = tokens // block - 1
    rows = pl.BlockSpec((block, width), lambda i: (last - i, 0))
    cols = pl.BlockSpec((NS, block), lambda i: (0, last - i))
    halves_spec = pl.BlockSpec((block, 2 * NS), lambda i: (last - i, 0))
    fixed = pl.BlockSpec((NS, width), lambda i: (0, 0))
    eye = jnp.concatenate([jnp.eye(NS, dtype=f32)] * 2, 1)
    return pl.pallas_call(
        scan_bwd_body,
        grid=(tokens // block,),
        in_specs=[
            rows, rows, rows, halves_spec, halves_spec,
            pl.BlockSpec((block, NS, width), lambda i: (last - i, 0, 0)),
            pl.BlockSpec((1, NS, width), lambda i: (jnp.maximum((last - i) * block - 1, 0), 0, 0)),
            fixed, pl.BlockSpec(eye.shape, lambda i: (0, 0)),
        ] + [pl.BlockSpec(memory_space=pl.ANY)] * len(after),
        out_specs=[rows, rows, cols, cols, fixed],
        out_shape=[
            jax.ShapeDtypeStruct((tokens, width), f32),
            jax.ShapeDtypeStruct((tokens, width), f32),
            jax.ShapeDtypeStruct((NS, tokens), f32),
            jax.ShapeDtypeStruct((NS, tokens), f32),
            jax.ShapeDtypeStruct((NS, width), f32),
        ],
        scratch_shapes=[
            pltpu.VMEM((NS, width), f32),
            pltpu.VMEM((NS, width), f32),
            pltpu.VMEM((padded // 2, 128), f32),
            pltpu.VMEM((padded // 2, 128), f32),
            pltpu.VMEM((block * NS, 128), f32),
            pltpu.VMEM((block * NS, 128), f32),
            pltpu.VMEM((block * NS, width), bf16),
        ],
        compiler_params=pltpu.CompilerParams(vmem_limit_bytes=40 << 20),
        cost_estimate=pl.CostEstimate(
            flops=tokens * width * NS * 18, bytes_accessed=tokens * width * NS * 4, transcendentals=tokens * width * NS
        ),
        name="scan_backward",
    )(step_keep, push, d_pre, split_halves(b_t), split_halves(c_t), states, states, rate, eye, *after)


def places():
    me = lax.axis_index("seq")
    core, x, y = me % 2, (me // 2) % 2, me // 4
    sibling = me + 1 - 2 * core
    return me, core, sibling, 2 - 4 * x, 4 - 8 * y


def remote(src, dst, sems, k, to, axis="seq"):
    return pltpu.make_async_remote_copy(
        src_ref=src,
        dst_ref=dst,
        send_sem=sems.at[0, k],
        recv_sem=sems.at[1, k],
        device_id={axis: to},
        device_id_type=MESH,
    )


def greet(devices, axis="seq"):
    barrier = pltpu.get_barrier_semaphore()
    for d in devices:
        pl.semaphore_signal(barrier, inc=1, device_id={axis: d}, device_id_type=MESH)
    pl.semaphore_wait(barrier, len(devices))


def block_at(ref, d):
    if len(ref.shape) == 3:
        return ref.at[d]
    width = ref.shape[1] // 8
    return ref.at[:, pl.ds(pl.multiple_of(d * width, width), width)]


def halves(ref, tile):
    rows = ref.shape[0]
    top = (rows // 2 + tile - 1) // tile * tile
    return ref.at[pl.ds(0, top)], ref.at[pl.ds(top, rows - top)]


def gather_steps(out, sems, base, tile):
    me, core, sib, step_x, step_y = places()
    at_x, at_y = me + step_x, me + step_y
    diag = me + step_x + step_y

    def send(block, k, to):
        copy = remote(block, block, sems, base + k, to)
        copy.start()
        return copy

    mine, from_x, from_y, far = (block_at(out, d) for d in (me, at_x, at_y, diag))
    own_x, own_y, own_s = send(mine, 0, at_x), send(mine, 1, at_y), send(mine, 2, sib)
    own_x.wait_recv()
    on_y = send(halves(from_x, tile)[0], 3, at_y)
    pass_x = send(from_x, 5, sib)
    own_y.wait_recv()
    on_x = send(halves(from_y, tile)[1], 4, at_x)
    pass_y = send(from_y, 6, sib)
    on_y.wait_recv()
    pass_top = send(halves(far, tile)[0], 7, sib)
    on_x.wait_recv()
    pass_low = send(halves(far, tile)[1], 8, sib)
    for copy in (own_s, pass_x, pass_y, pass_top, pass_low):
        copy.wait()
    for copy in (own_x, own_y, on_x, on_y):
        copy.wait_send()


def gather_body(x_ref, *refs):
    out_ref, sems, local_sem = refs[-3:]
    me, core, sib, step_x, step_y = places()
    mine = pltpu.make_async_copy(x_ref, out_ref.at[me], local_sem)
    mine.start()
    greet([sib, me + step_x, me + step_y])
    mine.wait()
    gather_steps(out_ref, sems, 0, 16)


def add_rows(out, parts, rows):
    def step(i, _):
        at = pl.ds(pl.multiple_of(i * rows, rows), rows)
        total = parts[0][at, :].astype(f32)
        for p in parts[1:]:
            total = total + p[at, :].astype(f32)
        out[at, :] = total.astype(out.dtype)
        return 0

    lax.fori_loop(0, out.shape[0] // rows, step, 0)


def scatter_steps(p_ref, out, from_sib, acc, got_x, got_y, last_x, last_y, sems, tile):
    me, core, sib, step_x, step_y = places()
    dests = (me + step_x + step_y, me + step_x, me + step_y, me)

    def send(src, dst, k, to):
        copy = remote(src, dst, sems, k, to)
        copy.start()
        return copy

    pairs = [send(block_at(p_ref, d + 1 - 2 * core), from_sib.at[k], k, sib) for k, d in enumerate(dests)]
    out_x, out_y = [], []
    for k, d in enumerate(dests):
        pairs[k].wait_recv()
        add_rows(acc.at[k], [block_at(p_ref, d), from_sib.at[k]], tile)
        top, low = halves(acc.at[k], tile)
        if k == 0:
            out_x.append(send(top, got_x.at[0], 4, me + step_x))
            out_y.append(send(low, got_y.at[0], 5, me + step_y))
        if k == 1:
            out_x.append(send(top, got_x.at[1], 6, me + step_x))
        if k == 2:
            out_y.append(send(low, got_y.at[1], 7, me + step_y))
    out_x[0].wait_recv()
    add_rows(got_x.at[0], [got_x.at[0], halves(acc.at[2], tile)[0]], tile)
    last_a = send(got_x.at[0], last_y, 8, me + step_y)
    out_y[0].wait_recv()
    add_rows(got_y.at[0], [got_y.at[0], halves(acc.at[1], tile)[1]], tile)
    last_b = send(got_y.at[0], last_x, 9, me + step_x)
    out_x[1].wait_recv()
    out_y[1].wait_recv()
    top, low = halves(acc.at[3], tile)
    out_top, out_low = halves(out, tile)
    last_a.wait_recv()
    add_rows(out_top, [got_x.at[1], top, last_y], tile)
    last_b.wait_recv()
    add_rows(out_low, [got_y.at[1], low, last_x], tile)
    for copy in pairs + out_x + out_y + [last_a, last_b]:
        copy.wait_send()


def product_scatter_body(transposed, a_ref, w_ref, *refs):
    out_ref, stage, from_sib, acc, got_x, got_y, last_x, last_y, sems = refs[-9:]
    me, core, sib, step_x, step_y = places()
    rows, width = out_ref.shape
    greet([sib, me + step_x, me + step_y])
    dests = (me + step_x + step_y, me + step_x, me + step_y, me)

    def multiply(d, store):
        left = a_ref[pl.ds(pl.multiple_of(d * rows, rows), rows), :]

        def part(cols):
            if transposed:
                return dot_nt(left, w_ref[cols, :])
            return matmul(left, w_ref[:, cols])

        def step(i, _):
            cols = pl.ds(pl.multiple_of(i * 512, 512), 512)
            store(cols, part(cols))
            return 0

        lax.fori_loop(0, width // 512, step, 0, unroll=True)
        if width % 512:
            cols = pl.ds(width // 512 * 512, width % 512)
            store(cols, part(cols))

    def send(src, dst, k, to):
        copy = remote(src, dst, sems, k, to)
        copy.start()
        return copy

    def for_sibling(k):
        def store(cols, value):
            stage[k, :, cols] = value.astype(bf16)

        multiply(dests[k] + 1 - 2 * core, store)
        return send(stage.at[k], from_sib.at[k], k, sib)

    def for_chip(k):
        def store(cols, value):
            acc[k, :, cols] = (value + from_sib[k, :, cols].astype(f32)).astype(bf16)

        pairs[k].wait_recv()
        multiply(dests[k], store)
        return halves(acc.at[k], 16)

    pairs = [for_sibling(0), for_sibling(1)]
    top, low = for_chip(0)
    out_x = [send(top, got_x.at[0], 4, me + step_x)]
    out_y = [send(low, got_y.at[0], 5, me + step_y)]
    pairs.append(for_sibling(2))
    top, low = for_chip(1)
    out_x.append(send(top, got_x.at[1], 6, me + step_x))
    pairs.append(for_sibling(3))
    top, low = for_chip(2)
    out_y.append(send(low, got_y.at[1], 7, me + step_y))
    out_x[0].wait_recv()
    add_rows(got_x.at[0], [got_x.at[0], halves(acc.at[2], 16)[0]], 16)
    last_a = send(got_x.at[0], last_y, 8, me + step_y)
    out_y[0].wait_recv()
    add_rows(got_y.at[0], [got_y.at[0], halves(acc.at[1], 16)[1]], 16)
    last_b = send(got_y.at[0], last_x, 9, me + step_x)
    top, low = for_chip(3)
    out_x[1].wait_recv()
    out_y[1].wait_recv()
    out_top, out_low = halves(out_ref, 16)
    last_a.wait_recv()
    add_rows(out_top, [got_x.at[1], top, last_y], 16)
    last_b.wait_recv()
    add_rows(out_low, [got_y.at[1], low, last_x], 16)
    for copy in pairs + out_x + out_y + [last_a, last_b]:
        copy.wait_send()


def scatter_body(p_ref, *refs):
    out_ref, from_sib, acc, got_x, got_y, last_x, last_y, sems = refs[-8:]
    me, core, sib, step_x, step_y = places()
    greet([sib, me + step_x, me + step_y])
    scatter_steps(p_ref, out_ref, from_sib, acc, got_x, got_y, last_x, last_y, sems, 16)


def sum_body(p_ref, out_ref, from_sib, acc, got_x, got_y, last_x, last_y, sems):
    me, core, sib, step_x, step_y = places()
    greet([sib, me + step_x, me + step_y])
    scatter_steps(p_ref, block_at(out_ref, me), from_sib, acc, got_x, got_y, last_x, last_y, sems, 8)
    gather_steps(out_ref, sems, 10, 8)


def scatter_scratch(rows, width, dtype, tile):
    top = (rows // 2 + tile - 1) // tile * tile
    low = rows - top
    return [
        pltpu.VMEM((4, rows, width), dtype),
        pltpu.VMEM((4, rows, width), dtype),
        pltpu.VMEM((2, top, width), dtype),
        pltpu.VMEM((2, low, width), dtype),
        pltpu.VMEM((low, width), dtype),
        pltpu.VMEM((top, width), dtype),
    ]


def direct_copies(sizes, axes, modes, ins, outs, sems, local_sems):
    me = {axis: lax.axis_index(axis) for axis in sizes}
    others = {axis: [(me[axis] + k) % size for k in range(1, size)] for axis, size in sizes.items()}
    own, copies = [], []
    for a, (x, out, axis, mode) in enumerate(zip(ins, outs, axes, modes)):
        at = me[axis]
        own.append(pltpu.make_async_copy(x.at[at] if mode == "exchange" else x, out.at[at], local_sems.at[a]))
        for to in others[axis]:
            src = x.at[to] if mode == "exchange" else x
            copies.append(remote(src, out.at[at], sems, len(copies), to, axis))
    return others, own, copies


def direct_start(plan):
    others, own, copies = plan
    for copy in own:
        copy.start()
    barrier = pltpu.get_barrier_semaphore()
    for axis, devices in others.items():
        for d in devices:
            pl.semaphore_signal(barrier, inc=1, device_id={axis: d}, device_id_type=MESH)
    pl.semaphore_wait(barrier, sum(len(devices) for devices in others.values()))
    for copy in copies:
        copy.start()


def direct_wait(plan):
    for copy in plan[1] + plan[2]:
        copy.wait()


def direct_scratch(sizes, axes):
    return [
        pltpu.SemaphoreType.DMA((2, sum(sizes[axis] - 1 for axis in axes))),
        pltpu.SemaphoreType.DMA((len(axes),)),
    ]


def direct_body(sizes, axes, modes, unused, *refs):
    count = len(modes)
    ins, refs = refs[:count], refs[count + unused :]
    plan = direct_copies(sizes, axes, modes, ins, refs[:count], *refs[count:])
    direct_start(plan)
    direct_wait(plan)


any_space = pl.BlockSpec(memory_space=pl.ANY)
vmem_space = pl.BlockSpec(memory_space=pltpu.VMEM)


def comm_params(collective_id):
    return pltpu.CompilerParams(
        collective_id=collective_id, has_side_effects=True, vmem_limit_bytes=48 << 20
    )


def direct(sizes, arrays, collective_id, after=()):
    values = [x for x, _, _ in arrays]
    axes = [axis for _, axis, _ in arrays]
    modes = [mode for _, _, mode in arrays]
    sizes = {axis: sizes[axis] for axis in sorted(set(axes))}
    shapes = [x.shape if mode == "exchange" else (sizes[axis],) + x.shape for x, axis, mode in arrays]
    return pl.pallas_call(
        functools.partial(direct_body, sizes, axes, modes, len(after)),
        out_shape=[jax.ShapeDtypeStruct(s, x.dtype) for s, x in zip(shapes, values)],
        in_specs=[any_space] * (len(values) + len(after)),
        out_specs=[any_space] * len(values),
        scratch_shapes=direct_scratch(sizes, axes),
        compiler_params=comm_params(collective_id),
        name="direct",
    )(*values, *after)


def seq_gather(n, block, collective_id, after=()):
    if n != 8:
        return lax.all_gather(block, "seq", axis=0, tiled=False)
    return pl.pallas_call(
        gather_body,
        out_shape=jax.ShapeDtypeStruct((8,) + block.shape, block.dtype),
        in_specs=[any_space] * (1 + len(after)),
        out_specs=any_space,
        scratch_shapes=[pltpu.SemaphoreType.DMA((2, 9)), pltpu.SemaphoreType.DMA],
        compiler_params=comm_params(collective_id),
        name="seq_gather",
    )(block, *after)


def seq_scatter(n, parts, collective_id, after=()):
    if n != 8:
        return lax.psum_scatter(parts, "seq", scatter_dimension=0, tiled=False).astype(f32)
    _, rows, width = parts.shape
    return pl.pallas_call(
        scatter_body,
        out_shape=jax.ShapeDtypeStruct((rows, width), f32),
        in_specs=[vmem_space] + [any_space] * len(after),
        out_specs=vmem_space,
        scratch_shapes=scatter_scratch(rows, width, parts.dtype, 16) + [pltpu.SemaphoreType.DMA((2, 10))],
        compiler_params=comm_params(collective_id),
        name="seq_scatter",
    )(parts, *after)


def product_scatter(n, a, w, transposed, collective_id, after=()):
    if n != 8:
        product = (dot_nt if transposed else matmul)(a, w).astype(bf16)
        return lax.psum_scatter(product, "seq", scatter_dimension=0, tiled=True).astype(f32)
    rows, width = a.shape[0] // 8, w.shape[0 if transposed else 1]
    return pl.pallas_call(
        functools.partial(product_scatter_body, transposed),
        out_shape=jax.ShapeDtypeStruct((rows, width), f32),
        in_specs=[vmem_space, vmem_space] + [any_space] * len(after),
        out_specs=vmem_space,
        scratch_shapes=[pltpu.VMEM((4, rows, width), bf16)]
        + scatter_scratch(rows, width, bf16, 16)
        + [pltpu.SemaphoreType.DMA((2, 10))],
        compiler_params=comm_params(collective_id),
        cost_estimate=pl.CostEstimate(
            flops=2 * a.shape[0] * a.shape[1] * width, bytes_accessed=100 << 20, transcendentals=0
        ),
        name="product_scatter",
    )(a, w, *after)


def seq_sum(n, parts, collective_id):
    if n != 8:
        return lax.psum(parts, "seq")
    rows, length = parts.shape
    return pl.pallas_call(
        sum_body,
        out_shape=jax.ShapeDtypeStruct(parts.shape, f32),
        in_specs=[vmem_space],
        out_specs=vmem_space,
        scratch_shapes=scatter_scratch(rows, length // 8, f32, 8) + [pltpu.SemaphoreType.DMA((2, 19))],
        compiler_params=comm_params(collective_id),
        name="seq_sum",
    )(parts)


def seq_token_sum(n, value, collective_id):
    if n != 8:
        return lax.psum(value, "seq")
    (got,) = direct({"seq": n}, [(value.reshape(-1, 128), "seq", "gather")], collective_id)
    return jnp.sum(got, 0).reshape(-1)


def exchange(n, blocks, collective_id, after=()):
    if n != 8:
        return lax.all_to_all(blocks, "seq", 0, 0, tiled=False)
    return direct({"seq": n}, [(blocks, "seq", "exchange")], collective_id, after)[0]


def deal(total, parts, n):
    unit = 5 * n
    nat = jnp.arange(total, dtype=jnp.int32)
    start = jnp.zeros_like(nat)
    at = 0
    for w in parts[:-1]:
        at += w
        start = jnp.where(nat >= at, at, start)
    inside = nat - start
    owner = (inside % unit) // 5
    col = owner * (total // n) + start // n + (inside // unit) * 5 + inside % 5
    return (col[:, None] == nat[None, :]).astype(bf16)


def exact(left, right, contract, precision=None):
    return lax.dot_general(left, right, (contract, ((), ())), precision=precision, preferred_element_type=f32)


def window_start(tokens, span, length):
    me = lax.axis_index("seq")
    reach = (WINDOW_TOKENS + tokens - 2) // tokens
    if length == 2 * reach * tokens:
        first = me // reach * (me - reach) * tokens
    else:
        first = jnp.minimum(jnp.maximum(me - reach, 0) * tokens, length - span)
    return pl.ds(pl.multiple_of(first, math.gcd(tokens, length - span)), span)


def with_exchange(body, count, ins, outs):
    def whole(*refs):
        given, moved = refs[:ins], refs[ins : ins + count]
        refs = refs[ins + count :]
        made, arrived, sems = refs[:outs], refs[outs : outs + count], refs[outs + count :]
        if count:
            plan = direct_copies({"seq": 8}, ("seq",) * count, ("exchange",) * count, moved, arrived, *sems)

            @pl.when(pl.program_id(0) == 0)
            def _():
                direct_start(plan)

        body(*given, *made)
        if count:

            @pl.when(pl.program_id(0) == KEY_VALUE_HEADS - 1)
            def _():
                direct_wait(plan)

    return whole


def attn_fwd_body(qt_ref, kt_ref, vt_ref, bias_ref, out_ref, lse_ref):
    span, tokens = bias_ref.shape
    window = window_start(tokens, span, kt_ref.shape[1])
    keys = kt_ref[:, window].T
    values_t = vt_ref[:, window]
    for head in range(qt_ref.shape[0] // HEAD_SIZE):
        rows = slice(head * HEAD_SIZE, (head + 1) * HEAD_SIZE)
        scores = matmul(keys, qt_ref[rows, :]) + bias_ref[...]
        row_max = jnp.max(scores, 0, keepdims=True)
        exp_scores = jnp.exp(scores - row_max)
        row_total = jnp.sum(exp_scores, 0, keepdims=True)
        probs = (exp_scores * (1.0 / row_total)).astype(bf16)
        out_ref[rows, :] = matmul(values_t, probs)
        lse_ref[0, head : head + 1, :] = row_max + jnp.log(row_total)


def attn_bwd_body(qt_ref, kt_ref, vt_ref, dot_ref, lse_ref, bias_ref, dqt_ref, dkt_ref, dvt_ref):
    span, tokens = bias_ref.shape
    window = window_start(tokens, span, kt_ref.shape[1])
    keys_t = kt_ref[:, window]
    keys, values = keys_t.T, vt_ref[:, window].T
    dk = jnp.zeros(keys.shape, f32)
    dv = jnp.zeros(values.shape, f32)
    for head in range(qt_ref.shape[0] // HEAD_SIZE):
        rows = slice(head * HEAD_SIZE, (head + 1) * HEAD_SIZE)
        q_t, do_t = qt_ref[rows, :], dot_ref[rows, :]
        scores = matmul(keys, q_t) + bias_ref[...]
        probs = jnp.exp(scores - lse_ref[0, head : head + 1, :])
        d_probs = matmul(values, do_t)
        inner = jnp.sum(probs * d_probs, 0, keepdims=True)
        d_scores = (probs * (d_probs - inner)).astype(bf16)
        dqt_ref[rows, :] = (matmul(keys_t, d_scores) * (HEAD_SIZE**-0.5)).astype(bf16)
        dk = dk + matmul(d_scores, q_t.T)
        dv = dv + matmul(probs.astype(bf16), do_t.T)
    dkt_ref[...] = jnp.zeros_like(dkt_ref)
    dvt_ref[...] = jnp.zeros_like(dvt_ref)
    dkt_ref[:, window] = dk.T.astype(bf16)
    dvt_ref[:, window] = dv.T.astype(bf16)


def attn_specs(tokens, span, groups, length):
    heads = pl.BlockSpec((groups * HEAD_SIZE, tokens), lambda h: (h, 0))
    key = pl.BlockSpec((HEAD_SIZE, length), lambda h: (h, 0))
    value = pl.BlockSpec((HEAD_SIZE, length), lambda h: (KEY_VALUE_HEADS + h, 0))
    lse = pl.BlockSpec((1, 8, tokens), lambda h: (h, 0, 0))
    bias = pl.BlockSpec((span, tokens), lambda h: (0, 0))
    return heads, key, value, lse, bias


def attention_call(body, name, in_specs, out_specs, out_shape, arrays, moved, collective_id, cost):
    count = len(moved)
    params = comm_params(collective_id) if count else pltpu.CompilerParams(vmem_limit_bytes=48 << 20)
    return pl.pallas_call(
        with_exchange(body, count, len(in_specs), len(out_specs)),
        grid=(KEY_VALUE_HEADS,),
        in_specs=in_specs + [any_space] * count,
        out_specs=out_specs + [any_space] * count,
        out_shape=out_shape + [jax.ShapeDtypeStruct(x.shape, x.dtype) for x in moved],
        scratch_shapes=direct_scratch({"seq": 8}, ("seq",) * count) if count else [],
        compiler_params=params,
        cost_estimate=cost,
        name=name,
    )(*arrays, *moved)


def attention_forward(q_t, kv_t, bias, moved, collective_id):
    span, tokens = bias.shape
    heads, key, value, lse, bias_spec = attn_specs(tokens, span, QUERY_HEADS // KEY_VALUE_HEADS, kv_t.shape[1])
    return attention_call(
        attn_fwd_body,
        "attention_forward",
        [heads, key, value, bias_spec],
        [heads, lse],
        [
            jax.ShapeDtypeStruct(q_t.shape, f32),
            jax.ShapeDtypeStruct((KEY_VALUE_HEADS, 8, tokens), f32),
        ],
        (q_t, kv_t, kv_t, bias),
        moved,
        collective_id,
        pl.CostEstimate(
            flops=QUERY_HEADS * span * tokens * 512, bytes_accessed=8 << 20, transcendentals=QUERY_HEADS * span * tokens
        ),
    )


def attention_backward(q_t, kv_t, do_t, lse, bias, moved, collective_id):
    span, tokens = bias.shape
    heads, key, value, lse_spec, bias_spec = attn_specs(
        tokens, span, QUERY_HEADS // KEY_VALUE_HEADS, kv_t.shape[1]
    )
    grad = jax.ShapeDtypeStruct((KEY_VALUE_HEADS * HEAD_SIZE, kv_t.shape[1]), bf16)
    return attention_call(
        attn_bwd_body,
        "attention_backward",
        [heads, key, value, heads, lse_spec, bias_spec],
        [heads, key, key],
        [jax.ShapeDtypeStruct(q_t.shape, bf16), grad, grad],
        (q_t, kv_t, kv_t, do_t, lse, bias),
        moved,
        collective_id,
        pl.CostEstimate(
            flops=QUERY_HEADS * span * tokens * 1280, bytes_accessed=16 << 20, transcendentals=QUERY_HEADS * span * tokens
        ),
    )


def layer(
    n,
    m,
    tokens,
    doc_ids,
    in_weight,
    out_weight,
    gate_up,
    down_weight,
    select_weight,
    step_weight,
    first_gain,
    second_gain,
    attn_gain,
    mamba_gain,
    conv_weight,
    conv_bias,
    step_bias,
    decay_log,
    skip_gain,
    cotangent,
):
    fast = n == 8
    sizes = {"seq": n, "fsdp": m}
    me = lax.axis_index("seq")
    query_w = QUERY_HEADS * HEAD_SIZE
    key_w = KEY_VALUE_HEADS * HEAD_SIZE
    q_own, k_own, c_own, f_own = query_w // n, key_w // n, DI // n, F // n
    p_own = q_own + 2 * k_own + 2 * c_own
    kinds = (query_w, key_w, key_w, DI, DI)
    local, width = tokens.shape[1:]
    length = local * n
    z_rows = in_weight.shape[0]
    sel_rows = select_weight.shape[0]
    wide = p_own * n
    starts = (0, query_w, query_w + key_w, query_w + 2 * key_w, query_w + 2 * key_w + DI)
    widths = (q_own, k_own, k_own, c_own, c_own)
    highest = lax.Precision.HIGHEST

    small_w = jnp.concatenate([select_weight, step_weight], 0)
    if fast:
        deal_in, deal_small, deal_out = deal(p_own, (p_own,), n), deal(c_own, (c_own,), n), deal(out_weight.shape[0], (out_weight.shape[0],), n)
        in_blocks = exact(deal_in, in_weight, ((0,), (1,))).astype(bf16).reshape(n, p_own // n, z_rows)
        small_blocks = exact(deal_small, small_w, ((0,), (1,))).astype(bf16).reshape(n, c_own // n, -1)
        in_blocks, small_blocks, ids = direct(
            sizes,
            [(in_blocks, "seq", "exchange"), (small_blocks, "seq", "exchange"), (doc_ids.reshape(-1, 128), "seq", "gather")],
            0,
        )
        ids = ids.reshape(-1)
        in_cols = in_blocks.reshape(p_own, z_rows).T
        small_cols = small_blocks.reshape(c_own, -1).T
        seq_x = tokens[0].astype(f32)
        normed_one, scale_one = rms_norm(seq_x, first_gain)
        normed_one = seq_gather(n, normed_one.astype(bf16), 3, (in_blocks,))
        gu_blocks = gate_up.T.reshape(n, -1, z_rows)
        out_blocks = exact(deal_out, out_weight, ((0,), (0,))).astype(bf16).reshape(n, -1, out_weight.shape[1])
        down_blocks = down_weight.reshape(n, -1, down_weight.shape[1])
        out_blocks, down_blocks, small_full = direct(
            sizes,
            [(x, "seq", "exchange") for x in (out_blocks, down_blocks)] + [(small_cols, "fsdp", "gather")],
            1,
            (normed_one,),
        )
        out_rows = out_blocks.transpose(1, 0, 2).reshape(-1, width)
        down_rows = down_blocks.transpose(1, 0, 2).reshape(-1, width)
        in_full = lax.all_gather(in_cols, "fsdp", axis=0, tiled=True)
        in_full, out_rows, down_rows = lax.optimization_barrier((in_full, out_rows, down_rows))
        out_full = lax.all_gather(out_rows, "fsdp", axis=0, tiled=True)
        down_full = lax.all_gather(down_rows, "fsdp", axis=0, tiled=True)
    else:
        seq_x = tokens[0].astype(f32)
        normed_one, scale_one = rms_norm(seq_x, first_gain)
        normed_one = seq_gather(n, normed_one.astype(bf16), 3)
        ids = lax.all_gather(doc_ids[0], "seq", axis=0, tiled=True)
        in_cols = lax.all_gather(in_weight, "seq", axis=1, tiled=True)
        in_cols = jnp.concatenate(
            [lax.dynamic_slice_in_dim(in_cols, s + me * w, w, 1) for s, w in zip(starts, widths)], 1
        )
        small_full = lax.all_gather(small_w, "fsdp", axis=0, tiled=False)
        half = n // 2
        route_a = [(d, 2 * d if d < half else 2 * (d - half) + 1) for d in range(n)]
        route_b = [(d, 2 * d + 1 if d < half else 2 * (d - half)) for d in range(n)]
        low_half = me < half
        even = me % 2 == 0
        piece0, piece1 = gate_up[:, :f_own], gate_up[:, f_own:]
        got_a = lax.ppermute(jnp.where(low_half, piece0, piece1), "seq", route_a)
        got_b = lax.ppermute(jnp.where(low_half, piece1, piece0), "seq", route_b)
        gu_cols = jnp.concatenate([jnp.where(even, got_a, got_b), jnp.where(even, got_b, got_a)], 1)
        out_rows = lax.all_gather(out_weight, "fsdp", axis=0, tiled=True)
        out_rows = jnp.concatenate(
            [out_rows[:query_w].reshape(n, q_own, -1), out_rows[query_w:].reshape(n, c_own, -1)], 1
        )
        out_full = exchange(n, out_rows, None).transpose(1, 0, 2).reshape(q_own + c_own, -1)
        down_rows = lax.all_gather(down_weight, "fsdp", axis=0, tiled=True).reshape(n, f_own, -1)
        down_full = exchange(n, down_rows, None).transpose(1, 0, 2).reshape(f_own, -1)
        in_full = lax.all_gather(in_cols, "fsdp", axis=0, tiled=True)
        gu_full = lax.all_gather(gu_cols, "fsdp", axis=0, tiled=True)
    select_own = small_full[:, :sel_rows].reshape(-1, c_own)
    step_own = small_full[:, sel_rows:].reshape(-1, c_own)

    params = jnp.concatenate(
        [mamba_gain[None], conv_weight, conv_bias[None], step_bias[None], decay_log, skip_gain[None]], 0
    )
    if fast:
        params = params.reshape(-1, c_own)
        params = exact(params, deal(c_own, (c_own,), n), ((1,), (0,)), highest).reshape(-1, n, n, c_own // n)
        params = lax.dynamic_index_in_dim(params, me, 2, False).reshape(-1, c_own)
    else:
        params = lax.dynamic_slice_in_dim(params, me * c_own, c_own, 1)
    mamba_g, conv_w, conv_b, step_b = params[0], params[1 : 1 + KC], params[1 + KC], params[2 + KC]
    decay_l, skip_g = params[3 + KC : 3 + KC + NS], params[3 + KC + NS]

    def heads_in(blocks):
        blocks = blocks.reshape(query_w, local)
        return exact(deal(query_w, (query_w,), n), blocks, ((1,), (0,))).astype(bf16) if fast else blocks

    def heads_out(value):
        if fast:
            value = exact(deal(query_w, (query_w,), n), value, ((0,), (0,))).astype(bf16)
        return value.reshape(n, q_own, local)

    normed_one = normed_one.reshape(length, width)
    qkv_w = q_own + 2 * k_own
    qkv_t = exact(in_full[:, :qkv_w], normed_one, ((0,), (1,))).astype(bf16)
    branch = matmul(normed_one, in_full[:, qkv_w:]).astype(bf16)
    inputs = branch[:, :c_own].astype(f32)
    gate_z = branch[:, c_own:].astype(f32)

    q_blocks = qkv_t[:q_own].reshape(q_own, n, local).transpose(1, 0, 2)
    q_t = heads_in(exchange(n, q_blocks, 4)) * bf16(HEAD_SIZE**-0.5)
    kv_all = seq_gather(n, qkv_t[q_own:], 5)
    reach = (WINDOW_TOKENS + local - 2) // local
    span = min((reach + 1) * local, length)
    first_key = jnp.clip((me - reach) * local, 0, length - span)
    nat = jnp.arange(2 * key_w, dtype=jnp.int32)
    inside = nat % key_w
    block_order = inside // k_own * 2 * k_own + nat // key_w * k_own + inside % k_own
    deal_kv = (
        deal(2 * key_w, (key_w, key_w), n) if fast else (block_order[:, None] == nat[None, :]).astype(bf16)
    )
    kv_t = exact(deal_kv, kv_all.reshape(2 * key_w, length), ((1,), (0,))).astype(bf16)
    query_pos = me * local + jnp.arange(local, dtype=jnp.int32)
    key_pos = first_key + jnp.arange(span, dtype=jnp.int32)
    offset = query_pos[None, :] - key_pos[:, None]
    key_ids = lax.dynamic_slice_in_dim(ids, first_key, span, 0)
    allowed = (offset >= 0) & (offset < WINDOW_TOKENS) & (doc_ids[0][None, :] == key_ids[:, None])
    bias = jnp.where(allowed, 0.0, masked_score).astype(f32)
    attended, lse, *moved = attention_forward(q_t, kv_t, bias, [gu_blocks] if fast else [], 23)
    if fast:
        gu_full = lax.all_gather(moved[0].reshape(-1, z_rows).T, "fsdp", axis=0, tiled=True)
    attn_scale = lax.rsqrt(jnp.mean(attended * attended, axis=0, keepdims=True) + norm_eps)
    attn_normed = (attended * attn_scale * attn_gain[:, None]).astype(bf16)
    attn_c = exchange(n, heads_out(attn_normed), 6).transpose(0, 2, 1).reshape(length, q_own)

    padded_inputs = jnp.pad(inputs, ((KC - 1, 0), (0, 0)))
    padded_ids = jnp.pad(ids, (KC - 1, 0), constant_values=-1)
    conv_sum = conv_b + jnp.zeros_like(inputs)
    same_masks = []
    for tap in range(KC):
        begin = KC - 1 - tap
        same = (padded_ids[begin : begin + length] == ids).astype(f32)[:, None]
        same_masks.append(same)
        conv_sum = conv_sum + conv_w[tap] * padded_inputs[begin : begin + length] * same
    activated_b = jax.nn.silu(conv_sum).astype(bf16)
    activated = activated_b.astype(f32)
    sel_pad = jnp.pad(select_own, ((0, (-select_own.shape[0]) % 8), (0, 0)))
    selected = seq_sum(n, dot_nt(sel_pad, activated_b), 7)
    step_raw = selected[:DTR].astype(bf16)
    b_t = selected[DTR : DTR + NS]
    c_t = selected[DTR + NS : DTR + 2 * NS]
    step_pre = dot_tn(step_raw, step_own) + step_b
    step_size = jax.nn.softplus(step_pre)
    rate = -jnp.exp(decay_l)
    changed = jnp.concatenate([jnp.zeros((1,), f32), (ids[1:] != ids[:-1]).astype(f32)])
    step_keep = step_size + 1e30 * changed[:, None]
    push = step_size * activated
    scan_out, states = scan_forward(step_keep, push, b_t, c_t, rate)
    mamba_pre = scan_out + skip_g * activated
    gate_sig = jax.nn.sigmoid(gate_z)
    mamba_out = mamba_pre * gate_z * gate_sig
    square_sum = seq_token_sum(n, jnp.sum(mamba_out * mamba_out, -1), 8)
    mamba_scale = lax.rsqrt(square_sum / DI + norm_eps)[:, None]
    mamba_normed = mamba_out * mamba_scale * mamba_g
    joined = jnp.concatenate([attn_c, mamba_normed.astype(bf16)], 1)
    mixed = product_scatter(n, joined, out_full, False, 9)
    hidden = seq_x + 0.5 * mixed
    normed_two, scale_two = rms_norm(hidden, second_gain)
    normed_two = seq_gather(n, normed_two.astype(bf16), 10).reshape(length, width)
    gate_up_out = matmul(normed_two, gu_full).astype(bf16)
    gate_part = gate_up_out[:, :f_own].astype(f32)
    up_part = gate_up_out[:, f_own:].astype(f32)
    gate_act = jax.nn.sigmoid(gate_part)
    inner = (gate_part * gate_act * up_part).astype(bf16)
    ffn = matmul(inner, down_full).astype(bf16)

    own_d_out = cotangent[0] if fast else lax.optimization_barrier((cotangent[0], inner))[0]
    d_ffn = lax.all_gather(own_d_out, "seq", axis=0, tiled=True)
    down_term = dot_tn(inner, d_ffn).astype(bf16)
    d_inner = dot_nt(d_ffn, down_full)
    d_gate_up = jnp.concatenate(
        [
            d_inner * up_part * gate_act * (1.0 + gate_part * (1.0 - gate_act)),
            d_inner * gate_part * gate_act,
        ],
        1,
    ).astype(bf16)
    gate_up_term = dot_tn(normed_two, d_gate_up).astype(bf16)
    gu_part = lax.psum_scatter(gate_up_term, "fsdp", scatter_dimension=0, tiled=True)
    if fast:
        down_part = lax.psum_scatter(down_term.reshape(m, -1, width), "fsdp", scatter_dimension=0, tiled=False)
    d_normed_two = product_scatter(n, d_gate_up, gu_full, True, 13, (down_term, gate_up_term))
    d_hidden_part, second_grad = norm_back(hidden, scale_two, second_gain, d_normed_two)
    d_hidden = cotangent[0].astype(f32) + d_hidden_part
    d_mixed = seq_gather(n, d_hidden.astype(bf16), 14, (down_part,) if fast else ()).reshape(length, width)
    out_term = (0.5 * dot_tn(joined, d_mixed)).astype(bf16)
    if fast:
        out_part = lax.psum_scatter(out_term.reshape(m, -1, width), "fsdp", scatter_dimension=0, tiled=False)
    d_joined = 0.5 * dot_nt(d_mixed, out_full)

    u = d_joined[:, q_own:]
    weighted = u * mamba_g
    inner_mean = seq_token_sum(n, jnp.sum(weighted * mamba_out, -1), 18)[:, None] / DI
    mamba_grad = jnp.sum(u * mamba_out * mamba_scale, 0)
    d_mamba = mamba_scale * weighted - mamba_out * (mamba_scale * mamba_scale * mamba_scale) * inner_mean
    d_pre = d_mamba * gate_z * gate_sig
    d_gate = d_mamba * mamba_pre * gate_sig * (1.0 + gate_z * (1.0 - gate_sig))
    skip_grad = jnp.sum(d_pre * activated, 0)
    by_rate, pushed, db_t, dc_t, decay_log_grad = scan_backward(
        step_keep, push, d_pre, b_t, c_t, states, rate, (out_part,) if fast else ()
    )
    ffn, db_t = lax.optimization_barrier((ffn, db_t))
    ffn = lax.psum_scatter(ffn, "seq", scatter_dimension=0, tiled=True)
    out_tokens = (hidden + ffn.astype(f32)).astype(bf16)

    d_attn = d_joined[:, :q_own].astype(bf16).reshape(n, local, q_own).transpose(0, 2, 1)
    d_attn = heads_in(exchange(n, d_attn, 15, (gu_part,))).astype(f32)
    weighted_a = d_attn * attn_gain[:, None]
    attn_grad = jnp.sum(d_attn * attended * attn_scale, 1)
    mean_a = jnp.mean(weighted_a * attended, axis=0, keepdims=True)
    d_attended = attn_scale * weighted_a - attended * (attn_scale * attn_scale * attn_scale) * mean_a
    moved = []
    if fast:
        out_blocks = out_part.reshape(-1, n, width // n).transpose(1, 0, 2)
        down_blocks = down_part.reshape(-1, n, width // n).transpose(1, 0, 2)
        gu_blocks = gu_part.T.reshape(n, -1, z_rows)
        moved = [gu_blocks, out_blocks, down_blocks]
    dq_t, dk_t, dv_t, *moved = attention_backward(
        q_t, kv_t, d_attended.astype(bf16), lse, bias, moved, 24
    )
    d_queries = exchange(n, heads_out(dq_t), 16, (out_tokens,)).transpose(0, 2, 1).reshape(length, q_own)
    dkv = exact(deal_kv, jnp.concatenate([dk_t, dv_t], 0), ((0,), (0,))).astype(bf16).reshape(n, 2 * k_own, length)
    dkv = seq_scatter(n, dkv, 17).astype(bf16).T

    step_grads = by_rate + pushed * activated
    d_step_pre = step_grads * jax.nn.sigmoid(step_pre)
    step_bias_grad = jnp.sum(d_step_pre, 0)
    d_step_low = d_step_pre.astype(bf16)
    step_term = matmul(step_raw, d_step_low)
    d_selected = jnp.concatenate(
        [dot_nt(step_own, d_step_low), db_t, dc_t, jnp.zeros(((-DTR - 2 * NS) % 8, length), f32)], 0
    )
    d_selected = seq_sum(n, d_selected, 19)[: DTR + 2 * NS].astype(bf16)
    select_term = matmul(d_selected, activated_b)
    d_activated = d_pre * skip_g + pushed * step_size + dot_tn(d_selected, select_own)
    conv_sig = jax.nn.sigmoid(conv_sum)
    d_conv = d_activated * conv_sig * (1.0 + conv_sum * (1.0 - conv_sig))
    conv_bias_grad = jnp.sum(d_conv, 0)
    ext_grad = jnp.zeros((length + KC - 1, c_own), f32)
    conv_rows = []
    for tap in range(KC):
        begin = KC - 1 - tap
        masked_grad = d_conv * same_masks[tap]
        conv_rows.append(jnp.sum(masked_grad * padded_inputs[begin : begin + length], 0))
        ext_grad = ext_grad + jnp.pad(conv_w[tap] * masked_grad, ((begin, tap), (0, 0)))
    d_inputs = ext_grad[KC - 1 :]
    d_projected = jnp.concatenate([d_queries, dkv, d_inputs.astype(bf16), d_gate.astype(bf16)], 1)
    in_term = dot_tn(normed_one, d_projected).astype(bf16)
    d_normed_one = product_scatter(n, d_projected, in_full, True, 20, (in_term,))
    d_x_part, first_grad = norm_back(seq_x, scale_one, first_gain, d_normed_one)
    tokens_grad = (d_hidden + d_x_part).astype(bf16)

    in_part = lax.psum_scatter(in_term, "fsdp", scatter_dimension=0, tiled=True)
    small_term = jnp.concatenate(
        [select_term.reshape(m, sel_rows, c_own), step_term.reshape(m, -1, c_own)], 1
    ).astype(bf16)
    channel = jnp.concatenate(
        [
            mamba_grad[None], jnp.stack(conv_rows), conv_bias_grad[None], step_bias_grad[None],
            decay_log_grad, skip_grad[None],
        ],
        0,
    )
    wide_grads = jnp.stack([first_grad, second_grad, attn_grad])
    small_specs = [(small_term, "fsdp", "exchange"), (channel, "fsdp", "gather"), (wide_grads, "fsdp", "gather")]
    if fast:
        gu_blocks, out_blocks, down_blocks = moved
    small_z, channel_z, wide_z = direct(sizes, small_specs, 21)
    small_part = jnp.sum(small_z.astype(f32), 0)
    channel, wide_grads = jnp.sum(channel_z, 0), jnp.sum(wide_z, 0)
    if fast:
        gu_sum = gu_blocks.reshape(-1, z_rows).T.astype(f32)
        out_sum = exact(deal_out, out_blocks.reshape(-1, width // n), ((1,), (0,)))
        down_sum = down_blocks.reshape(-1, width // n).astype(f32)
        small_blocks = small_part.astype(bf16).T.reshape(n, c_own // n, -1)
        in_blocks, small_blocks, channel_all, wide_all = direct(
            sizes,
            [
                (in_part.T.reshape(n, -1, z_rows), "seq", "exchange"), (small_blocks, "seq", "exchange"),
                (channel, "seq", "gather"), (wide_grads, "seq", "gather"),
            ],
            22,
        )
        small_sum = exact(small_blocks.reshape(c_own, -1), deal_small, ((0,), (1,)))
        channel_rows = channel.shape[0]
        channel = channel_all.reshape(n, channel_rows, n, c_own // n).transpose(1, 2, 0, 3).reshape(-1, c_own)
        channel = exact(channel, deal_small, ((1,), (1,)), highest).reshape(channel_rows, DI)
        wide_grads = jnp.sum(wide_all, 0)
        in_sum = exact(in_blocks.reshape(p_own, z_rows), deal_in, ((0,), (1,)))
    else:
        out_blocks = exchange(n, out_term.reshape(q_own + c_own, n, -1).transpose(1, 0, 2), None)
        out_sum = jnp.concatenate(
            [out_blocks[:, :q_own].reshape(query_w, -1), out_blocks[:, q_own:].reshape(DI, -1)], 0
        )
        out_sum = lax.psum_scatter(out_sum, "fsdp", scatter_dimension=0, tiled=True).astype(f32)
        down_sum = exchange(n, down_term.reshape(f_own, n, -1).transpose(1, 0, 2), None).reshape(F, -1)
        down_sum = lax.psum_scatter(down_sum, "fsdp", scatter_dimension=0, tiled=True).astype(f32)
        gate_g, up_g = gu_part[:, :f_own], gu_part[:, f_own:]
        back_a = lax.ppermute(jnp.where(even, gate_g, up_g), "seq", [(t, s) for s, t in route_a])
        back_b = lax.ppermute(jnp.where(even, up_g, gate_g), "seq", [(t, s) for s, t in route_b])
        gu_sum = jnp.concatenate(
            [jnp.where(low_half, back_a, back_b), jnp.where(low_half, back_b, back_a)], 1
        ).astype(f32)
        in_sum = jnp.zeros((z_rows, wide), bf16)
        at = 0
        for s, w in zip(starts, widths):
            in_sum = lax.dynamic_update_slice_in_dim(in_sum, in_part[:, at : at + w], s + me * w, 1)
            at += w
        in_sum = lax.psum_scatter(in_sum, "seq", scatter_dimension=1, tiled=True).astype(f32)
        small_sum = small_part
        channel = lax.all_gather(channel, "seq", axis=1, tiled=True)
        wide_grads = lax.psum(wide_grads, "seq")
    return (
        out_tokens[None],
        tokens_grad[None],
        in_sum,
        out_sum,
        gu_sum,
        down_sum,
        small_sum[:sel_rows],
        small_sum[sel_rows:],
        wide_grads[0],
        wide_grads[1],
        wide_grads[2],
        channel[0],
        channel[1 : 1 + KC],
        channel[1 + KC],
        channel[2 + KC],
        channel[3 + KC : 3 + KC + NS],
        channel[3 + KC + NS],
    )


def solution(mesh):
    split = P("fsdp", "seq")
    seq3 = P("fsdp", "seq", None)
    return jax.shard_map(
        functools.partial(layer, mesh.shape["seq"], mesh.shape["fsdp"]),
        mesh=mesh,
        in_specs=(seq3,) + (split,) * 7 + (P(),) * 9 + (seq3,),
        out_specs=(seq3, seq3) + (split,) * 6 + (P(),) * 9,
        check_vma=False,
    )
```

```python
import functools
import math

import jax
import jax.numpy as jnp
from jax import lax
from jax.experimental import pallas as pl
from jax.experimental.pallas import tpu as pltpu
from jax.sharding import PartitionSpec as P

QUERY_HEADS = 25
KEY_VALUE_HEADS = 5
HEAD_SIZE = 64
DI = 3200
NS = 16
DTR = 100
KC = 4
F = 5504
WINDOW_TOKENS = 1024

norm_eps = 1e-05
masked_score = -1e30
log2e = 1.4426950408889634
bf16 = jnp.bfloat16
f32 = jnp.float32
MESH = pl.DeviceIdType.MESH


def matmul(left, right):
    return jnp.dot(left, right, preferred_element_type=f32)


def dot_tn(left, right):
    return lax.dot_general(left, right, (((0,), (0,)), ((), ())), preferred_element_type=f32)


def dot_nt(left, right):
    return lax.dot_general(left, right, (((1,), (1,)), ((), ())), preferred_element_type=f32)


def rms_norm(value, gain):
    scale = lax.rsqrt(jnp.mean(value * value, axis=-1, keepdims=True) + norm_eps)
    return (value * scale * gain, scale)


def norm_back(value, scale, gain, upstream):
    weighted = upstream * gain
    gain_grad = jnp.sum(upstream * value * scale, 0)
    inner_mean = jnp.mean(weighted * value, axis=-1, keepdims=True)
    return (scale * weighted - value * (scale * scale * scale) * inner_mean, gain_grad)


def park(part, j, value):
    for k, lane in enumerate(range(0, value.shape[1], 128)):
        end = min(lane + 128, value.shape[1])
        part[64 * k + 8 * j : 64 * k + 8 * j + 8, : end - lane] = value[:, lane:end]


def fold(part, out, t0):
    for k, lane in enumerate(range(0, out.shape[1], 128)):
        end = min(lane + 128, out.shape[1])
        total = part[pl.ds(64 * k, 8, stride=8), :]
        for s in range(1, 8):
            total = total + part[pl.ds(64 * k + s, 8, stride=8), :]
        out[pl.ds(t0, 8), lane:end] = total[:, : end - lane]


def spread(split_ref, eye_ref, out_scr):
    eye = eye_ref[...]
    ones = jnp.ones((2 * NS, 128), bf16)
    for first in range(0, split_ref.shape[0], 16):
        split = split_ref[first : first + 16, :]
        spaced = jnp.concatenate([split[j : j + 1, :] * eye for j in range(16)], 0).astype(bf16)
        out_scr[first * NS : (first + 16) * NS, :] = matmul(spaced, ones)


def widen(value, width):
    return jnp.concatenate([value] * (width // 128) + ([value[:, : width % 128]] if width % 128 else []), 1)


def scan_fwd_body(
    step_ref, push_ref, b_ref, c_ref, rate_ref, eye_ref, y_ref, st_ref, h_scr, part_scr, b_scr, c_scr
):
    block = step_ref.shape[0]

    @pl.when(pl.program_id(0) == 0)
    def _():
        h_scr[...] = jnp.zeros_like(h_scr)

    spread(b_ref, eye_ref, b_scr)
    spread(c_ref, eye_ref, c_scr)
    rate = rate_ref[...]
    width = rate.shape[1]

    def group(index, state):
        t0 = pl.multiple_of(index * 8, 8)
        step8 = step_ref[pl.ds(t0, 8), :]
        push8 = push_ref[pl.ds(t0, 8), :]
        for j in range(8):
            at = pl.ds(pl.multiple_of((t0 + j) * NS, NS), NS)
            decay = jnp.exp(step8[j : j + 1, :] * rate)
            state = decay * state + push8[j : j + 1, :] * widen(b_scr[at, :], width)
            st_ref[t0 + j] = state.astype(bf16)
            out = widen(c_scr[at, :], width) * state
            park(part_scr, j, out[:8] + out[8:])
        fold(part_scr, y_ref, t0)
        return state

    h_scr[...] = lax.fori_loop(0, block // 8, group, h_scr[...])


def scan_bwd_body(
    step_ref, push_ref, dpre_ref, b_ref, c_ref, st_ref, prev_ref, rate_ref, eye_ref, *refs
):
    pr_ref, pushed_ref, db_ref, dc_ref, log_ref = refs[-12:-7]
    g_scr, log_scr, part1, part2, b_scr, c_scr, grad_scr = refs[-7:]
    block = step_ref.shape[0]
    count = pl.num_programs(0)
    which = pl.program_id(0)

    @pl.when(which == 0)
    def _():
        g_scr[...] = jnp.zeros_like(g_scr)
        log_scr[...] = jnp.zeros_like(log_scr)

    spread(b_ref, eye_ref, b_scr)
    spread(c_ref, eye_ref, c_scr)
    width = rate_ref.shape[1]
    before = prev_ref[0].astype(f32) * jnp.where(which == count - 1, 0.0, 1.0)

    def group(turn, grad_in):
        t0 = pl.multiple_of((block // 8 - 1 - turn) * 8, 8)
        step8 = step_ref[pl.ds(t0, 8), :]
        dpre8 = dpre_ref[pl.ds(t0, 8), :]
        rate = rate_ref[...]
        log_acc = log_scr[...]
        for j in range(7, -1, -1):
            at = pl.ds(pl.multiple_of((t0 + j) * NS, NS), NS)
            if j > 0:
                prior = st_ref[t0 + (j - 1)].astype(f32)
            else:
                prior = jnp.where(t0 > 0, st_ref[jnp.maximum(t0 - 1, 0)].astype(f32), before)
            step_row = step8[j : j + 1, :]
            grad = widen(c_scr[at, :], width) * dpre8[j : j + 1, :] + grad_in
            grad_scr[at, :] = grad.astype(bf16)
            grad_in = grad * jnp.exp(step_row * rate)
            flow = grad_in * prior
            by_rate = flow * rate
            park(part1, j, by_rate[:8] + by_rate[8:])
            by_b = grad * widen(b_scr[at, :], width)
            park(part2, j, by_b[:8] + by_b[8:])
            log_acc = log_acc + flow * step_row
        log_scr[...] = log_acc
        fold(part1, pr_ref, t0)
        fold(part2, pushed_ref, t0)
        return grad_in

    g_scr[...] = lax.fori_loop(0, block // 8, group, g_scr[...])

    lanes = lax.broadcasted_iota(jnp.int32, (NS, block), 1)

    def own_token(left, right_ref, out_ref):
        right = right_ref[...].astype(bf16)

        totals = []
        for i in range(block // 16):
            pairs = dot_nt(left(i), right)
            total = pairs[:NS]
            for j in range(1, 16):
                total = jnp.where(lanes == i * 16 + j, pairs[j * NS : (j + 1) * NS], total)
            totals.append(total)
        total = totals[0]
        for i in range(1, block // 16):
            total = jnp.where(lanes >= i * 16, totals[i], total)
        out_ref[...] = total

    own_token(lambda i: grad_scr[i * 16 * NS : (i + 1) * 16 * NS, :], push_ref, db_ref)
    own_token(lambda i: st_ref[i * 16 : (i + 1) * 16].reshape(16 * NS, width), dpre_ref, dc_ref)

    @pl.when(which == count - 1)
    def _():
        log_ref[...] = log_scr[...] * rate_ref[...]


SCAN_BLOCK = 128


def split_halves(value):
    high = lax.reduce_precision(value, 8, 7)
    low = lax.reduce_precision(value - high, 8, 7)
    return jnp.concatenate([high, low], 0).T


def scan_forward(step_keep, push, b_t, c_t, rate):
    tokens, width = step_keep.shape
    block = SCAN_BLOCK
    padded = (width + 127) // 128 * 128
    rows = pl.BlockSpec((block, width), lambda i: (i, 0))
    halves_spec = pl.BlockSpec((block, 2 * NS), lambda i: (i, 0))
    fixed = pl.BlockSpec((NS, width), lambda i: (0, 0))
    eye = jnp.concatenate([jnp.eye(NS, dtype=f32)] * 2, 1)
    return pl.pallas_call(
        scan_fwd_body,
        grid=(tokens // block,),
        in_specs=[rows, rows, halves_spec, halves_spec, fixed, pl.BlockSpec(eye.shape, lambda i: (0, 0))],
        out_specs=[rows, pl.BlockSpec((block, NS, width), lambda i: (i, 0, 0))],
        out_shape=[
            jax.ShapeDtypeStruct((tokens, width), f32),
            jax.ShapeDtypeStruct((tokens, NS, width), bf16),
        ],
        scratch_shapes=[
            pltpu.VMEM((NS, width), f32),
            pltpu.VMEM((padded // 2, 128), f32),
            pltpu.VMEM((block * NS, 128), f32),
            pltpu.VMEM((block * NS, 128), f32),
        ],
        compiler_params=pltpu.CompilerParams(vmem_limit_bytes=40 << 20),
        cost_estimate=pl.CostEstimate(
            flops=tokens * width * NS * 8, bytes_accessed=tokens * width * NS * 4, transcendentals=tokens * width * NS
        ),
        name="scan_forward",
    )(step_keep, push, split_halves(b_t), split_halves(c_t), rate, eye)


def scan_backward(step_keep, push, d_pre, b_t, c_t, states, rate, after=()):
    tokens, width = step_keep.shape
    block = SCAN_BLOCK
    padded = (width + 127) // 128 * 128
    last = tokens // block - 1
    rows = pl.BlockSpec((block, width), lambda i: (last - i, 0))
    cols = pl.BlockSpec((NS, block), lambda i: (0, last - i))
    halves_spec = pl.BlockSpec((block, 2 * NS), lambda i: (last - i, 0))
    fixed = pl.BlockSpec((NS, width), lambda i: (0, 0))
    eye = jnp.concatenate([jnp.eye(NS, dtype=f32)] * 2, 1)
    return pl.pallas_call(
        scan_bwd_body,
        grid=(tokens // block,),
        in_specs=[
            rows, rows, rows, halves_spec, halves_spec,
            pl.BlockSpec((block, NS, width), lambda i: (last - i, 0, 0)),
            pl.BlockSpec((1, NS, width), lambda i: (jnp.maximum((last - i) * block - 1, 0), 0, 0)),
            fixed, pl.BlockSpec(eye.shape, lambda i: (0, 0)),
        ] + [pl.BlockSpec(memory_space=pl.ANY)] * len(after),
        out_specs=[rows, rows, cols, cols, fixed],
        out_shape=[
            jax.ShapeDtypeStruct((tokens, width), f32),
            jax.ShapeDtypeStruct((tokens, width), f32),
            jax.ShapeDtypeStruct((NS, tokens), f32),
            jax.ShapeDtypeStruct((NS, tokens), f32),
            jax.ShapeDtypeStruct((NS, width), f32),
        ],
        scratch_shapes=[
            pltpu.VMEM((NS, width), f32),
            pltpu.VMEM((NS, width), f32),
            pltpu.VMEM((padded // 2, 128), f32),
            pltpu.VMEM((padded // 2, 128), f32),
            pltpu.VMEM((block * NS, 128), f32),
            pltpu.VMEM((block * NS, 128), f32),
            pltpu.VMEM((block * NS, width), bf16),
        ],
        compiler_params=pltpu.CompilerParams(vmem_limit_bytes=40 << 20),
        cost_estimate=pl.CostEstimate(
            flops=tokens * width * NS * 18, bytes_accessed=tokens * width * NS * 4, transcendentals=tokens * width * NS
        ),
        name="scan_backward",
    )(step_keep, push, d_pre, split_halves(b_t), split_halves(c_t), states, states, rate, eye, *after)


def places():
    me = lax.axis_index("seq")
    core, x, y = me % 2, (me // 2) % 2, me // 4
    sibling = me + 1 - 2 * core
    return me, core, sibling, 2 - 4 * x, 4 - 8 * y


def remote(src, dst, sems, k, to, axis="seq"):
    return pltpu.make_async_remote_copy(
        src_ref=src,
        dst_ref=dst,
        send_sem=sems.at[0, k],
        recv_sem=sems.at[1, k],
        device_id={axis: to},
        device_id_type=MESH,
    )


def greet(devices, axis="seq"):
    barrier = pltpu.get_barrier_semaphore()
    for d in devices:
        pl.semaphore_signal(barrier, inc=1, device_id={axis: d}, device_id_type=MESH)
    pl.semaphore_wait(barrier, len(devices))


def block_at(ref, d):
    if len(ref.shape) == 3:
        return ref.at[d]
    width = ref.shape[1] // 8
    return ref.at[:, pl.ds(pl.multiple_of(d * width, width), width)]


def halves(ref, tile):
    rows = ref.shape[0]
    top = (rows // 2 + tile - 1) // tile * tile
    return ref.at[pl.ds(0, top)], ref.at[pl.ds(top, rows - top)]


def gather_steps(out, sems, base, tile, early=None, late=None, use=None):
    me, core, sib, step_x, step_y = places()
    at_x, at_y = me + step_x, me + step_y
    diag = me + step_x + step_y

    def send(block, k, to):
        copy = remote(block, block, sems, base + k, to)
        copy.start()
        return copy

    mine, from_x, from_y, far = (block_at(out, d) for d in (me, at_x, at_y, diag))
    own_x, own_y, own_s = send(mine, 0, at_x), send(mine, 1, at_y), send(mine, 2, sib)
    if early is not None:
        early()
    if use is not None:
        use(me)
        own_s.wait_recv()
        use(sib)
    own_x.wait_recv()
    on_y = send(halves(from_x, tile)[0], 3, at_y)
    pass_x = send(from_x, 5, sib)
    own_y.wait_recv()
    on_x = send(halves(from_y, tile)[1], 4, at_x)
    pass_y = send(from_y, 6, sib)
    if late is not None:
        late()
    if use is not None:
        use(at_x)
        use(at_y)
        pass_x.wait_recv()
        use(sib + step_x)
        pass_y.wait_recv()
        use(sib + step_y)
    on_y.wait_recv()
    pass_top = send(halves(far, tile)[0], 7, sib)
    on_x.wait_recv()
    pass_low = send(halves(far, tile)[1], 8, sib)
    if use is None:
        for copy in (own_s, pass_x, pass_y, pass_top, pass_low):
            copy.wait_recv()
    else:
        use(diag)
        pass_top.wait_recv()
        pass_low.wait_recv()
        use(sib + step_x + step_y)
    for copy in (own_s, pass_x, pass_y, pass_top, pass_low, own_x, own_y, on_x, on_y):
        copy.wait_send()


def gather_body(x_ref, *refs):
    out_ref, sems, local_sem = refs[-3:]
    me, core, sib, step_x, step_y = places()
    mine = pltpu.make_async_copy(x_ref, out_ref.at[me], local_sem)
    mine.start()
    greet([sib, me + step_x, me + step_y])
    mine.wait()
    gather_steps(out_ref, sems, 0, 16)


def gather_product_body(x_ref, w_ref, out_ref, y_ref, sems, local_sem):
    me, core, sib, step_x, step_y = places()
    rows, width = x_ref.shape[0], w_ref.shape[1]
    mine = pltpu.make_async_copy(x_ref, out_ref.at[me], local_sem)
    mine.start()
    greet([sib, me + step_x, me + step_y])
    mine.wait()

    def use(d):
        left = out_ref[d]
        at = pl.ds(pl.multiple_of(d * rows, rows), rows)
        for first in range(0, width, 512):
            cols = slice(first, min(first + 512, width))
            y_ref[at, cols] = matmul(left, w_ref[:, cols]).astype(bf16)

    gather_steps(out_ref, sems, 0, 16, use=use)


def column_products(out_ref, a_ref, b_ref):
    count = a_ref.shape[1]

    def step(i, _):
        at = pl.ds(pl.multiple_of(i * 256, 256), 256)
        out_ref[at, :] = dot_tn(a_ref[:, at], b_ref[...]).astype(bf16)
        return 0

    lax.fori_loop(0, count // 256, step, 0)
    if count % 256:
        at = pl.ds(count // 256 * 256, count % 256)
        out_ref[at, :] = dot_tn(a_ref[:, at], b_ref[...]).astype(bf16)


def gather_beside_body(x_ref, a1_ref, b1_ref, a2_ref, b2_ref, out_ref, p1_ref, p2_ref, *refs):
    a1, b1, a2, b2, sems, local_sems = refs
    me, core, sib, step_x, step_y = places()
    mine = pltpu.make_async_copy(x_ref, out_ref.at[me], local_sems.at[4])
    mine.start()
    pairs = ((a1_ref, a1), (b1_ref, b1), (a2_ref, a2), (b2_ref, b2))
    loads = [pltpu.make_async_copy(src, dst, local_sems.at[k]) for k, (src, dst) in enumerate(pairs)]
    greet([sib, me + step_x, me + step_y])
    mine.wait()

    def early():
        for load in loads:
            load.start()
        loads[0].wait()
        loads[1].wait()
        column_products(p1_ref, a1, b1)

    def late():
        loads[2].wait()
        loads[3].wait()
        column_products(p2_ref, a2, b2)

    gather_steps(out_ref, sems, 0, 16, early, late)


def add_rows(out, parts, rows):
    def step(i, _):
        at = pl.ds(pl.multiple_of(i * rows, rows), rows)
        total = parts[0][at, :].astype(f32)
        for p in parts[1:]:
            total = total + p[at, :].astype(f32)
        out[at, :] = total.astype(out.dtype)
        return 0

    lax.fori_loop(0, out.shape[0] // rows, step, 0)


def scatter_steps(p_ref, out, from_sib, acc, got_x, got_y, last_x, last_y, sems, tile):
    me, core, sib, step_x, step_y = places()
    dests = (me + step_x + step_y, me + step_x, me + step_y, me)

    def send(src, dst, k, to):
        copy = remote(src, dst, sems, k, to)
        copy.start()
        return copy

    pairs = [send(block_at(p_ref, d + 1 - 2 * core), from_sib.at[k], k, sib) for k, d in enumerate(dests)]
    out_x, out_y = [], []
    for k, d in enumerate(dests):
        pairs[k].wait_recv()
        add_rows(acc.at[k], [block_at(p_ref, d), from_sib.at[k]], tile)
        top, low = halves(acc.at[k], tile)
        if k == 0:
            out_x.append(send(top, got_x.at[0], 4, me + step_x))
            out_y.append(send(low, got_y.at[0], 5, me + step_y))
        if k == 1:
            out_x.append(send(top, got_x.at[1], 6, me + step_x))
        if k == 2:
            out_y.append(send(low, got_y.at[1], 7, me + step_y))
    out_x[0].wait_recv()
    add_rows(got_x.at[0], [got_x.at[0], halves(acc.at[2], tile)[0]], tile)
    last_a = send(got_x.at[0], last_y, 8, me + step_y)
    out_y[0].wait_recv()
    add_rows(got_y.at[0], [got_y.at[0], halves(acc.at[1], tile)[1]], tile)
    last_b = send(got_y.at[0], last_x, 9, me + step_x)
    out_x[1].wait_recv()
    out_y[1].wait_recv()
    top, low = halves(acc.at[3], tile)
    out_top, out_low = halves(out, tile)
    last_a.wait_recv()
    add_rows(out_top, [got_x.at[1], top, last_y], tile)
    last_b.wait_recv()
    add_rows(out_low, [got_y.at[1], low, last_x], tile)
    for copy in pairs + out_x + out_y + [last_a, last_b]:
        copy.wait_send()


def product_scatter_body(transposed, axes, modes, sizes, a_ref, w_ref, *refs):
    count = len(modes)
    moved, out_ref, arrived, refs = refs[:count], refs[count], refs[count + 1 : 2 * count + 1], refs[2 * count + 1 :]
    stage, from_sib, acc, got_x, got_y, last_x, last_y, sems = refs[:8]
    plan = direct_copies(sizes, axes, modes, moved, arrived, *refs[8:]) if count else None
    others = [(axis, d) for axis, devices in plan[0].items() for d in devices] if count else []
    me, core, sib, step_x, step_y = places()
    rows, width = out_ref.shape
    barrier = pltpu.get_barrier_semaphore()
    others += [("seq", sib), ("seq", me + step_x), ("seq", me + step_y)]
    for axis, d in others:
        pl.semaphore_signal(barrier, inc=1, device_id={axis: d}, device_id_type=MESH)
    pl.semaphore_wait(barrier, len(others))
    if count:
        for copy in plan[1] + plan[2]:
            copy.start()
    dests = (me + step_x + step_y, me + step_x, me + step_y, me)

    def multiply(d, store):
        left = a_ref[pl.ds(pl.multiple_of(d * rows, rows), rows), :]

        def part(cols):
            if transposed:
                return dot_nt(left, w_ref[cols, :])
            return matmul(left, w_ref[:, cols])

        def step(i, _):
            cols = pl.ds(pl.multiple_of(i * 512, 512), 512)
            store(cols, part(cols))
            return 0

        lax.fori_loop(0, width // 512, step, 0, unroll=True)
        if width % 512:
            cols = pl.ds(width // 512 * 512, width % 512)
            store(cols, part(cols))

    def send(src, dst, k, to):
        copy = remote(src, dst, sems, k, to)
        copy.start()
        return copy

    def for_sibling(k):
        def store(cols, value):
            stage[k, :, cols] = value.astype(bf16)

        multiply(dests[k] + 1 - 2 * core, store)
        return send(stage.at[k], from_sib.at[k], k, sib)

    def for_chip(k):
        def store(cols, value):
            acc[k, :, cols] = (value + from_sib[k, :, cols].astype(f32)).astype(bf16)

        pairs[k].wait_recv()
        multiply(dests[k], store)
        return halves(acc.at[k], 16)

    pairs = [for_sibling(0), for_sibling(1)]
    top, low = for_chip(0)
    out_x = [send(top, got_x.at[0], 4, me + step_x)]
    out_y = [send(low, got_y.at[0], 5, me + step_y)]
    pairs.append(for_sibling(2))
    top, low = for_chip(1)
    out_x.append(send(top, got_x.at[1], 6, me + step_x))
    pairs.append(for_sibling(3))
    top, low = for_chip(2)
    out_y.append(send(low, got_y.at[1], 7, me + step_y))
    out_x[0].wait_recv()
    add_rows(got_x.at[0], [got_x.at[0], halves(acc.at[2], 16)[0]], 16)
    last_a = send(got_x.at[0], last_y, 8, me + step_y)
    out_y[0].wait_recv()
    add_rows(got_y.at[0], [got_y.at[0], halves(acc.at[1], 16)[1]], 16)
    last_b = send(got_y.at[0], last_x, 9, me + step_x)
    top, low = for_chip(3)
    out_x[1].wait_recv()
    out_y[1].wait_recv()
    out_top, out_low = halves(out_ref, 16)
    last_a.wait_recv()
    add_rows(out_top, [got_x.at[1], top, last_y], 16)
    last_b.wait_recv()
    add_rows(out_low, [got_y.at[1], low, last_x], 16)
    for copy in pairs + out_x + out_y + [last_a, last_b]:
        copy.wait_send()
    if count:
        direct_wait(plan)


def scatter_body(p_ref, *refs):
    out_ref, from_sib, acc, got_x, got_y, last_x, last_y, sems = refs[-8:]
    me, core, sib, step_x, step_y = places()
    greet([sib, me + step_x, me + step_y])
    scatter_steps(p_ref, out_ref, from_sib, acc, got_x, got_y, last_x, last_y, sems, 16)


def sum_body(p_ref, *refs):
    out_ref, from_sib, acc, got_x, got_y, last_x, last_y, sems = refs[-8:]
    me, core, sib, step_x, step_y = places()
    greet([sib, me + step_x, me + step_y])
    scatter_steps(p_ref, block_at(out_ref, me), from_sib, acc, got_x, got_y, last_x, last_y, sems, 8)
    gather_steps(out_ref, sems, 10, 8)


def scatter_scratch(rows, width, dtype, tile):
    top = (rows // 2 + tile - 1) // tile * tile
    low = rows - top
    return [
        pltpu.VMEM((4, rows, width), dtype),
        pltpu.VMEM((4, rows, width), dtype),
        pltpu.VMEM((2, top, width), dtype),
        pltpu.VMEM((2, low, width), dtype),
        pltpu.VMEM((low, width), dtype),
        pltpu.VMEM((top, width), dtype),
    ]


def direct_copies(sizes, axes, modes, ins, outs, sems, local_sems):
    me = {axis: lax.axis_index(axis) for axis in sizes}
    others = {axis: [(me[axis] + k) % size for k in range(1, size)] for axis, size in sizes.items()}
    own, copies = [], []
    for a, (x, out, axis, mode) in enumerate(zip(ins, outs, axes, modes)):
        at = me[axis]
        own.append(pltpu.make_async_copy(x.at[at] if mode == "exchange" else x, out.at[at], local_sems.at[a]))
        for to in others[axis]:
            src = x.at[to] if mode == "exchange" else x
            copies.append(remote(src, out.at[at], sems, len(copies), to, axis))
    return others, own, copies


def direct_start(plan):
    others, own, copies = plan
    for copy in own:
        copy.start()
    barrier = pltpu.get_barrier_semaphore()
    for axis, devices in others.items():
        for d in devices:
            pl.semaphore_signal(barrier, inc=1, device_id={axis: d}, device_id_type=MESH)
    pl.semaphore_wait(barrier, sum(len(devices) for devices in others.values()))
    for copy in copies:
        copy.start()


def direct_wait(plan):
    for copy in plan[1] + plan[2]:
        copy.wait()


def direct_scratch(sizes, axes):
    return [
        pltpu.SemaphoreType.DMA((2, sum(sizes[axis] - 1 for axis in axes))),
        pltpu.SemaphoreType.DMA((len(axes),)),
    ]


def direct_body(sizes, axes, modes, unused, *refs):
    count = len(modes)
    ins, refs = refs[:count], refs[count + unused :]
    plan = direct_copies(sizes, axes, modes, ins, refs[:count], *refs[count:])
    direct_start(plan)
    direct_wait(plan)


def gather_exchange_body(x_ref, e_ref, out_ref, e_out, sems, local_sem, *e_sems):
    mine = pltpu.make_async_copy(x_ref, out_ref.at[lax.axis_index("seq")], local_sem)
    mine.start()
    others, own, copies = direct_copies({"seq": 8}, ("seq",), ("exchange",), [e_ref], [e_out], *e_sems)
    greet(others["seq"])
    mine.wait()

    def early():
        for copy in own + copies:
            copy.start()

    gather_steps(out_ref, sems, 0, 16, early)
    for copy in own + copies:
        copy.wait()


def scatter_exchange_body(p_ref, e_ref, out_ref, e_out, *refs):
    others, own, copies = direct_copies({"seq": 8}, ("seq",), ("exchange",), [e_ref], [e_out], *refs[7:])
    greet(others["seq"])
    for copy in own + copies:
        copy.start()
    scatter_steps(p_ref, out_ref, *refs[:7], 16)
    for copy in own + copies:
        copy.wait()


any_space = pl.BlockSpec(memory_space=pl.ANY)
vmem_space = pl.BlockSpec(memory_space=pltpu.VMEM)


def comm_params(collective_id):
    return pltpu.CompilerParams(
        collective_id=collective_id, has_side_effects=True, vmem_limit_bytes=48 << 20
    )


def direct(sizes, arrays, collective_id, after=()):
    values = [x for x, _, _ in arrays]
    axes = [axis for _, axis, _ in arrays]
    modes = [mode for _, _, mode in arrays]
    sizes = {axis: sizes[axis] for axis in sorted(set(axes))}
    shapes = [x.shape if mode == "exchange" else (sizes[axis],) + x.shape for x, axis, mode in arrays]
    return pl.pallas_call(
        functools.partial(direct_body, sizes, axes, modes, len(after)),
        out_shape=[jax.ShapeDtypeStruct(s, x.dtype) for s, x in zip(shapes, values)],
        in_specs=[any_space] * (len(values) + len(after)),
        out_specs=[any_space] * len(values),
        scratch_shapes=direct_scratch(sizes, axes),
        compiler_params=comm_params(collective_id),
        name="direct",
    )(*values, *after)


def seq_gather(n, block, collective_id, after=()):
    if n != 8:
        return lax.all_gather(block, "seq", axis=0, tiled=False)
    return pl.pallas_call(
        gather_body,
        out_shape=jax.ShapeDtypeStruct((8,) + block.shape, block.dtype),
        in_specs=[any_space] * (1 + len(after)),
        out_specs=any_space,
        scratch_shapes=[pltpu.SemaphoreType.DMA((2, 9)), pltpu.SemaphoreType.DMA],
        compiler_params=comm_params(collective_id),
        name="seq_gather",
    )(block, *after)


def gather_exchange(n, block, blocks, collective_id):
    if n != 8:
        return seq_gather(n, block, None), exchange(n, blocks, None)
    return pl.pallas_call(
        gather_exchange_body,
        out_shape=[
            jax.ShapeDtypeStruct((8,) + block.shape, block.dtype),
            jax.ShapeDtypeStruct(blocks.shape, blocks.dtype),
        ],
        in_specs=[any_space, any_space],
        out_specs=[any_space, any_space],
        scratch_shapes=[pltpu.SemaphoreType.DMA((2, 9)), pltpu.SemaphoreType.DMA]
        + direct_scratch({"seq": 8}, ("seq",)),
        compiler_params=comm_params(collective_id),
        name="gather_exchange",
    )(block, blocks)


def scatter_exchange(n, parts, blocks, collective_id):
    if n != 8:
        return seq_scatter(n, parts, None), exchange(n, blocks, None)
    _, rows, width = parts.shape
    return pl.pallas_call(
        scatter_exchange_body,
        out_shape=[jax.ShapeDtypeStruct((rows, width), f32), jax.ShapeDtypeStruct(blocks.shape, blocks.dtype)],
        in_specs=[vmem_space, any_space],
        out_specs=[vmem_space, any_space],
        scratch_shapes=scatter_scratch(rows, width, parts.dtype, 16)
        + [pltpu.SemaphoreType.DMA((2, 10))]
        + direct_scratch({"seq": 8}, ("seq",)),
        compiler_params=comm_params(collective_id),
        name="scatter_exchange",
    )(parts, blocks)


def exchange_token_sum(n, blocks, value, collective_id, after=()):
    if n != 8:
        return exchange(n, blocks, None), lax.psum(value, "seq")
    arrays = [(blocks, "seq", "exchange"), (value.reshape(-1, 128), "seq", "gather")]
    moved, got = direct({"seq": n}, arrays, collective_id, after)
    return moved, jnp.sum(got, 0).reshape(-1)


def gather_product(n, block, w, collective_id):
    if n != 8:
        full = lax.all_gather(block, "seq", axis=0, tiled=True)
        return full, matmul(full, w).astype(bf16)
    rows = 8 * block.shape[0]
    full, product = pl.pallas_call(
        gather_product_body,
        out_shape=[
            jax.ShapeDtypeStruct((8,) + block.shape, bf16),
            jax.ShapeDtypeStruct((rows, w.shape[1]), bf16),
        ],
        in_specs=[vmem_space, vmem_space],
        out_specs=[vmem_space, vmem_space],
        scratch_shapes=[pltpu.SemaphoreType.DMA((2, 9)), pltpu.SemaphoreType.DMA],
        compiler_params=comm_params(collective_id),
        name="gather_product",
    )(block, w)
    return full.reshape(rows, -1), product


def gather_beside(n, block, first, second, collective_id):
    if n != 8:
        full = lax.all_gather(block, "seq", axis=0, tiled=True)
        return full, dot_tn(*first).astype(bf16), dot_tn(*second).astype(bf16)
    operands = first + second
    full, one, two = pl.pallas_call(
        gather_beside_body,
        out_shape=[jax.ShapeDtypeStruct((8,) + block.shape, bf16)]
        + [jax.ShapeDtypeStruct((a.shape[1], b.shape[1]), bf16) for a, b in (first, second)],
        in_specs=[any_space] * 5,
        out_specs=[any_space, vmem_space, vmem_space],
        scratch_shapes=[pltpu.VMEM(x.shape, bf16) for x in operands]
        + [pltpu.SemaphoreType.DMA((2, 9)), pltpu.SemaphoreType.DMA((5,))],
        compiler_params=comm_params(collective_id),
        name="gather_beside",
    )(block, *operands)
    return full.reshape(8 * block.shape[0], -1), one, two


def seq_scatter(n, parts, collective_id, after=()):
    if n != 8:
        return lax.psum_scatter(parts, "seq", scatter_dimension=0, tiled=False).astype(f32)
    _, rows, width = parts.shape
    return pl.pallas_call(
        scatter_body,
        out_shape=jax.ShapeDtypeStruct((rows, width), f32),
        in_specs=[vmem_space] + [any_space] * len(after),
        out_specs=vmem_space,
        scratch_shapes=scatter_scratch(rows, width, parts.dtype, 16) + [pltpu.SemaphoreType.DMA((2, 10))],
        compiler_params=comm_params(collective_id),
        name="seq_scatter",
    )(parts, *after)


def product_scatter(n, a, w, transposed, collective_id, sizes=None, arrays=()):
    if n != 8:
        product = (dot_nt if transposed else matmul)(a, w).astype(bf16)
        product = lax.psum_scatter(product, "seq", scatter_dimension=0, tiled=True).astype(f32)
        return [product] + (list(direct(sizes, arrays, collective_id)) if arrays else [])
    rows, width = a.shape[0] // 8, w.shape[0 if transposed else 1]
    moved = [x for x, _, _ in arrays]
    axes = [axis for _, axis, _ in arrays]
    modes = [mode for _, _, mode in arrays]
    sizes = {axis: sizes[axis] for axis in sorted(set(axes))}
    shapes = [x.shape if mode == "exchange" else (sizes[axis],) + x.shape for x, axis, mode in arrays]
    return pl.pallas_call(
        functools.partial(product_scatter_body, transposed, axes, modes, sizes),
        out_shape=[jax.ShapeDtypeStruct((rows, width), f32)]
        + [jax.ShapeDtypeStruct(shape, x.dtype) for shape, x in zip(shapes, moved)],
        in_specs=[vmem_space, vmem_space] + [any_space] * len(moved),
        out_specs=[vmem_space] + [any_space] * len(moved),
        scratch_shapes=[pltpu.VMEM((4, rows, width), bf16)]
        + scatter_scratch(rows, width, bf16, 16)
        + [pltpu.SemaphoreType.DMA((2, 10))]
        + (direct_scratch(sizes, axes) if moved else []),
        compiler_params=comm_params(collective_id),
        cost_estimate=pl.CostEstimate(
            flops=2 * a.shape[0] * a.shape[1] * width, bytes_accessed=100 << 20, transcendentals=0
        ),
        name="product_scatter",
    )(a, w, *moved)


def seq_sum(n, parts, collective_id, after=()):
    if n != 8:
        return lax.psum(parts, "seq")
    rows, length = parts.shape
    return pl.pallas_call(
        sum_body,
        out_shape=jax.ShapeDtypeStruct(parts.shape, f32),
        in_specs=[vmem_space] + [any_space] * len(after),
        out_specs=vmem_space,
        scratch_shapes=scatter_scratch(rows, length // 8, f32, 8) + [pltpu.SemaphoreType.DMA((2, 19))],
        compiler_params=comm_params(collective_id),
        name="seq_sum",
    )(parts, *after)


def exchange(n, blocks, collective_id, after=()):
    if n != 8:
        return lax.all_to_all(blocks, "seq", 0, 0, tiled=False)
    return direct({"seq": n}, [(blocks, "seq", "exchange")], collective_id, after)[0]


def deal(total, parts, n):
    unit = 5 * n
    nat = jnp.arange(total, dtype=jnp.int32)
    start = jnp.zeros_like(nat)
    at = 0
    for w in parts[:-1]:
        at += w
        start = jnp.where(nat >= at, at, start)
    inside = nat - start
    owner = (inside % unit) // 5
    col = owner * (total // n) + start // n + (inside // unit) * 5 + inside % 5
    return (col[:, None] == nat[None, :]).astype(bf16)


def exact(left, right, contract, precision=None):
    return lax.dot_general(left, right, (contract, ((), ())), precision=precision, preferred_element_type=f32)


def window_start(tokens, span, length):
    me = lax.axis_index("seq")
    reach = (WINDOW_TOKENS + tokens - 2) // tokens
    if length == 2 * reach * tokens:
        first = me // reach * (me - reach) * tokens
    else:
        first = jnp.minimum(jnp.maximum(me - reach, 0) * tokens, length - span)
    return pl.ds(pl.multiple_of(first, math.gcd(tokens, length - span)), span)


def with_exchange(body, count, ins, outs):
    def whole(*refs):
        given, moved = refs[:ins], refs[ins : ins + count]
        refs = refs[ins + count :]
        made, arrived, sems = refs[:outs], refs[outs : outs + count], refs[outs + count :]
        if count:
            plan = direct_copies({"seq": 8}, ("seq",) * count, ("exchange",) * count, moved, arrived, *sems)

            @pl.when(pl.program_id(0) == 0)
            def _():
                direct_start(plan)

        body(*given, *made)
        if count:

            @pl.when(pl.program_id(0) == KEY_VALUE_HEADS - 1)
            def _():
                direct_wait(plan)

    return whole


def attn_fwd_body(qt_ref, kt_ref, vt_ref, bias_ref, out_ref, lse_ref):
    span, tokens = bias_ref.shape
    window = window_start(tokens, span, kt_ref.shape[1])
    keys = kt_ref[:, window].T
    values_t = vt_ref[:, window]
    for head in range(qt_ref.shape[0] // HEAD_SIZE):
        rows = slice(head * HEAD_SIZE, (head + 1) * HEAD_SIZE)
        scores = matmul(keys, qt_ref[rows, :]) + bias_ref[...]
        row_max = jnp.max(scores, 0, keepdims=True)
        exp_scores = jnp.exp(scores - row_max)
        row_total = jnp.sum(exp_scores, 0, keepdims=True)
        probs = (exp_scores * (1.0 / row_total)).astype(bf16)
        out_ref[rows, :] = matmul(values_t, probs)
        lse_ref[0, head : head + 1, :] = row_max + jnp.log(row_total)


def attn_bwd_body(qt_ref, kt_ref, vt_ref, dot_ref, lse_ref, bias_ref, dqt_ref, dkt_ref, dvt_ref):
    span, tokens = bias_ref.shape
    window = window_start(tokens, span, kt_ref.shape[1])
    keys_t = kt_ref[:, window]
    keys, values = keys_t.T, vt_ref[:, window].T
    dk = jnp.zeros(keys.shape, f32)
    dv = jnp.zeros(values.shape, f32)
    for head in range(qt_ref.shape[0] // HEAD_SIZE):
        rows = slice(head * HEAD_SIZE, (head + 1) * HEAD_SIZE)
        q_t, do_t = qt_ref[rows, :], dot_ref[rows, :]
        scores = matmul(keys, q_t) + bias_ref[...]
        probs = jnp.exp(scores - lse_ref[0, head : head + 1, :])
        d_probs = matmul(values, do_t)
        inner = jnp.sum(probs * d_probs, 0, keepdims=True)
        d_scores = (probs * (d_probs - inner)).astype(bf16)
        dqt_ref[rows, :] = (matmul(keys_t, d_scores) * (HEAD_SIZE**-0.5)).astype(bf16)
        dk = dk + matmul(d_scores, q_t.T)
        dv = dv + matmul(probs.astype(bf16), do_t.T)
    dkt_ref[...] = jnp.zeros_like(dkt_ref)
    dvt_ref[...] = jnp.zeros_like(dvt_ref)
    dkt_ref[:, window] = dk.T.astype(bf16)
    dvt_ref[:, window] = dv.T.astype(bf16)


def attn_specs(tokens, span, groups, length):
    heads = pl.BlockSpec((groups * HEAD_SIZE, tokens), lambda h: (h, 0))
    key = pl.BlockSpec((HEAD_SIZE, length), lambda h: (h, 0))
    value = pl.BlockSpec((HEAD_SIZE, length), lambda h: (KEY_VALUE_HEADS + h, 0))
    lse = pl.BlockSpec((1, 8, tokens), lambda h: (h, 0, 0))
    bias = pl.BlockSpec((span, tokens), lambda h: (0, 0))
    return heads, key, value, lse, bias


def attention_call(body, name, in_specs, out_specs, out_shape, arrays, moved, collective_id, cost):
    count = len(moved)
    params = comm_params(collective_id) if count else pltpu.CompilerParams(vmem_limit_bytes=48 << 20)
    return pl.pallas_call(
        with_exchange(body, count, len(in_specs), len(out_specs)),
        grid=(KEY_VALUE_HEADS,),
        in_specs=in_specs + [any_space] * count,
        out_specs=out_specs + [any_space] * count,
        out_shape=out_shape + [jax.ShapeDtypeStruct(x.shape, x.dtype) for x in moved],
        scratch_shapes=direct_scratch({"seq": 8}, ("seq",) * count) if count else [],
        compiler_params=params,
        cost_estimate=cost,
        name=name,
    )(*arrays, *moved)


def attention_forward(q_t, kv_t, bias, moved, collective_id):
    span, tokens = bias.shape
    heads, key, value, lse, bias_spec = attn_specs(tokens, span, QUERY_HEADS // KEY_VALUE_HEADS, kv_t.shape[1])
    return attention_call(
        attn_fwd_body,
        "attention_forward",
        [heads, key, value, bias_spec],
        [heads, lse],
        [
            jax.ShapeDtypeStruct(q_t.shape, f32),
            jax.ShapeDtypeStruct((KEY_VALUE_HEADS, 8, tokens), f32),
        ],
        (q_t, kv_t, kv_t, bias),
        moved,
        collective_id,
        pl.CostEstimate(
            flops=QUERY_HEADS * span * tokens * 512, bytes_accessed=8 << 20, transcendentals=QUERY_HEADS * span * tokens
        ),
    )


def attention_backward(q_t, kv_t, do_t, lse, bias, moved, collective_id):
    span, tokens = bias.shape
    heads, key, value, lse_spec, bias_spec = attn_specs(
        tokens, span, QUERY_HEADS // KEY_VALUE_HEADS, kv_t.shape[1]
    )
    grad = jax.ShapeDtypeStruct((KEY_VALUE_HEADS * HEAD_SIZE, kv_t.shape[1]), bf16)
    return attention_call(
        attn_bwd_body,
        "attention_backward",
        [heads, key, value, heads, lse_spec, bias_spec],
        [heads, key, key],
        [jax.ShapeDtypeStruct(q_t.shape, bf16), grad, grad],
        (q_t, kv_t, kv_t, do_t, lse, bias),
        moved,
        collective_id,
        pl.CostEstimate(
            flops=QUERY_HEADS * span * tokens * 1280, bytes_accessed=16 << 20, transcendentals=QUERY_HEADS * span * tokens
        ),
    )


def layer(
    n,
    m,
    tokens,
    doc_ids,
    in_weight,
    out_weight,
    gate_up,
    down_weight,
    select_weight,
    step_weight,
    first_gain,
    second_gain,
    attn_gain,
    mamba_gain,
    conv_weight,
    conv_bias,
    step_bias,
    decay_log,
    skip_gain,
    cotangent,
):
    fast = n == 8
    sizes = {"seq": n, "fsdp": m}
    me = lax.axis_index("seq")
    query_w = QUERY_HEADS * HEAD_SIZE
    key_w = KEY_VALUE_HEADS * HEAD_SIZE
    q_own, k_own, c_own, f_own = query_w // n, key_w // n, DI // n, F // n
    p_own = q_own + 2 * k_own + 2 * c_own
    kinds = (query_w, key_w, key_w, DI, DI)
    local, width = tokens.shape[1:]
    length = local * n
    z_rows = in_weight.shape[0]
    sel_rows = select_weight.shape[0]
    wide = p_own * n
    starts = (0, query_w, query_w + key_w, query_w + 2 * key_w, query_w + 2 * key_w + DI)
    widths = (q_own, k_own, k_own, c_own, c_own)
    highest = lax.Precision.HIGHEST

    small_w = jnp.concatenate([select_weight, step_weight], 0)
    if fast:
        deal_in, deal_small, deal_out = deal(p_own, (p_own,), n), deal(c_own, (c_own,), n), deal(out_weight.shape[0], (out_weight.shape[0],), n)
        in_blocks = exact(deal_in, in_weight, ((0,), (1,))).astype(bf16).reshape(n, p_own // n, z_rows)
        small_blocks = exact(deal_small, small_w, ((0,), (1,))).astype(bf16).reshape(n, c_own // n, -1)
        in_blocks, small_blocks, ids = direct(
            sizes,
            [(in_blocks, "seq", "exchange"), (small_blocks, "seq", "exchange"), (doc_ids.reshape(-1, 128), "seq", "gather")],
            0,
        )
        ids = ids.reshape(-1)
        in_cols = in_blocks.reshape(p_own, z_rows).T
        small_cols = small_blocks.reshape(c_own, -1).T
        seq_x = tokens[0].astype(f32)
        normed_one, scale_one = rms_norm(seq_x, first_gain)
        normed_one = seq_gather(n, normed_one.astype(bf16), 3, (in_blocks,))
        gu_blocks = gate_up.T.reshape(n, -1, z_rows)
        out_blocks = exact(deal_out, out_weight, ((0,), (0,))).astype(bf16).reshape(n, -1, out_weight.shape[1])
        down_blocks = down_weight.reshape(n, -1, down_weight.shape[1])
        out_blocks, down_blocks, small_full = direct(
            sizes,
            [(x, "seq", "exchange") for x in (out_blocks, down_blocks)] + [(small_cols, "fsdp", "gather")],
            1,
            (normed_one,),
        )
        out_rows = out_blocks.transpose(1, 0, 2).reshape(-1, width)
        down_rows = down_blocks.transpose(1, 0, 2).reshape(-1, width)
        in_full = lax.all_gather(in_cols, "fsdp", axis=0, tiled=True)
        in_full, out_rows, down_rows = lax.optimization_barrier((in_full, out_rows, down_rows))
        out_full = lax.all_gather(out_rows, "fsdp", axis=0, tiled=True)
        down_full = lax.all_gather(down_rows, "fsdp", axis=0, tiled=True)
    else:
        seq_x = tokens[0].astype(f32)
        normed_one, scale_one = rms_norm(seq_x, first_gain)
        normed_one = seq_gather(n, normed_one.astype(bf16), 3)
        ids = lax.all_gather(doc_ids[0], "seq", axis=0, tiled=True)
        in_cols = lax.all_gather(in_weight, "seq", axis=1, tiled=True)
        in_cols = jnp.concatenate(
            [lax.dynamic_slice_in_dim(in_cols, s + me * w, w, 1) for s, w in zip(starts, widths)], 1
        )
        small_full = lax.all_gather(small_w, "fsdp", axis=0, tiled=False)
        half = n // 2
        route_a = [(d, 2 * d if d < half else 2 * (d - half) + 1) for d in range(n)]
        route_b = [(d, 2 * d + 1 if d < half else 2 * (d - half)) for d in range(n)]
        low_half = me < half
        even = me % 2 == 0
        piece0, piece1 = gate_up[:, :f_own], gate_up[:, f_own:]
        got_a = lax.ppermute(jnp.where(low_half, piece0, piece1), "seq", route_a)
        got_b = lax.ppermute(jnp.where(low_half, piece1, piece0), "seq", route_b)
        gu_cols = jnp.concatenate([jnp.where(even, got_a, got_b), jnp.where(even, got_b, got_a)], 1)
        out_rows = lax.all_gather(out_weight, "fsdp", axis=0, tiled=True)
        out_rows = jnp.concatenate(
            [out_rows[:query_w].reshape(n, q_own, -1), out_rows[query_w:].reshape(n, c_own, -1)], 1
        )
        out_full = exchange(n, out_rows, None).transpose(1, 0, 2).reshape(q_own + c_own, -1)
        down_rows = lax.all_gather(down_weight, "fsdp", axis=0, tiled=True).reshape(n, f_own, -1)
        down_full = exchange(n, down_rows, None).transpose(1, 0, 2).reshape(f_own, -1)
        in_full = lax.all_gather(in_cols, "fsdp", axis=0, tiled=True)
        gu_full = lax.all_gather(gu_cols, "fsdp", axis=0, tiled=True)
    select_own = small_full[:, :sel_rows].reshape(-1, c_own)
    step_own = small_full[:, sel_rows:].reshape(-1, c_own)

    params = jnp.concatenate(
        [mamba_gain[None], conv_weight, conv_bias[None], step_bias[None], decay_log, skip_gain[None]], 0
    )
    if fast:
        params = params.reshape(-1, c_own)
        params = exact(params, deal(c_own, (c_own,), n), ((1,), (0,)), highest).reshape(-1, n, n, c_own // n)
        params = lax.dynamic_index_in_dim(params, me, 2, False).reshape(-1, c_own)
    else:
        params = lax.dynamic_slice_in_dim(params, me * c_own, c_own, 1)
    mamba_g, conv_w, conv_b, step_b = params[0], params[1 : 1 + KC], params[1 + KC], params[2 + KC]
    decay_l, skip_g = params[3 + KC : 3 + KC + NS], params[3 + KC + NS]

    def heads_in(blocks):
        blocks = blocks.reshape(query_w, local)
        return exact(deal(query_w, (query_w,), n), blocks, ((1,), (0,))).astype(bf16) if fast else blocks

    def heads_out(value):
        if fast:
            value = exact(deal(query_w, (query_w,), n), value, ((0,), (0,))).astype(bf16)
        return value.reshape(n, q_own, local)

    normed_one = normed_one.reshape(length, width)
    qkv_w = q_own + 2 * k_own
    qkv_t = exact(in_full[:, :qkv_w], normed_one, ((0,), (1,))).astype(bf16)
    branch = matmul(normed_one, in_full[:, qkv_w:]).astype(bf16)
    inputs = branch[:, :c_own].astype(f32)
    gate_z = branch[:, c_own:].astype(f32)

    q_blocks = qkv_t[:q_own].reshape(q_own, n, local).transpose(1, 0, 2)
    kv_all, q_blocks = gather_exchange(n, qkv_t[q_own:], q_blocks, 4)
    q_t = heads_in(q_blocks) * bf16(HEAD_SIZE**-0.5)
    reach = (WINDOW_TOKENS + local - 2) // local
    span = min((reach + 1) * local, length)
    first_key = jnp.clip((me - reach) * local, 0, length - span)
    nat = jnp.arange(2 * key_w, dtype=jnp.int32)
    inside = nat % key_w
    block_order = inside // k_own * 2 * k_own + nat // key_w * k_own + inside % k_own
    deal_kv = (
        deal(2 * key_w, (key_w, key_w), n) if fast else (block_order[:, None] == nat[None, :]).astype(bf16)
    )
    kv_t = exact(deal_kv, kv_all.reshape(2 * key_w, length), ((1,), (0,))).astype(bf16)
    query_pos = me * local + jnp.arange(local, dtype=jnp.int32)
    key_pos = first_key + jnp.arange(span, dtype=jnp.int32)
    offset = query_pos[None, :] - key_pos[:, None]
    key_ids = lax.dynamic_slice_in_dim(ids, first_key, span, 0)
    allowed = (offset >= 0) & (offset < WINDOW_TOKENS) & (doc_ids[0][None, :] == key_ids[:, None])
    bias = jnp.where(allowed, 0.0, masked_score).astype(f32)
    attended, lse, *moved = attention_forward(q_t, kv_t, bias, [gu_blocks] if fast else [], 23)
    if fast:
        gu_full = lax.all_gather(moved[0].reshape(-1, z_rows).T, "fsdp", axis=0, tiled=True)
    attn_scale = lax.rsqrt(jnp.mean(attended * attended, axis=0, keepdims=True) + norm_eps)
    attn_normed = (attended * attn_scale * attn_gain[:, None]).astype(bf16)

    padded_inputs = jnp.pad(inputs, ((KC - 1, 0), (0, 0)))
    padded_ids = jnp.pad(ids, (KC - 1, 0), constant_values=-1)
    conv_sum = conv_b + jnp.zeros_like(inputs)
    same_masks = []
    for tap in range(KC):
        begin = KC - 1 - tap
        same = (padded_ids[begin : begin + length] == ids).astype(f32)[:, None]
        same_masks.append(same)
        conv_sum = conv_sum + conv_w[tap] * padded_inputs[begin : begin + length] * same
    activated_b = jax.nn.silu(conv_sum).astype(bf16)
    activated = activated_b.astype(f32)
    sel_pad = jnp.pad(select_own, ((0, (-select_own.shape[0]) % 8), (0, 0)))
    selected = seq_sum(n, dot_nt(sel_pad, activated_b), 7)
    step_raw = selected[:DTR].astype(bf16)
    b_t = selected[DTR : DTR + NS]
    c_t = selected[DTR + NS : DTR + 2 * NS]
    step_pre = dot_tn(step_raw, step_own) + step_b
    step_size = jax.nn.softplus(step_pre)
    rate = -jnp.exp(decay_l)
    changed = jnp.concatenate([jnp.zeros((1,), f32), (ids[1:] != ids[:-1]).astype(f32)])
    step_keep = step_size + 1e30 * changed[:, None]
    push = step_size * activated
    scan_out, states = scan_forward(step_keep, push, b_t, c_t, rate)
    mamba_pre = scan_out + skip_g * activated
    gate_sig = jax.nn.sigmoid(gate_z)
    mamba_out = mamba_pre * gate_z * gate_sig
    attn_c, square_sum = exchange_token_sum(n, heads_out(attn_normed), jnp.sum(mamba_out * mamba_out, -1), 6)
    attn_c = attn_c.transpose(0, 2, 1).reshape(length, q_own)
    mamba_scale = lax.rsqrt(square_sum / DI + norm_eps)[:, None]
    mamba_normed = mamba_out * mamba_scale * mamba_g
    joined = jnp.concatenate([attn_c, mamba_normed.astype(bf16)], 1)
    (mixed,) = product_scatter(n, joined, out_full, False, 9)
    hidden = seq_x + 0.5 * mixed
    normed_two, scale_two = rms_norm(hidden, second_gain)
    normed_two, gate_up_out = gather_product(n, normed_two.astype(bf16), gu_full, 10)
    gate_part = gate_up_out[:, :f_own].astype(f32)
    up_part = gate_up_out[:, f_own:].astype(f32)
    gate_act = jax.nn.sigmoid(gate_part)
    inner = (gate_part * gate_act * up_part).astype(bf16)
    ffn = matmul(inner, down_full).astype(bf16)

    own_d_out = cotangent[0] if fast else lax.optimization_barrier((cotangent[0], inner))[0]
    d_ffn = lax.all_gather(own_d_out, "seq", axis=0, tiled=True)
    d_inner = dot_nt(d_ffn, down_full)
    d_gate_up = jnp.concatenate(
        [
            d_inner * up_part * gate_act * (1.0 + gate_part * (1.0 - gate_act)),
            d_inner * gate_part * gate_act,
        ],
        1,
    ).astype(bf16)
    (d_normed_two,) = product_scatter(n, d_gate_up, gu_full, True, 13)
    d_hidden_part, second_grad = norm_back(hidden, scale_two, second_gain, d_normed_two)
    d_hidden = cotangent[0].astype(f32) + d_hidden_part
    d_mixed, down_term, gate_up_term = gather_beside(
        n, d_hidden.astype(bf16), (inner, d_ffn), (normed_two, d_gate_up), 14
    )
    gu_part = lax.psum_scatter(gate_up_term, "fsdp", scatter_dimension=0, tiled=True)
    if fast:
        down_part = lax.psum_scatter(down_term.reshape(m, -1, width), "fsdp", scatter_dimension=0, tiled=False)
    out_term = (0.5 * dot_tn(joined, d_mixed)).astype(bf16)
    if fast:
        out_part = lax.psum_scatter(out_term.reshape(m, -1, width), "fsdp", scatter_dimension=0, tiled=False)
    d_joined = 0.5 * dot_nt(d_mixed, out_full)

    u = d_joined[:, q_own:]
    weighted = u * mamba_g
    d_attn = d_joined[:, :q_own].astype(bf16).reshape(n, local, q_own).transpose(0, 2, 1)
    d_attn, inner_mean = exchange_token_sum(n, d_attn, jnp.sum(weighted * mamba_out, -1), 15)
    inner_mean = inner_mean[:, None] / DI
    mamba_grad = jnp.sum(u * mamba_out * mamba_scale, 0)
    d_mamba = mamba_scale * weighted - mamba_out * (mamba_scale * mamba_scale * mamba_scale) * inner_mean
    d_pre = d_mamba * gate_z * gate_sig
    d_gate = d_mamba * mamba_pre * gate_sig * (1.0 + gate_z * (1.0 - gate_sig))
    skip_grad = jnp.sum(d_pre * activated, 0)
    ffn, d_pre = lax.optimization_barrier((ffn, d_pre))
    ffn = lax.psum_scatter(ffn, "seq", scatter_dimension=0, tiled=True)
    by_rate, pushed, db_t, dc_t, decay_log_grad = scan_backward(
        step_keep, push, d_pre, b_t, c_t, states, rate
    )

    step_grads = by_rate + pushed * activated
    d_step_pre = step_grads * jax.nn.sigmoid(step_pre)
    step_bias_grad = jnp.sum(d_step_pre, 0)
    d_step_low = d_step_pre.astype(bf16)
    step_term = matmul(step_raw, d_step_low)
    d_selected = jnp.concatenate(
        [dot_nt(step_own, d_step_low), db_t, dc_t, jnp.zeros(((-DTR - 2 * NS) % 8, length), f32)], 0
    )
    d_selected = seq_sum(n, d_selected, 19)[: DTR + 2 * NS].astype(bf16)
    select_term = matmul(d_selected, activated_b)
    d_activated = d_pre * skip_g + pushed * step_size + dot_tn(d_selected, select_own)
    conv_sig = jax.nn.sigmoid(conv_sum)
    d_conv = d_activated * conv_sig * (1.0 + conv_sum * (1.0 - conv_sig))
    conv_bias_grad = jnp.sum(d_conv, 0)
    ext_grad = jnp.zeros((length + KC - 1, c_own), f32)
    conv_rows = []
    for tap in range(KC):
        begin = KC - 1 - tap
        masked_grad = d_conv * same_masks[tap]
        conv_rows.append(jnp.sum(masked_grad * padded_inputs[begin : begin + length], 0))
        ext_grad = ext_grad + jnp.pad(conv_w[tap] * masked_grad, ((begin, tap), (0, 0)))
    d_inputs = ext_grad[KC - 1 :].astype(bf16)
    d_attn, d_inputs, ffn = lax.optimization_barrier((d_attn, d_inputs, ffn))
    out_tokens = (hidden + ffn.astype(f32)).astype(bf16)
    d_attn = heads_in(d_attn).astype(f32)
    weighted_a = d_attn * attn_gain[:, None]
    attn_grad = jnp.sum(d_attn * attended * attn_scale, 1)
    mean_a = jnp.mean(weighted_a * attended, axis=0, keepdims=True)
    d_attended = attn_scale * weighted_a - attended * (attn_scale * attn_scale * attn_scale) * mean_a
    moved = []
    if fast:
        down_blocks = down_part.reshape(-1, n, width // n).transpose(1, 0, 2)
        gu_blocks = gu_part.T.reshape(n, -1, z_rows)
        moved = [gu_blocks, down_blocks]
    dq_t, dk_t, dv_t, *moved = attention_backward(
        q_t, kv_t, d_attended.astype(bf16), lse, bias, moved, 24
    )
    dkv = exact(deal_kv, jnp.concatenate([dk_t, dv_t], 0), ((0,), (0,))).astype(bf16).reshape(n, 2 * k_own, length)
    dkv, d_queries = scatter_exchange(n, dkv, heads_out(dq_t), 16)
    dkv = dkv.astype(bf16).T
    d_queries = d_queries.transpose(0, 2, 1).reshape(length, q_own)

    d_projected = jnp.concatenate([d_queries, dkv, d_inputs, d_gate.astype(bf16)], 1)
    in_term = dot_tn(normed_one, d_projected).astype(bf16)
    in_part = lax.psum_scatter(in_term, "fsdp", scatter_dimension=0, tiled=True)
    small_term = jnp.concatenate(
        [select_term.reshape(m, sel_rows, c_own), step_term.reshape(m, -1, c_own)], 1
    ).astype(bf16)
    channel = jnp.concatenate(
        [
            mamba_grad[None], jnp.stack(conv_rows), conv_bias_grad[None], step_bias_grad[None],
            decay_log_grad, skip_grad[None],
        ],
        0,
    )
    wide_grads = jnp.stack([second_grad, attn_grad])
    small_specs = [(small_term, "fsdp", "exchange"), (channel, "fsdp", "gather"), (wide_grads, "fsdp", "gather")]
    if fast:
        gu_blocks, down_blocks = moved
        out_blocks = out_part.reshape(-1, n, width // n).transpose(1, 0, 2)
        small_specs.append((out_blocks, "seq", "exchange"))
    d_normed_one, small_z, channel_z, wide_z, *moved = product_scatter(
        n, d_projected, in_full, True, 20, sizes, small_specs
    )
    if fast:
        (out_blocks,) = moved
    d_x_part, first_grad = norm_back(seq_x, scale_one, first_gain, d_normed_one)
    (first_z,) = direct(sizes, [(first_grad[None], "fsdp", "gather")], 25)
    tokens_grad = (d_hidden + d_x_part).astype(bf16)

    small_part = jnp.sum(small_z.astype(f32), 0)
    channel, wide_grads = jnp.sum(channel_z, 0), jnp.concatenate([jnp.sum(first_z, 0), jnp.sum(wide_z, 0)], 0)
    if fast:
        gu_sum = gu_blocks.reshape(-1, z_rows).T.astype(f32)
        out_sum = exact(deal_out, out_blocks.reshape(-1, width // n), ((1,), (0,)))
        down_sum = down_blocks.reshape(-1, width // n).astype(f32)
        small_blocks = small_part.astype(bf16).T.reshape(n, c_own // n, -1)
        small_blocks, channel_all, wide_all = direct(
            sizes,
            [(small_blocks, "seq", "exchange"), (channel, "seq", "gather"), (wide_grads, "seq", "gather")],
            22,
        )
        (in_blocks,) = direct(sizes, [(in_part.T.reshape(n, -1, z_rows), "seq", "exchange")], 21, (wide_all,))
        small_sum = exact(small_blocks.reshape(c_own, -1), deal_small, ((0,), (1,)))
        channel_rows = channel.shape[0]
        channel = channel_all.reshape(n, channel_rows, n, c_own // n).transpose(1, 2, 0, 3).reshape(-1, c_own)
        channel = exact(channel, deal_small, ((1,), (1,)), highest).reshape(channel_rows, DI)
        wide_grads = jnp.sum(wide_all, 0)
        in_sum = exact(in_blocks.reshape(p_own, z_rows), deal_in, ((0,), (1,)))
    else:
        out_blocks = exchange(n, out_term.reshape(q_own + c_own, n, -1).transpose(1, 0, 2), None)
        out_sum = jnp.concatenate(
            [out_blocks[:, :q_own].reshape(query_w, -1), out_blocks[:, q_own:].reshape(DI, -1)], 0
        )
        out_sum = lax.psum_scatter(out_sum, "fsdp", scatter_dimension=0, tiled=True).astype(f32)
        down_sum = exchange(n, down_term.reshape(f_own, n, -1).transpose(1, 0, 2), None).reshape(F, -1)
        down_sum = lax.psum_scatter(down_sum, "fsdp", scatter_dimension=0, tiled=True).astype(f32)
        gate_g, up_g = gu_part[:, :f_own], gu_part[:, f_own:]
        back_a = lax.ppermute(jnp.where(even, gate_g, up_g), "seq", [(t, s) for s, t in route_a])
        back_b = lax.ppermute(jnp.where(even, up_g, gate_g), "seq", [(t, s) for s, t in route_b])
        gu_sum = jnp.concatenate(
            [jnp.where(low_half, back_a, back_b), jnp.where(low_half, back_b, back_a)], 1
        ).astype(f32)
        in_sum = jnp.zeros((z_rows, wide), bf16)
        at = 0
        for s, w in zip(starts, widths):
            in_sum = lax.dynamic_update_slice_in_dim(in_sum, in_part[:, at : at + w], s + me * w, 1)
            at += w
        in_sum = lax.psum_scatter(in_sum, "seq", scatter_dimension=1, tiled=True).astype(f32)
        small_sum = small_part
        channel = lax.all_gather(channel, "seq", axis=1, tiled=True)
        wide_grads = lax.psum(wide_grads, "seq")
    return (
        out_tokens[None],
        tokens_grad[None],
        in_sum,
        out_sum,
        gu_sum,
        down_sum,
        small_sum[:sel_rows],
        small_sum[sel_rows:],
        wide_grads[0],
        wide_grads[1],
        wide_grads[2],
        channel[0],
        channel[1 : 1 + KC],
        channel[1 + KC],
        channel[2 + KC],
        channel[3 + KC : 3 + KC + NS],
        channel[3 + KC + NS],
    )


def solution(mesh):
    split = P("fsdp", "seq")
    seq3 = P("fsdp", "seq", None)
    return jax.shard_map(
        functools.partial(layer, mesh.shape["seq"], mesh.shape["fsdp"]),
        mesh=mesh,
        in_specs=(seq3,) + (split,) * 7 + (P(),) * 9 + (seq3,),
        out_specs=(seq3, seq3) + (split,) * 6 + (P(),) * 9,
        check_vma=False,
    )
```
